32 devices in a mesh: expert: 8 (over z, x), dp: 4 (over y, core).
Axes of the slice: x: 2, y: 2, z: 4, core: 2. Of those that a mesh axis runs over, the one named last changes fastest.
Arguments:
- tokens: bfloat16 [4096, 2048], P(('expert', 'dp')), may hold values from -6 to 6
- doc_ids: int32 [32, 128], P(('expert', 'dp')), may hold values from 0 to 3, never falling along the last dimension, each value on 1 to 64 neighbouring positions
- routes: int32 [4096, 6], P(('expert', 'dp')), may hold values from 0 to 15, all different within a row; in each aligned block of 128 rows (0 to 127, 128 to 255, ...) at most 64 rows name the same one
- gain_attn: bfloat16 [2048], P(('expert', 'dp')), may hold values from 0.25 to 1.75
- w_query: bfloat16 [2048, 2048], P(('expert', 'dp')), may hold values from -0.125 to 0.125
- w_key: bfloat16 [2048, 512], P(('expert', 'dp')), may hold values from -0.125 to 0.125
- w_value: bfloat16 [2048, 512], P(('expert', 'dp')), may hold values from -0.125 to 0.125
- w_out: bfloat16 [2048, 2048], P(('expert', 'dp')), may hold values from -0.5 to 0.5
- gain_moe: bfloat16 [2048], P(('expert', 'dp')), may hold values from 0.25 to 1.75
- w_router: bfloat16 [2048, 16], P(('expert', 'dp')), may hold values from -0.0625 to 0.0625
- shared_gate: bfloat16 [2048, 2816], P(('expert', 'dp')), may hold values from -0.125 to 0.125
- shared_up: bfloat16 [2048, 2816], P(('expert', 'dp')), may hold values from -0.125 to 0.125
- shared_down: bfloat16 [2816, 2048], P(('expert', 'dp')), may hold values from -0.109375 to 0.109375
- expert_gate: bfloat16 [16, 2048, 1408], P('expert', 'dp'), may hold values from -0.125 to 0.125
- expert_up: bfloat16 [16, 2048, 1408], P('expert', 'dp'), may hold values from -0.125 to 0.125
- expert_down: bfloat16 [16, 2048, 1408], P('expert', 'dp'), may hold values from -0.4375 to 0.4375
- cotangent: bfloat16 [4096, 2048], P(('expert', 'dp')), may hold values from -6 to 6
Outputs:
- output: bfloat16 [4096, 2048], P(('expert', 'dp'))
- grad_tokens: float32 [4096, 2048], P(('expert', 'dp'))
- grad_gain_attn: float32 [2048], P(('expert', 'dp'))
- grad_w_query: float32 [2048, 2048], P(('expert', 'dp'))
- grad_w_key: float32 [2048, 512], P(('expert', 'dp'))
- grad_w_value: float32 [2048, 512], P(('expert', 'dp'))
- grad_w_out: float32 [2048, 2048], P(('expert', 'dp'))
- grad_gain_moe: float32 [2048], P(('expert', 'dp'))
- grad_w_router: float32 [2048, 16], P(('expert', 'dp'))
- grad_shared_gate: float32 [2048, 2816], P(('expert', 'dp'))
- grad_shared_up: float32 [2048, 2816], P(('expert', 'dp'))
- grad_shared_down: float32 [2816, 2048], P(('expert', 'dp'))
- grad_expert_gate: float32 [16, 2048, 1408], P('expert', 'dp')
- grad_expert_up: float32 [16, 2048, 1408], P('expert', 'dp')
- grad_expert_down: float32 [16, 2048, 1408], P('expert', 'dp')
The draws below stay inside these ranges and needn't reach their ends.
Inputs may be any that keep to these rules, and one draw needn't show every extreme that they name: `doc_ids`: within each sequence the document numbers never fall, each document has 1 to 64 positions. `routes`: A token's 6 experts differ. Among the 128 rows of one sequence no expert is named by more than 64 rows; in some sequences one is named by exactly 64.
All inputs are finite; a program needn't handle non-finite values.
Results may differ from the reference program's by a relative error of at most 0.015.
Values may be sent and summed in bfloat16 or wider, within the bound.
A program may use at most 384 MiB of HBM per device.

```python
import math
import jax
import jax.numpy as jnp
import numpy as np
from jax import lax

D = 2048
HEADS = 16
KV_HEADS = 4
HEAD_DIM = 128
FFE = 1408
TOP = 6
TOK_DEV = 128
QW = 2048
KVW = 512
SH = 2816
EXPERTS = 16
CAP = 64
SEQS = 32
TOKENS = 4096


def levels(own_key, extent, split, least, high):
    level, own = 1.0, jax.random.fold_in(own_key, 6)
    for axis_at, parts in split:
        draws = jnp.exp(jax.random.uniform(jax.random.fold_in(own, axis_at), (parts,), jnp.float32, least / len(split), high / len(split)))
        level = level * jnp.repeat(draws, extent[axis_at] // parts).reshape([-1 if axis == axis_at else 1 for axis in range(len(extent))])
    return level


def length_profile(count, total, limit, lean):
    loads = [(1 << 20) // math.isqrt(standing ** lean) + 1 for standing in range(2, count + 1)]
    rest, given = total - limit - (count - 1), [1] * (count - 1)
    while rest > 0:
        free = [i for i in range(count - 1) if given[i] < limit]
        mass, remaining = sum([loads[i] for i in free]), rest
        for i in free:
            addition = min(limit - given[i], max(1, remaining * loads[i] // mass), rest)
            given[i] = given[i] + addition
            rest = rest - addition
    return np.array([limit] + given)


def uneven_parts(rng, number_of, total, limit, skew):
    if number_of == 2:
        one = jax.random.randint(rng, (), max(1, total - limit), min(limit, total - 1) + 1)
        return jnp.stack([one, total - one])
    lengths = jnp.asarray(length_profile(number_of, total, limit, skew), jnp.int32)
    couples = (number_of - 1) // 2
    giver, taker = lengths[1:1 + 2 * couples:2], lengths[2:2 + 2 * couples:2]
    slack = jnp.minimum(giver - 1, limit - taker)
    shifted = jax.random.randint(jax.random.fold_in(rng, 1), (couples,), 0, 1 << 20) % (slack + 1)
    lengths = lengths.at[1:1 + 2 * couples:2].set(giver - shifted).at[2:2 + 2 * couples:2].set(taker + shifted)
    return lengths[jax.random.permutation(jax.random.fold_in(rng, 2), number_of)]


def deal_out(rng, own, number, rows, amount, top, reach, skew):
    order = jax.random.permutation(rng, amount)
    heavy_load, usual = load_shares(amount, rows * top, reach, skew, True), load_shares(amount, rows * top, reach, skew, False)
    places = jnp.arange(amount)

    def named(tallies, offset_by):
        used = int((tallies > 0).sum())
        fixed = max(1, used // 4)
        passed = fixed + (places - fixed + offset_by * (used - fixed)) % max(1, amount - fixed)
        return jnp.zeros((amount,), jnp.int32).at[order[jnp.where(places < fixed, places, passed)]].set(jnp.asarray(tallies, jnp.int32))

    tallies = jnp.where(number % 4 == 0, named(heavy_load, number // 4), named(usual, number - number // 4 - 1))
    mixed = jax.random.permutation(jax.random.fold_in(own, 3), amount)
    donor, sink = mixed[0:amount // 2 * 2:2], mixed[1:amount // 2 * 2:2]
    room = jnp.minimum(tallies[donor] - 1, reach - tallies[sink]) // 2
    room = jnp.where((donor == order[0]) | (sink == order[0]) | (tallies[sink] == 0), 0, jnp.maximum(room, 0))
    passed = jax.random.randint(jax.random.fold_in(own, 4), (amount // 2,), 0, 1 << 20) % (room + 1)
    tallies = tallies.at[donor].add(-passed).at[sink].add(passed)
    labels = jnp.searchsorted(jnp.cumsum(tallies), jnp.arange(rows * top), side="right").astype(jnp.int32)
    listing = labels.reshape(top, rows).T
    listing = listing[jax.random.permutation(jax.random.fold_in(own, 1), rows)]
    offset_by = jax.random.randint(jax.random.fold_in(own, 2), (rows, 1), 0, top)
    return jnp.take_along_axis(listing, (jnp.arange(top)[None, :] + offset_by) % top, axis=1)


def load_shares(number_of, total, reach, skew, full):
    weights = [(1 << 20) // math.isqrt(standing ** skew) + 1 for standing in range(1, number_of + 1)]
    largest = reach if full else min(reach, max(-(-total // number_of), total * weights[0] // sum(weights)))
    least = 1 if total - largest >= number_of - 1 else 0
    given, surplus = [largest] + [least] * (number_of - 1), total - largest - least * (number_of - 1)
    while surplus > 0:
        free = [i for i in range(1, number_of) if given[i] < largest] or [i for i in range(1, number_of) if given[i] < reach]
        pool, remaining = sum([weights[i] for i in free]), surplus
        for i in free:
            extra = min(reach - given[i], max(1, remaining * weights[i] // pool), surplus)
            given[i] = given[i] + extra
            surplus = surplus - extra
    return np.array(given)


def scatter_about(rng, dims, scale, most, shards=(), dtype=jnp.bfloat16):
    level = levels(rng, dims, shards, -0.22, 0.18) if shards else 1.0
    values = jax.random.normal(rng, dims, jnp.float32) * scale * level
    return jnp.minimum(jnp.maximum(values, -most), most).astype(dtype)


def setup_inputs(seed: int = 0) -> dict:
    key_of = jax.random.split(jax.random.key(seed), 18)
    tokens = scatter_about(key_of[0], (TOKENS, D), 1.0, 6.0, ((0, 32),))
    doc_ids = jax.vmap(lambda own: jnp.searchsorted(jnp.cumsum(uneven_parts(own, 4, TOK_DEV, TOK_DEV // 2, 0)), jnp.arange(TOK_DEV), side="right"))(jax.random.split(key_of[1], SEQS)).reshape((SEQS, TOK_DEV)).astype(jnp.int32)
    routes_keys = jax.random.split(jax.random.fold_in(key_of[2], 1), TOKENS // TOK_DEV)
    routes_turns = jax.random.permutation(jax.random.fold_in(key_of[2], 3), TOKENS // TOK_DEV)
    routes = jax.vmap(lambda own, number: deal_out(jax.random.fold_in(key_of[2], 2), own, number, TOK_DEV, EXPERTS, TOP, CAP, 2))(routes_keys, routes_turns).reshape((TOKENS, TOP))
    gain_attn = jnp.clip(1.0 + 0.15 * jax.random.normal(key_of[3], (D,), jnp.float32), 0.25, 1.75).astype(jnp.bfloat16)
    w_query = scatter_about(key_of[4], (D, QW), D ** -0.5, 0.125, ((0, 32),))
    w_key = scatter_about(key_of[5], (D, KVW), D ** -0.5, 0.125, ((0, 32),))
    w_value = scatter_about(key_of[6], (D, KVW), D ** -0.5, 0.125, ((0, 32),))
    w_out = scatter_about(key_of[7], (QW, D), (QW // 16) ** -0.5, 0.5, ((0, 32),))
    gain_moe = jnp.clip(1.0 + 0.15 * jax.random.normal(key_of[8], (D,), jnp.float32), 0.25, 1.75).astype(jnp.bfloat16)
    w_router = scatter_about(key_of[9], (D, EXPERTS), (4 * D) ** -0.5, 0.0625, ((0, 32),))
    shared_gate = scatter_about(key_of[10], (D, SH), D ** -0.5, 0.125, ((0, 32),))
    shared_up = scatter_about(key_of[11], (D, SH), D ** -0.5, 0.125, ((0, 32),))
    shared_down = scatter_about(key_of[12], (SH, D), SH ** -0.5, 0.109375, ((0, 32),))
    expert_gate = scatter_about(key_of[13], (EXPERTS, D, FFE), D ** -0.5, 0.125, ((0, 8), (1, 4)))
    expert_up = scatter_about(key_of[14], (EXPERTS, D, FFE), D ** -0.5, 0.125, ((0, 8), (1, 4)))
    expert_down = scatter_about(key_of[15], (EXPERTS, D, FFE), (FFE // 8) ** -0.5, 0.4375, ((0, 8), (1, 4)))
    cotangent = scatter_about(key_of[16], (TOKENS, D), 1.0, 6.0, ((0, 32),))
    return {"tokens": tokens, "doc_ids": doc_ids, "routes": routes, "gain_attn": gain_attn, "w_query": w_query, "w_key": w_key, "w_value": w_value, "w_out": w_out, "gain_moe": gain_moe, "w_router": w_router, "shared_gate": shared_gate, "shared_up": shared_up, "shared_down": shared_down, "expert_gate": expert_gate, "expert_up": expert_up, "expert_down": expert_down, "cotangent": cotangent}


@jax.custom_vjp
def low(v):
    return lax.optimization_barrier(v.astype(jnp.bfloat16)).astype(jnp.float32)

@jax.custom_vjp
def low_back(v):
    return v

def low_keep(v):
    return (low(v), None)

def low_pass(kept, grad):
    return (grad,)

def back_keep(v):
    return (v, None)

def back_low(kept, grad):
    return (low(grad),)
low.defvjp(low_keep, low_pass)
low_back.defvjp(back_keep, back_low)
highest = lax.Precision.HIGHEST
epsilon = 1e-06
rope_base = 10000.0

def matmul(left, right):
    return jnp.dot(left, right, precision=highest)

def rms_norm(values, gain_row):
    factor = lax.rsqrt(lax.optimization_barrier(jnp.mean(values * values, axis=-1, keepdims=True)) + epsilon)
    return values * factor * gain_row

def rotate(values):
    length = values.shape[0]
    half_dim = values.shape[-1] // 2
    position = jnp.arange(length).astype(jnp.float32)
    inverse = rope_base ** (-jnp.arange(half_dim).astype(jnp.float32) * 2.0 / values.shape[-1])
    angle_table = position[:, None] * inverse[None, :]
    cosine = jnp.cos(angle_table)[:, None, :]
    sine_table = jnp.sin(angle_table)[:, None, :]
    lower_half = values[..., :half_dim]
    upper_half = values[..., half_dim:]
    return jnp.concatenate([lower_half * cosine - upper_half * sine_table, upper_half * cosine + lower_half * sine_table], axis=-1)

def route_slots(routes, experts_total, capacity):
    flat_routes = routes.reshape(-1).astype(jnp.int32)
    hit_table = (flat_routes[:, None] == jnp.arange(experts_total).astype(jnp.int32)[None, :]).astype(jnp.int32)
    before = jnp.cumsum(hit_table, axis=0).astype(jnp.int32) - hit_table
    return (flat_routes * capacity + lax.optimization_barrier(jnp.sum(before * hit_table, axis=1))).astype(jnp.int32)

def sequence_forward(params, seq_tokens, seq_routes, seq_docs):
    gain_attn, w_query, w_key, w_value, w_out, gain_moe, w_router, shared_gate, shared_up, shared_down, expert_gate, expert_up, expert_down = params
    length = seq_tokens.shape[0]
    group_size = HEADS // KV_HEADS
    normed = low(rms_norm(seq_tokens, gain_attn))
    queries = low(rotate(low_back(matmul(normed, w_query)).reshape(length, HEADS, HEAD_DIM)))
    keys = low(rotate(low_back(matmul(normed, w_key)).reshape(length, KV_HEADS, HEAD_DIM)))
    values = low(low_back(matmul(normed, w_value))).reshape(length, KV_HEADS, HEAD_DIM)
    grouped = queries.reshape(length, KV_HEADS, group_size, HEAD_DIM)
    scores = low_back(jnp.einsum('tkgd,skd->kgts', grouped, keys, precision=highest) * HEAD_DIM ** (-0.5))
    position = jnp.arange(length).astype(jnp.int32)
    allowed = (position[None, :] <= position[:, None]) & (seq_docs[None, :] == seq_docs[:, None])
    scores = jnp.where(allowed, scores, -1e+30)
    attend = low(jax.nn.softmax(scores, axis=-1))
    mixed_rows = jnp.einsum('kgts,skd->tkgd', attend, values, precision=highest).reshape(length, HEADS * HEAD_DIM)
    mixed_rows = low(low_back(mixed_rows))
    hidden = seq_tokens + low_back(matmul(mixed_rows, w_out))
    normed_moe = low(rms_norm(hidden, gain_moe))
    logits = low_back(matmul(normed_moe, w_router))
    chosen = jnp.take_along_axis(logits, seq_routes, axis=1)
    gate_weights = jax.nn.softmax(chosen, axis=-1)
    flat_slot = route_slots(seq_routes, EXPERTS, CAP)
    token_index = (jnp.arange(length * TOP) // TOP).astype(jnp.int32)
    slot_token = jnp.full((EXPERTS * CAP,), -1, jnp.int32).at[flat_slot].set(token_index)
    dispatch = (slot_token[:, None] == jnp.arange(length).astype(jnp.int32)[None, :]).astype(jnp.float32)
    buffer = low_back(matmul(dispatch, normed_moe)).reshape(EXPERTS, CAP, -1)
    gate_rows = low_back(jnp.einsum('ecd,edf->ecf', buffer, expert_gate, precision=highest))
    up_rows = low_back(jnp.einsum('ecd,edf->ecf', buffer, expert_up, precision=highest))
    inner_low = low(jax.nn.silu(gate_rows) * up_rows)
    produced = low(low_back(jnp.einsum('ecf,edf->ecd', inner_low, expert_down, precision=highest)))
    produced = produced.reshape(EXPERTS * CAP, -1)
    picked = jnp.take(produced, flat_slot, axis=0).reshape(length, TOP, -1)
    routed = lax.optimization_barrier(jnp.sum(gate_weights[:, :, None] * picked, axis=1))
    share_g = low_back(matmul(normed_moe, shared_gate))
    share_u = low_back(matmul(normed_moe, shared_up))
    share_low = low(jax.nn.silu(share_g) * share_u)
    shared_out = low_back(matmul(share_low, shared_down))
    return hidden + routed + shared_out

def reference(tokens, doc_ids, routes, gain_attn, w_query, w_key, w_value, w_out, gain_moe, w_router, shared_gate, shared_up, shared_down, expert_gate, expert_up, expert_down, cotangent):
    params = tuple((weight.astype(jnp.float32) for weight in (gain_attn, w_query, w_key, w_value, w_out, gain_moe, w_router, shared_gate, shared_up, shared_down, expert_gate, expert_up, expert_down)))
    inputs = tokens.astype(jnp.float32)
    width = inputs.shape[1]
    seq_routes_all = routes.reshape(-1, TOK_DEV, TOP)

    def forward(layer_in, layer_params):

        def step(carried, sequence_item):
            seq_tokens, seq_routes, seq_docs = sequence_item
            return (carried, sequence_forward(layer_params, seq_tokens, seq_routes, seq_docs))
        stepped = jax.checkpoint(step)
        carried, outputs = lax.scan(stepped, jnp.zeros((), jnp.float32), (layer_in.reshape(-1, TOK_DEV, width), seq_routes_all, doc_ids))
        return outputs.reshape(-1, width)
    output, pullback = jax.vjp(forward, inputs, params)
    grad_tokens, grads = pullback(cotangent.astype(jnp.float32))
    return (output.astype(jnp.bfloat16), grad_tokens, grads[0], grads[1], grads[2], grads[3], grads[4], grads[5], grads[6], grads[7], grads[8], grads[9], grads[10], grads[11], grads[12])
```

```python
import functools

import jax
import jax.numpy as jnp
from jax import lax
from jax.experimental import pallas as pl
from jax.experimental.pallas import tpu as pltpu
from jax.sharding import Mesh
from jax.sharding import PartitionSpec as P

HEADS = 16
KV_HEADS = 4
HEAD_DIM = 128
TOP = 6
EPS = 1e-06
ROPE_BASE = 10000.0
PLANE = ("a", "b", "l")
ALL = ("a", "b", "l", "s")
F32 = jnp.float32
BF16 = jnp.bfloat16
MESH = pl.DeviceIdType.MESH
VMEM_LIMIT = 60 * 1024 * 1024


def dot(left, right):
    return jnp.dot(left, right, preferred_element_type=F32)


def dot_tn(left, right):
    return lax.dot_general(left, right, (((0,), (0,)), ((), ())), preferred_element_type=F32)


def dot_nt(left, right):
    return lax.dot_general(left, right, (((1,), (1,)), ((), ())), preferred_element_type=F32)


class Grid:
    def __init__(self, sizes):
        self.na, self.nb, self.nl, self.ns = sizes
        self.a, self.b, self.l, self.s = (lax.axis_index(axis) for axis in "abls")

    def at(self, a=None, b=None, l=None, s=None):
        return tuple(
            own if other is None else other
            for own, other in zip((self.a, self.b, self.l, self.s), (a, b, l, s))
        )

    def other(self, axis, step):
        size, own = {"b": (self.nb, self.b), "l": (self.nl, self.l), "s": (self.ns, self.s)}[axis]
        return lax.rem(own + step, size)

    def greet(self, siblings):
        barrier = pltpu.get_barrier_semaphore()

        def hello(device):
            pl.semaphore_signal(barrier, inc=1, device_id=device, device_id_type=MESH)

        @pl.when(self.a > 0)
        def _():
            hello(self.at(a=self.a - 1))

        @pl.when(self.a < self.na - 1)
        def _():
            hello(self.at(a=self.a + 1))

        for step in range(1, self.nb):
            hello(self.at(b=self.other("b", step)))
        for step in range(1, self.nl):
            hello(self.at(l=self.other("l", step)))
        count = self.nb + self.nl - 2
        if siblings:
            for step in range(1, self.ns):
                hello(self.at(s=self.other("s", step)))
            count += self.ns - 1
        above = 1 - (self.a + 1) // self.na
        below = (self.a + self.na - 1) // self.na
        pl.semaphore_wait(barrier, count + above + below)


def remote(src, dst, send, recv, device):
    return pltpu.make_async_remote_copy(
        src_ref=src, dst_ref=dst, send_sem=send, recv_sem=recv, device_id=device, device_id_type=MESH
    )


def gather_kernel(sizes, siblings, x_ref, o_ref, own_sem, a_sem, b_sem, l_sem, bb_sem, ll_sem, s_sem):
    g = Grid(sizes)
    na, nb, nl, ns = sizes
    wide = x_ref.shape[-1]
    half = (wide // 256) * 128
    first, second = pl.ds(0, half), pl.ds(half, wide - half)
    me = g.s if siblings else 0
    g.greet(siblings)

    def slot(a, b, l, s=None):
        return o_ref.at[a, b, l, me if s is None else s]

    own = pltpu.make_async_copy(x_ref, slot(g.a, g.b, g.l), own_sem)
    own.start()
    sends = []

    def up(k):
        src = x_ref if k == 0 else slot(g.a - k, g.b, g.l)
        return remote(src, slot(g.a - k, g.b, g.l), a_sem.at[0, 0, k], a_sem.at[1, 0, k], g.at(a=g.a + 1))

    def down(k):
        src = x_ref if k == 0 else slot(g.a + k, g.b, g.l)
        return remote(src, slot(g.a + k, g.b, g.l), a_sem.at[0, 1, k], a_sem.at[1, 1, k], g.at(a=g.a - 1))

    def came(sem, dst):
        remote(dst, dst, sem, sem, g.at()).wait_recv()

    def sibling_sends(index, own_x=False):
        if siblings:
            a, b, l = index
            for step in range(1, ns):
                remote(
                    x_ref if own_x else slot(a, b, l),
                    slot(a, b, l),
                    s_sem.at[0, step - 1, a, b, l],
                    s_sem.at[1, step - 1, a, b, l],
                    g.at(s=g.other("s", step)),
                ).start()

    def spread(origin, own_x=False):
        src = x_ref if own_x else slot(origin, g.b, g.l)
        dst = slot(origin, g.b, g.l)
        for step in range(1, nb):
            remote(src, dst, b_sem.at[0, step - 1, origin], b_sem.at[1, step - 1, origin], g.at(b=g.other("b", step))).start()
        for step in range(1, nl):
            remote(src, dst, l_sem.at[0, step - 1, origin], l_sem.at[1, step - 1, origin], g.at(l=g.other("l", step))).start()
        sibling_sends((origin, g.b, g.l), own_x)

    def relay(origin):
        for step in range(1, nb):
            b_from = g.other("b", nb - step)
            came(b_sem.at[1, step - 1, origin], slot(origin, b_from, g.l))
            for turn in range(1, nl):
                part = slot(origin, b_from, g.l).at[:, first]
                remote(part, part, ll_sem.at[0, step - 1, turn - 1, origin], ll_sem.at[1, step - 1, turn - 1, origin], g.at(l=g.other("l", turn))).start()
            sibling_sends((origin, b_from, g.l))
        for step in range(1, nl):
            l_from = g.other("l", nl - step)
            came(l_sem.at[1, step - 1, origin], slot(origin, g.b, l_from))
            for turn in range(1, nb):
                part = slot(origin, g.b, l_from).at[:, second]
                remote(part, part, bb_sem.at[0, step - 1, turn - 1, origin], bb_sem.at[1, step - 1, turn - 1, origin], g.at(b=g.other("b", turn))).start()
            sibling_sends((origin, g.b, l_from))

    def finish(origin):
        for step in range(1, nb):
            b_from = g.other("b", nb - step)
            for turn in range(1, nl):
                l_from = g.other("l", nl - turn)
                came(ll_sem.at[1, step - 1, turn - 1, origin], slot(origin, b_from, l_from).at[:, first])
                came(bb_sem.at[1, turn - 1, step - 1, origin], slot(origin, b_from, l_from).at[:, second])
                sibling_sends((origin, b_from, l_from))

    has_up, has_down = g.a < na - 1, g.a > 0

    @pl.when(has_up)
    def _():
        up(0).start()

    @pl.when(has_down)
    def _():
        down(0).start()

    spread(g.a, True)
    for k in range(na - 1):
        @pl.when(g.a - 1 - k >= 0)
        def _():
            came(a_sem.at[1, 0, k], slot(g.a - 1 - k, g.b, g.l))
            if k + 1 < na - 1:
                @pl.when(has_up)
                def _():
                    up(k + 1).start()
            spread(g.a - 1 - k)

        @pl.when(g.a + 1 + k < na)
        def _():
            came(a_sem.at[1, 1, k], slot(g.a + 1 + k, g.b, g.l))
            if k + 1 < na - 1:
                @pl.when(has_down)
                def _():
                    down(k + 1).start()
            spread(g.a + 1 + k)

        if k == 0:
            relay(g.a)
        else:
            @pl.when(g.a - k >= 0)
            def _():
                relay(g.a - k)

            @pl.when(g.a + k < na)
            def _():
                relay(g.a + k)

    last = na - 1

    @pl.when(g.a - last >= 0)
    def _():
        relay(g.a - last)

    @pl.when(g.a + last < na)
    def _():
        relay(g.a + last)

    for origin in range(na):
        finish(origin)
    own.wait()
    for k in range(na - 1):
        @pl.when(has_up & (g.a - k >= 0))
        def _():
            up(k).wait_send()

        @pl.when(has_down & (g.a + k < na))
        def _():
            down(k).wait_send()

    def left(sem, ref):
        remote(ref, ref, sem, sem, g.at()).wait_send()

    for origin in range(na):
        whole = slot(origin, g.b, g.l)
        for step in range(1, nb):
            left(b_sem.at[0, step - 1, origin], whole)
            for turn in range(1, nl):
                left(ll_sem.at[0, step - 1, turn - 1, origin], whole.at[:, first])
        for step in range(1, nl):
            left(l_sem.at[0, step - 1, origin], whole)
            for turn in range(1, nb):
                left(bb_sem.at[0, step - 1, turn - 1, origin], whole.at[:, second])
        if siblings:
            for b in range(nb):
                for l in range(nl):
                    for step in range(1, ns):
                        s_from = g.other("s", ns - step)
                        came(s_sem.at[1, step - 1, origin, b, l], slot(origin, b, l, s_from))
                        left(s_sem.at[0, step - 1, origin, b, l], slot(origin, b, l))


def gather(x, sizes, siblings, collective_id):
    na, nb, nl, ns = sizes
    rows, wide = x.shape
    depth = ns if siblings else 1
    dma = pltpu.SemaphoreType.DMA
    out = pl.pallas_call(
        functools.partial(gather_kernel, sizes, siblings),
        out_shape=jax.ShapeDtypeStruct((na, nb, nl, depth, rows, wide), x.dtype),
        in_specs=[pl.BlockSpec(memory_space=pl.ANY)],
        out_specs=pl.BlockSpec(memory_space=pl.ANY),
        scratch_shapes=[
            dma,
            dma((2, 2, na - 1)),
            dma((2, nb - 1, na)),
            dma((2, nl - 1, na)),
            dma((2, nl - 1, nb - 1, na)),
            dma((2, nb - 1, nl - 1, na)),
            dma((2, max(ns - 1, 1), na, nb, nl)),
        ],
        compiler_params=pltpu.CompilerParams(collective_id=collective_id, has_side_effects=True),
        cost_estimate=pl.CostEstimate(flops=0, bytes_accessed=2 * na * nb * nl * depth * rows * wide * 2, transcendentals=0),
    )(x)
    return out.reshape(-1, wide)


def order(a, k):
    high, odd = a // 2, lax.rem(a, 2)
    return (3 * (1 - high), 2 + high - 2 * odd, 1 + odd, a)[k]


def add_rows(out, *terms):
    rows = out.shape[0]
    step = min(rows, 32)

    @pl.loop(0, rows, step=step)
    def _(r):
        at = pl.ds(pl.multiple_of(r, step), step)
        total = terms[0][at, :].astype(F32)
        for term in terms[1:]:
            total = total + term[at, :].astype(F32)
        out[at, :] = total.astype(out.dtype)


def scatter_kernel(sizes, siblings, p_ref, o_ref, l_one, b_one, b_two, l_two, total, line, s_buf,
                   l_sem, b_sem, bb_sem, ll_sem, a_sem, s_sem):
    g = Grid(sizes)
    na, nb, nl, ns = sizes
    wide = o_ref.shape[-1]
    half = (wide // 256) * 128
    first, second = pl.ds(0, half), pl.ds(half, wide - half)
    g.greet(siblings)

    def part(k, b, l, cols):
        if siblings:
            return s_buf.at[0, k, b, l, :, cols]
        return p_ref.at[order(g.a, k), b, l, 0, :, cols]

    def sibling_copy(k, step):
        to = g.other("s", step)
        return remote(p_ref.at[order(g.a, k), :, :, to], s_buf.at[step - 1, k],
                      s_sem.at[0, step - 1, k], s_sem.at[1, step - 1, k], g.at(s=to))

    def l_first(k, step):
        to = g.other("l", step)
        if siblings:
            src = s_buf.at[0, k, :, to, :, first]
        else:
            src = p_ref.at[order(g.a, k), :, to, 0, :, first]
        return remote(src, l_one.at[step - 1, k], l_sem.at[0, step - 1, k], l_sem.at[1, step - 1, k], g.at(l=to))

    def b_first(k, step):
        to = g.other("b", step)
        if siblings:
            src = s_buf.at[0, k, to, :, :, second]
        else:
            src = p_ref.at[order(g.a, k), to, :, 0, :, second]
        return remote(src, b_one.at[step - 1, k], b_sem.at[0, step - 1, k], b_sem.at[1, step - 1, k], g.at(b=to))

    def b_then(k, step):
        to = g.other("b", step)
        return remote(l_one.at[0, k, to], b_two.at[step - 1, k], bb_sem.at[0, step - 1, k], bb_sem.at[1, step - 1, k], g.at(b=to))

    def l_then(k, step):
        to = g.other("l", step)
        return remote(b_one.at[0, k, to], l_two.at[step - 1, k], ll_sem.at[0, step - 1, k], ll_sem.at[1, step - 1, k], g.at(l=to))

    def line_copy(k, way):
        dest = order(g.a, k)
        return remote(total.at[k], line.at[way, dest], a_sem.at[0, way, dest], a_sem.at[1, way, dest], g.at(a=g.a + 1 - 2 * way))

    def line_came(way, dest):
        remote(line.at[way, dest], line.at[way, dest], a_sem.at[1, way, dest], a_sem.at[1, way, dest], g.at()).wait_recv()

    def start_first(k):
        if siblings:
            for step in range(1, ns):
                sibling_copy(k, step).wait_recv()
            for b in range(nb):
                for l in range(nl):
                    add_rows(s_buf.at[0, k, b, l], p_ref.at[order(g.a, k), b, l, g.s], *[s_buf.at[step, k, b, l] for step in range(ns - 1)])
        for step in range(1, nl):
            l_first(k, step).start()
        for step in range(1, nb):
            b_first(k, step).start()

    def start_second(k):
        for step in range(1, nl):
            l_first(k, step).wait_recv()
        for turn in range(nb):
            b = g.other("b", turn)
            add_rows(l_one.at[0, k, b], part(k, b, g.l, first), *[l_one.at[step, k, b] for step in range(nl - 1)])
            if turn:
                b_then(k, turn).start()
        for step in range(1, nb):
            b_first(k, step).wait_recv()
        for turn in range(nl):
            l = g.other("l", turn)
            add_rows(b_one.at[0, k, l], part(k, g.b, l, second), *[b_one.at[step, k, l] for step in range(nb - 1)])
            if turn:
                l_then(k, turn).start()

    def start_third(k):
        for step in range(1, nb):
            b_then(k, step).wait_recv()
        add_rows(total.at[k, :, first], l_one.at[0, k, g.b], *[b_two.at[step, k] for step in range(nb - 1)])
        for step in range(1, nl):
            l_then(k, step).wait_recv()
        add_rows(total.at[k, :, second], b_one.at[0, k, g.l], *[l_two.at[step, k] for step in range(nl - 1)])
        if k < na - 1:
            dest = order(g.a, k)

            @pl.when((g.a == 0) & (dest > g.a))
            def _():
                line_copy(k, 0).start()

            @pl.when((g.a == na - 1) & (dest < g.a))
            def _():
                line_copy(k, 1).start()

    def pass_on(k):
        dest = order(g.a, k)

        @pl.when((g.a > 0) & (dest > g.a))
        def _():
            line_came(0, dest)
            add_rows(total.at[k], total.at[k], line.at[0, dest])
            line_copy(k, 0).start()

        @pl.when((g.a < na - 1) & (dest < g.a))
        def _():
            line_came(1, dest)
            add_rows(total.at[k], total.at[k], line.at[1, dest])
            line_copy(k, 1).start()

    if siblings:
        for k in range(na):
            for step in range(1, ns):
                sibling_copy(k, step).start()
    start_first(0)
    start_first(1)
    for k in range(na):
        start_second(k)
        if k + 2 < na:
            start_first(k + 2)
        if k >= 1:
            start_third(k - 1)
        if k >= 2:
            pass_on(k - 2)
    start_third(na - 1)
    pass_on(na - 2)

    last = total.at[na - 1]

    @pl.when(g.a == 0)
    def _():
        line_came(1, g.a)
        add_rows(o_ref, last, line.at[1, g.a])

    @pl.when(g.a == na - 1)
    def _():
        line_came(0, g.a)
        add_rows(o_ref, last, line.at[0, g.a])

    @pl.when((g.a > 0) & (g.a < na - 1))
    def _():
        line_came(0, g.a)
        line_came(1, g.a)
        add_rows(o_ref, last, line.at[0, g.a], line.at[1, g.a])

    for k in range(na):
        if siblings:
            for step in range(1, ns):
                sibling_copy(k, step).wait_send()
        for step in range(1, nl):
            l_first(k, step).wait_send()
            l_then(k, step).wait_send()
        for step in range(1, nb):
            b_first(k, step).wait_send()
            b_then(k, step).wait_send()
        if k < na - 1:
            dest = order(g.a, k)

            @pl.when(dest > g.a)
            def _():
                line_copy(k, 0).wait_send()

            @pl.when(dest < g.a)
            def _():
                line_copy(k, 1).wait_send()


def scatter(partial, sizes, siblings, collective_id, dtype=F32):
    na, nb, nl, ns = sizes
    depth = ns if siblings else 1
    places = na * nb * nl * depth
    rows, wide = partial.shape[0] // places, partial.shape[1]
    half = (wide // 256) * 128
    dma = pltpu.SemaphoreType.DMA
    vmem = pl.BlockSpec(memory_space=pltpu.VMEM)
    return pl.pallas_call(
        functools.partial(scatter_kernel, sizes, siblings),
        out_shape=jax.ShapeDtypeStruct((rows, wide), dtype),
        in_specs=[vmem],
        out_specs=vmem,
        scratch_shapes=[
            pltpu.VMEM((nl - 1, na, nb, rows, half), BF16),
            pltpu.VMEM((nb - 1, na, nl, rows, wide - half), BF16),
            pltpu.VMEM((nb - 1, na, rows, half), BF16),
            pltpu.VMEM((nl - 1, na, rows, wide - half), BF16),
            pltpu.VMEM((na, rows, wide), BF16),
            pltpu.VMEM((2, na, rows, wide), BF16),
            pltpu.VMEM((ns - 1, na, nb, nl, rows, wide) if siblings else (16, 128), BF16),
            dma((2, nl - 1, na)),
            dma((2, nb - 1, na)),
            dma((2, nb - 1, na)),
            dma((2, nl - 1, na)),
            dma((2, 2, na)),
            dma((2, max(ns - 1, 1), na)),
        ],
        compiler_params=pltpu.CompilerParams(collective_id=collective_id, has_side_effects=True, vmem_limit_bytes=VMEM_LIMIT),
        cost_estimate=pl.CostEstimate(flops=0, bytes_accessed=4 * partial.size, transcendentals=0),
    )(partial.reshape(na, nb, nl, depth, rows, wide))


def rms_norm(values, gain_row):
    factor = lax.rsqrt(jnp.mean(values * values, axis=-1, keepdims=True) + EPS)
    return values * factor * gain_row


def rotate(values):
    length = values.shape[0]
    half_dim = values.shape[-1] // 2
    position = jnp.arange(length).astype(F32)
    inverse = ROPE_BASE ** (-jnp.arange(half_dim).astype(F32) * 2.0 / values.shape[-1])
    angle_table = position[:, None] * inverse[None, :]
    cosine = jnp.cos(angle_table)[:, None, :]
    sine = jnp.sin(angle_table)[:, None, :]
    lower = values[..., :half_dim]
    upper = values[..., half_dim:]
    return jnp.concatenate(
        [lower * cosine - upper * sine, upper * cosine + lower * sine], axis=-1
    )


def silu_pair(gate_part, up_part):
    return jax.nn.silu(gate_part) * up_part


def ring(axis, step):
    size = lax.axis_size(axis)
    return [(i, (i + step) % size) for i in range(size)]


def pick(parts, index):
    return lax.dynamic_index_in_dim(parts, index, 0, keepdims=False)


def plane_gather(block):
    return lax.all_gather(block, PLANE, axis=0, tiled=True)


def expert_gather(shard):
    ranks, rows, ffe = shard.shape
    sub = lax.axis_size("s")
    l, s = lax.axis_index("l"), lax.axis_index("s")
    whole = jnp.zeros((ranks, sub, rows, ffe), shard.dtype)

    def place(whole, block, at_l, at_s):
        return lax.dynamic_update_slice(whole, block[None, None], (at_l, at_s, 0, 0))

    for turn in range(ranks):
        block = pick(shard, (l + turn) % ranks)
        if turn:
            block = lax.ppermute(block, "l", ring("l", turn))
        from_l = (l - turn) % ranks
        whole = place(whole, block, from_l, s)
        for step in range(1, sub):
            whole = place(whole, lax.ppermute(block, "s", ring("s", step)), from_l, (s - step) % sub)
    return whole.reshape(-1, ffe)


def expert_scatter(partial, ranks):
    depth, ffe = partial.shape
    sub = lax.axis_size("s")
    l, s = lax.axis_index("l"), lax.axis_index("s")
    rows = depth // (ranks * sub)
    parts = partial.astype(BF16).reshape(ranks, sub, rows, ffe).transpose(1, 0, 2, 3)
    total = pick(parts, s).astype(F32)
    for step in range(1, sub):
        total = total + lax.ppermute(pick(parts, (s + step) % sub), "s", ring("s", step)).astype(F32)
    out = jnp.zeros((ranks, rows, ffe), F32)
    for turn in range(ranks):
        block = pick(total, (l + turn) % ranks)
        if turn:
            block = lax.ppermute(block.astype(BF16), "l", ring("l", turn)).astype(F32)
        out = lax.dynamic_update_slice(out, block[None], ((l - turn) % ranks, 0, 0))
    return out


def columns_gather(shard, groups):
    rows, wide = shard.shape
    parts = shard.reshape(rows, groups, wide // groups).transpose(1, 0, 2)
    mine = lax.all_to_all(parts, PLANE, split_axis=0, concat_axis=0, tiled=True)
    both = lax.all_gather(mine, "s", axis=1, tiled=False)
    return both.reshape(-1, wide // groups)


def columns_scatter(partial, groups, sub):
    depth, narrow = partial.shape
    rows = depth // (groups * sub)
    parts = partial.reshape(groups, sub, rows, narrow)
    mine = lax.psum_scatter(parts, "s", scatter_dimension=1, tiled=False)
    back = lax.all_to_all(mine, PLANE, split_axis=0, concat_axis=0, tiled=True)
    return back.transpose(1, 0, 2).reshape(rows, groups * narrow)


def shards(
    tokens,
    doc_ids,
    routes,
    gain_attn,
    w_query,
    w_key,
    w_value,
    w_out,
    gain_moe,
    w_router,
    shared_gate,
    shared_up,
    shared_down,
    expert_gate,
    expert_up,
    expert_down,
    cotangent,
):
    length, width = tokens.shape
    group_size = HEADS // KV_HEADS
    score_scale = HEAD_DIM ** (-0.5)
    local_experts = expert_gate.shape[0]
    sub = lax.axis_size("s")
    groups = lax.axis_size("a") * lax.axis_size("b") * lax.axis_size("l")
    experts_total = groups
    capacity = length * TOP * 4 // (3 * experts_total)
    sizes = tuple(lax.axis_size(axis) for axis in ALL)
    my_expert = lax.axis_index(PLANE)
    kvw = w_key.shape[1]
    qw = w_query.shape[1]

    small = jnp.concatenate(
        [w_router, gain_attn[:, None], gain_moe[:, None]], axis=1
    )
    small = jnp.pad(small, ((0, 0), (0, 128 - small.shape[1])))
    dense = gather(
        jnp.concatenate([w_query, w_key, w_value, w_out, small], axis=1), sizes, True, 1
    )
    query_full = dense[:, :qw]
    key_full = dense[:, qw : qw + kvw]
    value_full = dense[:, qw + kvw : qw + 2 * kvw]
    out_full = dense[:, qw + 2 * kvw : qw + 2 * kvw + width]
    rest = dense[:, qw + 2 * kvw + width :]
    router_full = rest[:, :experts_total]
    attn_gain = rest[:, experts_total].astype(F32)
    moe_gain = rest[:, experts_total + 1].astype(F32)

    dy_all = plane_gather(cotangent)
    routes_all = plane_gather(routes)
    wg, wu, wd = expert_gather(expert_gate), expert_gather(expert_up), expert_gather(expert_down)
    sg_w = columns_gather(shared_gate, groups)
    su_w = columns_gather(shared_up, groups)
    sd_w = lax.all_gather(shared_down, "s", axis=0, tiled=True)

    inputs = tokens.astype(F32)
    normed, attn_norm_pull = jax.vjp(rms_norm, inputs, attn_gain)
    normed_low = normed.astype(BF16)
    query_pre = dot(normed_low, query_full).reshape(length, HEADS, HEAD_DIM)
    key_pre = dot(normed_low, key_full).reshape(length, KV_HEADS, HEAD_DIM)
    value_low = dot(normed_low, value_full).astype(BF16).reshape(length, KV_HEADS, HEAD_DIM)
    query_rot, query_pull = jax.vjp(rotate, query_pre)
    key_rot, key_pull = jax.vjp(rotate, key_pre)
    query_low = query_rot.astype(BF16).reshape(length, KV_HEADS, group_size, HEAD_DIM)
    key_low = key_rot.astype(BF16)
    position = jnp.arange(length)
    doc_row = doc_ids[0]
    allowed = (position[None, :] <= position[:, None]) & (doc_row[None, :] == doc_row[:, None])
    scores = (
        jnp.einsum("tkgd,skd->kgts", query_low, key_low, preferred_element_type=F32) * score_scale
    )
    scores = jnp.where(allowed, scores, -1e30)
    exp_scores = jnp.exp(scores - jnp.max(scores, axis=-1, keepdims=True))
    attend = exp_scores / jnp.sum(exp_scores, axis=-1, keepdims=True)
    attend_low = attend.astype(BF16)
    mixed_low = (
        jnp.einsum("kgts,skd->tkgd", attend_low, value_low, preferred_element_type=F32)
        .reshape(length, HEADS * HEAD_DIM)
        .astype(BF16)
    )
    hidden = inputs + dot(mixed_low, out_full)
    normed_moe, moe_norm_pull = jax.vjp(rms_norm, hidden, moe_gain)
    moe_low = normed_moe.astype(BF16)

    x_all = gather(moe_low, sizes, False, 2)
    seqs = groups
    chosen_hot = jnp.any(
        routes_all[:, :, None] == jnp.arange(experts_total)[None, None, :], axis=1
    )
    logits = dot(x_all, router_full)
    logits = jnp.where(chosen_hot, logits, -1e30)
    gates = jax.nn.softmax(logits, axis=-1)
    mine = jnp.any(routes_all == my_expert, axis=1).reshape(seqs, length)
    my_gate = jnp.sum(
        jnp.where(jnp.arange(experts_total)[None, :] == my_expert, gates, 0.0), axis=1
    ).reshape(seqs, length)
    hits = mine.astype(jnp.int32)
    before = jnp.cumsum(hits, axis=1) - hits
    pick = (jnp.arange(capacity)[None, :, None] == before[:, None, :]) & mine[:, None, :]
    pick_low = pick.astype(BF16)
    slot_gate = jnp.sum(jnp.where(pick, my_gate[:, None, :], 0.0), axis=2)
    x_rows = jnp.einsum(
        "nst,ntd->nsd", pick_low, x_all.reshape(seqs, length, width), preferred_element_type=F32
    )
    x_rows = x_rows.astype(BF16).reshape(-1, width)
    dy_rows = jnp.einsum(
        "nst,ntd->nsd", pick_low, dy_all.reshape(seqs, length, width), preferred_element_type=F32
    ).reshape(-1, width)
    slot_gate = slot_gate.reshape(-1, 1)
    gate_rows = dot(x_rows, wg)
    up_rows = dot(x_rows, wu)
    inner, expert_pull = jax.vjp(silu_pair, gate_rows, up_rows)
    inner_low = inner.astype(BF16)
    produced = dot_nt(inner_low, wd)
    scaled = (slot_gate * produced).astype(BF16).reshape(seqs, capacity, width)
    share_g = dot(x_all, sg_w)
    share_u = dot(x_all, su_w)
    share, share_pull = jax.vjp(silu_pair, share_g, share_u)
    share_low = share.astype(BF16)
    part = (
        jnp.einsum("nst,nsd->ntd", pick_low, scaled, preferred_element_type=F32).reshape(-1, width)
        + dot(share_low, sd_w)
    ).astype(BF16)
    moe_out = scatter(part, sizes, False, 3)
    output = (hidden + moe_out).astype(BF16)

    slot_grad = jnp.sum(dy_rows * produced, axis=1).reshape(seqs, 1, capacity)
    gate_grad = jnp.sum(
        jnp.where(pick.transpose(0, 2, 1), slot_grad, 0.0), axis=2
    )
    gate_grad = lax.all_to_all(gate_grad, PLANE, split_axis=0, concat_axis=0, tiled=True)
    gp = (slot_gate * dy_rows).astype(BF16)
    d_inner = dot(gp, wd)
    dg, du = expert_pull(d_inner)
    dg = dg.astype(BF16)
    du = du.astype(BF16)
    d_share = dot_nt(dy_all, sd_w)
    dsg, dsu = share_pull(d_share)
    dsg = dsg.astype(BF16)
    dsu = dsu.astype(BF16)
    back_rows = (dot_nt(dg, wg) + dot_nt(du, wu)).astype(BF16).reshape(seqs, capacity, width)
    dx_part = (
        jnp.einsum("nst,nsd->ntd", pick_low, back_rows, preferred_element_type=F32).reshape(
            -1, width
        )
        + dot_nt(dsg, sg_w)
        + dot_nt(dsu, su_w)
    ).astype(BF16)
    dx = scatter(dx_part, sizes, False, 4)
    grad_expert_down = expert_scatter(dot_tn(gp, inner_low), local_experts)
    grad_expert_gate = expert_scatter(dot_tn(x_rows, dg), local_experts)
    grad_expert_up = expert_scatter(dot_tn(x_rows, du), local_experts)
    grad_shared_gate = columns_scatter(dot_tn(x_all, dsg), groups, sub)
    grad_shared_up = columns_scatter(dot_tn(x_all, dsu), groups, sub)
    grad_shared_down = lax.psum_scatter(
        dot_tn(share_low, dy_all), "s", scatter_dimension=0, tiled=True
    )

    own_hot = jnp.any(routes[:, :, None] == jnp.arange(experts_total)[None, None, :], axis=1)
    own_logits = jnp.where(own_hot, dot(moe_low, router_full), -1e30)
    own_gates = jax.nn.softmax(own_logits, axis=-1)
    grad_gate = gate_grad.reshape(experts_total, length).T
    grad_logits = own_gates * (
        grad_gate - jnp.sum(own_gates * grad_gate, axis=-1, keepdims=True)
    )
    grad_logits = grad_logits.astype(BF16)
    grad_router = dot_tn(moe_low, grad_logits)
    dx = dx + dot_nt(grad_logits, router_full)
    grad_hidden_norm, grad_gain_moe = moe_norm_pull(dx)
    grad_hidden = cotangent.astype(F32) + grad_hidden_norm

    grad_hidden_low = grad_hidden.astype(BF16)
    grad_out_proj = dot_tn(mixed_low, grad_hidden_low)
    grad_mixed = (
        dot_nt(grad_hidden_low, out_full)
        .astype(BF16)
        .reshape(length, KV_HEADS, group_size, HEAD_DIM)
    )
    grad_value = jnp.einsum("kgts,tkgd->skd", attend_low, grad_mixed, preferred_element_type=F32)
    grad_attend = jnp.einsum("tkgd,skd->kgts", grad_mixed, value_low, preferred_element_type=F32)
    grad_scores = (
        attend * (grad_attend - jnp.sum(grad_attend * attend, axis=-1, keepdims=True))
    ).astype(BF16)
    grad_query = (
        jnp.einsum("kgts,skd->tkgd", grad_scores, key_low, preferred_element_type=F32) * score_scale
    )
    grad_key = (
        jnp.einsum("kgts,tkgd->skd", grad_scores, query_low, preferred_element_type=F32)
        * score_scale
    )
    grad_query_low = (
        query_pull(grad_query.reshape(length, HEADS, HEAD_DIM))[0].reshape(length, -1).astype(BF16)
    )
    grad_key_low = key_pull(grad_key)[0].reshape(length, -1).astype(BF16)
    grad_value_low = grad_value.reshape(length, -1).astype(BF16)
    grad_normed = (
        dot_nt(grad_query_low, query_full)
        + dot_nt(grad_key_low, key_full)
        + dot_nt(grad_value_low, value_full)
    )
    grad_inputs_norm, grad_gain_attn = attn_norm_pull(grad_normed)
    grad_tokens = grad_hidden + grad_inputs_norm
    grad_small = jnp.concatenate(
        [grad_router, grad_gain_attn[:, None], grad_gain_moe[:, None]], axis=1
    )
    grad_small = jnp.pad(grad_small, ((0, 0), (0, 128 - grad_small.shape[1])))
    dense_grads = jnp.concatenate(
        [
            dot_tn(normed_low, grad_query_low).astype(BF16),
            dot_tn(normed_low, grad_key_low).astype(BF16),
            dot_tn(normed_low, grad_value_low).astype(BF16),
            grad_out_proj.astype(BF16),
            grad_small.astype(BF16),
        ],
        axis=1,
    )
    total = scatter(dense_grads, sizes, True, 5)
    dense_sum, small_sum = total[:, :-128], total[:, -128:]
    return (
        output,
        grad_tokens,
        small_sum[:, experts_total],
        dense_sum[:, :qw],
        dense_sum[:, qw : qw + kvw],
        dense_sum[:, qw + kvw : qw + 2 * kvw],
        dense_sum[:, qw + 2 * kvw :],
        small_sum[:, experts_total + 1],
        small_sum[:, :experts_total],
        grad_shared_gate,
        grad_shared_up,
        grad_shared_down,
        grad_expert_gate,
        grad_expert_up,
        grad_expert_down,
    )


def solution(mesh):
    ranks, shards_of = mesh.shape["expert"], mesh.shape["dp"]
    local_experts = 2
    split = Mesh(
        mesh.devices.reshape(4, ranks // 4, local_experts, shards_of // local_experts), ALL
    )
    rows = P(ALL, None)
    flat = P(ALL)
    expert = P(("a", "b"), ("l", "s"), None)
    return jax.shard_map(
        shards,
        mesh=split,
        in_specs=(rows,) * 3
        + (flat,)
        + (rows,) * 4
        + (flat,)
        + (rows,) * 4
        + (expert,) * 3
        + (rows,),
        out_specs=(rows,) * 2
        + (flat,)
        + (rows,) * 4
        + (flat,)
        + (rows,) * 4
        + (expert,) * 3,
        check_vma=False,
    )
```

```python
import functools

import jax
import jax.numpy as jnp
from jax import lax
from jax.experimental import pallas as pl
from jax.experimental.pallas import tpu as pltpu
from jax.sharding import Mesh
from jax.sharding import PartitionSpec as P

HEADS = 16
KV_HEADS = 4
HEAD_DIM = 128
TOP = 6
EPS = 1e-06
ROPE_BASE = 10000.0
PLANE = ("a", "b", "l")
ALL = ("a", "b", "l", "s")
F32 = jnp.float32
BF16 = jnp.bfloat16
MESH = pl.DeviceIdType.MESH
VMEM_LIMIT = 60 * 1024 * 1024
DMA = pltpu.SemaphoreType.DMA
ANY = pl.BlockSpec(memory_space=pl.ANY)
VMEM = pl.BlockSpec(memory_space=pltpu.VMEM)


def dot(left, right):
    return jnp.dot(left, right, preferred_element_type=F32)


def dot_tn(left, right):
    return lax.dot_general(left, right, (((0,), (0,)), ((), ())), preferred_element_type=F32)


def dot_nt(left, right):
    return lax.dot_general(left, right, (((1,), (1,)), ((), ())), preferred_element_type=F32)


class Grid:
    def __init__(self, sizes):
        self.na, self.nb, self.nl, self.ns = self.sizes = sizes
        self.a, self.b, self.l, self.s = (lax.axis_index(axis) for axis in "abls")
        self.is_up = self.a < self.na - 1
        self.is_down = self.a > 0

    def at(self, a=None, b=None, l=None, s=None):
        return tuple(
            own if other is None else other
            for own, other in zip((self.a, self.b, self.l, self.s), (a, b, l, s))
        )

    def other(self, axis, step):
        size, own = {"b": (self.nb, self.b), "l": (self.nl, self.l), "s": (self.ns, self.s)}[axis]
        return lax.rem(own + step, size)

    def to(self, axis, step):
        return self.at(**{axis: self.other(axis, step)})

    def hello(self, device):
        pl.semaphore_signal(
            pltpu.get_barrier_semaphore(), inc=1, device_id=device, device_id_type=MESH
        )

    def greet_neighbours(self, siblings):
        @pl.when(self.is_down)
        def _():
            self.hello(self.at(a=self.a - 1))

        @pl.when(self.is_up)
        def _():
            self.hello(self.at(a=self.a + 1))

        count = 0
        for axis, size in (("b", self.nb), ("l", self.nl), ("s", self.ns if siblings else 1)):
            for step in range(1, size):
                self.hello(self.to(axis, step))
                count += 1
        above = 1 - (self.a + 1) // self.na
        below = (self.a + self.na - 1) // self.na
        pl.semaphore_wait(pltpu.get_barrier_semaphore(), count + above + below)

    def greet_plane(self, siblings):
        count = 0
        for index in self.plane_steps():
            self.hello(self.plane_at(index))
            count += 1
        for step in range(1, self.ns if siblings else 1):
            self.hello(self.to("s", step))
            count += 1
        pl.semaphore_wait(pltpu.get_barrier_semaphore(), count)

    def plane_steps(self):
        return [
            (i, j, k)
            for i in range(self.na)
            for j in range(self.nb)
            for k in range(self.nl)
            if i + j + k
        ]

    def plane_at(self, steps, sign=1):
        return self.at(
            a=lax.rem(self.a + sign * steps[0] + self.na, self.na),
            b=lax.rem(self.b + sign * steps[1] + self.nb, self.nb),
            l=lax.rem(self.l + sign * steps[2] + self.nl, self.nl),
        )


def remote(src, dst, sems, device):
    return pltpu.make_async_remote_copy(
        src_ref=src, dst_ref=dst, send_sem=sems[0], recv_sem=sems[1], device_id=device, device_id_type=MESH
    )


def came(g, sem, dst):
    remote(dst, dst, (sem, sem), g.at()).wait_recv()


def left(g, sem, src):
    remote(src, src, (sem, sem), g.at()).wait_send()


def split_of(wide):
    return (wide * 5 // 7) // 128 * 128


def gather_sems(sizes, siblings):
    na, nb, nl, ns = sizes
    return [
        DMA((2, 2, na)),
        DMA((2, 2, na)),
        DMA((2, nb - 1, na)),
        DMA((2, nl - 1, na)),
        DMA((2, nl - 1, nb - 1, na)),
        DMA((2, nb - 1, nl - 1)),
        DMA((2, ns, na)) if siblings else DMA((2, 1, 1)),
        DMA((1,)),
    ]


def gathering(g, siblings, x_ref, o_ref, sems):
    la_sem, lb_sem, b_sem, l_sem, lb2_sem, bl2_sem, s_sem, own_sem = sems
    na, nb, nl, ns = g.sizes
    wide = x_ref.shape[-1]
    cut = split_of(wide)
    head, tail = pl.ds(0, cut), pl.ds(cut, wide - cut)
    me = g.s if siblings else 0

    def slot(a, b, l):
        return o_ref.at[a, b, l, me]

    def square(a):
        return o_ref.at[a, :, :, me]

    def pair(sem, *index):
        return sem.at[(0, *index)], sem.at[(1, *index)]

    def cols(origin):
        return (slice(None), head)

    def line_head(way, origin, first=False):
        src = x_ref.at[:, head] if first else slot(origin, g.b, g.l).at[:, head]
        return remote(src, slot(origin, g.b, g.l).at[:, head], pair(la_sem, way, origin), g.at(a=g.a + 1 - 2 * way))

    def line_tail(way, origin):
        block = o_ref.at[origin, :, :, me, :, tail]
        return remote(block, block, pair(lb_sem, way, origin), g.at(a=g.a + 1 - 2 * way))

    def spread(origin, first=False):
        for step in range(1, nl):
            if first:
                remote(x_ref, slot(origin, g.b, g.l), pair(l_sem, step - 1, origin), g.to("l", step)).start()
            else:
                part = slot(origin, g.b, g.l).at[:, head]
                remote(part, part, pair(l_sem, step - 1, origin), g.to("l", step)).start()
        for step in range(1, nb):
            if first:
                remote(x_ref, slot(origin, g.b, g.l), pair(b_sem, step - 1, origin), g.to("b", step)).start()
            else:
                part = slot(origin, g.b, g.l).at[:, head]
                remote(part, part, pair(b_sem, step - 1, origin), g.to("b", step)).start()

    def l_came(step, origin, first=False):
        l_from = g.other("l", nl - step)
        ref = slot(origin, g.b, l_from)
        came(g, l_sem.at[1, step - 1, origin], ref if first else ref.at[:, head])
        return l_from

    def b_came(step, origin, first=False):
        b_from = g.other("b", nb - step)
        ref = slot(origin, b_from, g.l)
        came(g, b_sem.at[1, step - 1, origin], ref if first else ref.at[:, head])
        return b_from

    def relay_head(origin, first=False):
        for step in range(1, nl):
            l_from = l_came(step, origin, first)
            part = slot(origin, g.b, l_from).at[:, head]
            for turn in range(1, nb):
                remote(part, part, pair(lb2_sem, step - 1, turn - 1, origin), g.to("b", turn)).start()

    def relay_tail():
        for step in range(1, nb):
            b_from = b_came(step, g.a, True)
            part = slot(g.a, b_from, g.l).at[:, tail]
            for turn in range(1, nl):
                remote(part, part, pair(bl2_sem, step - 1, turn - 1), g.to("l", turn)).start()

    def diagonal_head(origin):
        for step in range(1, nl):
            for turn in range(1, nb):
                ref = slot(origin, g.other("b", nb - turn), g.other("l", nl - step))
                came(g, lb2_sem.at[1, step - 1, turn - 1, origin], ref.at[:, head])

    def diagonal_tail():
        for step in range(1, nb):
            for turn in range(1, nl):
                ref = slot(g.a, g.other("b", nb - step), g.other("l", nl - turn))
                came(g, bl2_sem.at[1, step - 1, turn - 1], ref.at[:, tail])

    def siblings_send(origin):
        if siblings:
            for step in range(1, ns):
                remote(square(origin), square(origin), pair(s_sem, step - 1, origin), g.to("s", step)).start()

    def when_up_origin(k, act):
        @pl.when(g.a - k >= 0)
        def _():
            act(0, g.a - k)

    def when_down_origin(k, act):
        @pl.when(g.a + k < na)
        def _():
            act(1, g.a + k)

    def both(k, act):
        when_up_origin(k, act)
        when_down_origin(k, act)

    def onward(way, copy):
        @pl.when(g.is_up if way == 0 else g.is_down)
        def _():
            copy.start()

    def head_arrives(way, origin):
        came(g, la_sem.at[1, way, origin], slot(origin, g.b, g.l).at[:, head])
        onward(way, line_head(way, origin))
        spread(origin)

    def tail_arrives(way, origin):
        came(g, lb_sem.at[1, way, origin], o_ref.at[origin, :, :, me, :, tail])
        onward(way, line_tail(way, origin))

    own = pltpu.make_async_copy(x_ref, slot(g.a, g.b, g.l), own_sem.at[0])
    own.start()
    onward(0, line_head(0, g.a, True))
    onward(1, line_head(1, g.a, True))
    spread(g.a, True)
    yield
    relay_head(g.a, True)
    relay_tail()
    yield
    both(1, head_arrives)
    diagonal_tail()
    own.wait()
    onward(0, line_tail(0, g.a))
    onward(1, line_tail(1, g.a))
    yield
    for k in range(1, na):
        both(k, lambda way, origin: relay_head(origin))
        if k + 1 < na:
            both(k + 1, head_arrives)
        both(k, tail_arrives)
        if k == 1:
            diagonal_head(g.a)
            siblings_send(g.a)
        yield

    def complete(way, origin):
        for step in range(1, nb):
            b_came(step, origin)
        diagonal_head(origin)
        siblings_send(origin)

    for k in range(1, na):
        both(k, complete)
    yield

    def sent_line(way, origin):
        @pl.when(g.is_up if way == 0 else g.is_down)
        def _():
            line_head(way, origin).wait_send()
            line_tail(way, origin).wait_send()

    when_up_origin(0, sent_line)
    when_down_origin(0, sent_line)
    for k in range(1, na):
        both(k, sent_line)

    def sent(way, origin, first=False):
        whole = slot(origin, g.b, g.l)
        for step in range(1, nl):
            left(g, l_sem.at[0, step - 1, origin], whole if first else whole.at[:, head])
            for turn in range(1, nb):
                left(g, lb2_sem.at[0, step - 1, turn - 1, origin], whole.at[:, head])
        for step in range(1, nb):
            left(g, b_sem.at[0, step - 1, origin], whole if first else whole.at[:, head])
        if siblings:
            for step in range(1, ns):
                left(g, s_sem.at[0, step - 1, origin], square(origin))
                came(g, s_sem.at[1, step - 1, origin], o_ref.at[origin, :, :, g.other("s", ns - step)])

    sent(0, g.a, True)
    for step in range(1, nb):
        for turn in range(1, nl):
            left(g, bl2_sem.at[0, step - 1, turn - 1], slot(g.a, g.b, g.l).at[:, tail])
    for k in range(1, na):
        both(k, sent)


def run_steps(*programs):
    alive = list(programs)
    while alive:
        for program in list(alive):
            try:
                next(program)
            except StopIteration:
                alive.remove(program)


def gather_kernel(sizes, x_ref, o_ref, *sems):
    g = Grid(sizes)
    g.greet_neighbours(False)
    run_steps(gathering(g, False, x_ref, o_ref, sems))


def gather(x, sizes, collective_id):
    na, nb, nl, ns = sizes
    rows, wide = x.shape
    out = pl.pallas_call(
        functools.partial(gather_kernel, sizes),
        out_shape=jax.ShapeDtypeStruct((na, nb, nl, 1, rows, wide), x.dtype),
        in_specs=[ANY],
        out_specs=ANY,
        scratch_shapes=gather_sems(sizes, False),
        compiler_params=pltpu.CompilerParams(collective_id=collective_id, has_side_effects=True),
    )(x)
    return out.reshape(-1, wide)


def expert_steps(g, shards, wholes, shared, columns, down, downs, sems):
    e_sem, es_sem, c_sem, cs_sem, d_sem, own_sem = sems
    na, nb, nl, ns = g.sizes

    def across(i, step):
        l_to = g.other("l", step)
        return remote(shards[i].at[l_to], wholes[i].at[g.l, g.s], (e_sem.at[0, i, step - 1], e_sem.at[1, i, step - 1]), g.at(l=l_to))

    def aside(i, turn, step):
        l_from = g.other("l", nl - turn) if turn else g.l
        src = wholes[i].at[l_from, g.s] if turn else shards[i].at[g.l]
        return remote(src, wholes[i].at[l_from, g.s], (es_sem.at[0, i, turn, step - 1], es_sem.at[1, i, turn, step - 1]), g.to("s", step))

    def aside_came(i, turn, step):
        l_from = g.other("l", nl - turn) if turn else g.l
        came(g, es_sem.at[1, i, turn, step - 1], wholes[i].at[l_from, g.other("s", ns - step)])

    def block(n, steps):
        a, b, l, _ = g.plane_at(steps)
        return remote(shared.at[a, b, l], columns.at[:, g.a, g.b, g.l, g.s], (c_sem.at[0, n], c_sem.at[1, n]), g.plane_at(steps))

    def downward(step):
        return remote(down, downs.at[g.s], (d_sem.at[0, step - 1], d_sem.at[1, step - 1]), g.to("s", step))

    def columns_aside(step):
        part = columns.at[:, :, :, :, g.s]
        return remote(part, part, (cs_sem.at[0, step - 1], cs_sem.at[1, step - 1]), g.to("s", step))

    count = len(shards)
    owns = [pltpu.make_async_copy(shards[i].at[g.l], wholes[i].at[g.l, g.s], own_sem.at[i]) for i in range(count)]
    owns.append(pltpu.make_async_copy(shared.at[g.a, g.b, g.l], columns.at[:, g.a, g.b, g.l, g.s], own_sem.at[count]))
    owns.append(pltpu.make_async_copy(down, downs.at[g.s], own_sem.at[count + 1]))
    steps = g.plane_steps()
    yield
    for step in range(1, nl):
        across(0, step).start()
    for copy in owns:
        copy.start()
    for step in range(1, ns):
        downward(step).start()
        for i in range(count):
            aside(i, 0, step).start()
    for n, at in enumerate(steps):
        block(n, at).start()
    yield
    for i in range(1, count):
        for step in range(1, nl):
            across(i, step).start()
        yield
    for copy in owns:
        copy.wait()
    for n, at in enumerate(steps):
        a, b, l, _ = g.plane_at(at, -1)
        came(g, c_sem.at[1, n], columns.at[:, a, b, l, g.s])
    for step in range(1, ns):
        columns_aside(step).start()
    for i in range(count):
        for turn in range(1, nl):
            came(g, e_sem.at[1, i, turn - 1], wholes[i].at[g.other("l", nl - turn), g.s])
            for step in range(1, ns):
                aside(i, turn, step).start()
    yield
    for n, at in enumerate(steps):
        block(n, at).wait_send()
    for step in range(1, ns):
        downward(step).wait_send()
        came(g, d_sem.at[1, step - 1], downs.at[g.other("s", ns - step)])
        columns_aside(step).wait_send()
        came(g, cs_sem.at[1, step - 1], columns.at[:, :, :, :, g.other("s", ns - step)])
    for i in range(count):
        for step in range(1, nl):
            across(i, step).wait_send()
        for turn in range(nl):
            for step in range(1, ns):
                aside(i, turn, step).wait_send()
                aside_came(i, turn, step)


def inputs_kernel(sizes, dense, wide_dy, gate, up, down, shared, sh_down, dense_o, dy_o, gate_o, up_o, down_o, columns_o, downs_o, *sems):
    g = Grid(sizes)
    g.greet_plane(True)
    run_steps(
        gathering(g, True, dense, dense_o, sems[:8]),
        gathering(g, False, wide_dy, dy_o, sems[8:16]),
        expert_steps(g, (gate, up, down), (gate_o, up_o, down_o), shared, columns_o, sh_down, downs_o, sems[16:]),
    )


def inputs_gather(dense, wide_dy, experts, shared, sh_down, sizes, collective_id):
    na, nb, nl, ns = sizes
    ranks, rows, ffe = experts[0].shape
    two, sh_rows, narrow = shared.shape[3:]
    shape = jax.ShapeDtypeStruct
    places = len(Grid.plane_steps(type("S", (), {"na": na, "nb": nb, "nl": nl})))
    dense_o, dy_o, *wholes, columns, downs = pl.pallas_call(
        functools.partial(inputs_kernel, sizes),
        out_shape=[
            shape((na, nb, nl, ns, *dense.shape), BF16),
            shape((na, nb, nl, 1, *wide_dy.shape), BF16),
            *[shape((ranks, ns, rows, ffe), BF16)] * 3,
            shape((two, na, nb, nl, ns, sh_rows, narrow), BF16),
            shape((ns, *sh_down.shape), BF16),
        ],
        in_specs=[ANY] * 7,
        out_specs=[ANY] * 7,
        scratch_shapes=gather_sems(sizes, True)
        + gather_sems(sizes, False)
        + [
            DMA((2, 3, nl - 1)),
            DMA((2, 3, nl, ns - 1)),
            DMA((2, places)),
            DMA((2, ns - 1)),
            DMA((2, ns - 1)),
            DMA((5,)),
        ],
        compiler_params=pltpu.CompilerParams(collective_id=collective_id, has_side_effects=True),
    )(dense, wide_dy, *experts, shared, sh_down)
    return (
        dense_o.reshape(-1, dense.shape[1]),
        dy_o.reshape(-1, wide_dy.shape[1]),
        [whole.reshape(-1, ffe) for whole in wholes],
        columns.reshape(two, -1, narrow),
        downs,
    )


def order(a, k):
    high, odd = a // 2, lax.rem(a, 2)
    return (3 * (1 - high), 2 + high - 2 * odd, 1 + odd, a)[k]


def add_rows(out, *terms):
    rows = out.shape[0]
    step = min(rows, 32)

    @pl.loop(0, rows, step=step)
    def _(r):
        at = pl.ds(pl.multiple_of(r, step), step)
        total = terms[0][at, :].astype(F32)
        for term in terms[1:]:
            total = total + term[at, :].astype(F32)
        out[at, :] = total.astype(out.dtype)


def scatter_scratch(sizes, siblings, rows, wide):
    na, nb, nl, ns = sizes
    head = split_of(wide)
    tail = wide - head
    shapes = [
        (nb - 1, na, nl, rows, head),
        (nl - 1, na, rows, head),
        (na, rows, head),
        (na + 1, rows, head),
        (na + 1, nb, nl, rows, tail),
        (nb, nl, rows, tail),
        (nl - 1, nb, rows, tail),
        (nb - 1, rows, tail),
        (ns - 1, na, nb, nl, rows, wide) if siblings else (16, 128),
    ]
    sems = [(2, nb - 1, na), (2, nl - 1, na), (2, 2, na), (2, 2, na), (2, nl - 1), (2, nb - 1), (2, ns - 1, na)]
    return [pltpu.VMEM(s, BF16) for s in shapes] + [DMA(s) for s in sems]


def scattering(g, siblings, p_ref, o_ref, scratch):
    one, two, total, line_a, line_b, tail_sum, tail_two, tail_three, s_buf = scratch[:9]
    b_sem, l_sem, la_sem, lb_sem, l2_sem, b2_sem, s_sem = scratch[9:]
    na, nb, nl, ns = g.sizes
    wide = o_ref.shape[-1]
    cut = split_of(wide)
    head, tail = pl.ds(0, cut), pl.ds(cut, wide - cut)

    def pair(sem, *index):
        return sem.at[(0, *index)], sem.at[(1, *index)]

    def block(k):
        return s_buf.at[0, k] if siblings else p_ref.at[order(g.a, k), :, :, 0]

    def sibling_copy(k, step):
        to = g.other("s", step)
        return remote(p_ref.at[order(g.a, k), :, :, to], s_buf.at[step - 1, k], pair(s_sem, step - 1, k), g.at(s=to))

    def b_copy(k, step):
        to = g.other("b", step)
        return remote(block(k).at[to, :, :, head], one.at[step - 1, k], pair(b_sem, step - 1, k), g.at(b=to))

    def l_copy(k, step):
        to = g.other("l", step)
        return remote(one.at[0, k, to], two.at[step - 1, k], pair(l_sem, step - 1, k), g.at(l=to))

    def place(way, dest, at):
        if way == 0:
            return dest
        far = (at - dest + na - 1) // na
        return dest * far + na * (1 - far)

    def head_copy(way, k):
        dest, to = order(g.a, k), g.a + 1 - 2 * way
        return remote(total.at[k], line_a.at[place(way, dest, to)], pair(la_sem, way, dest), g.at(a=to))

    def tail_copy(way, k, first):
        dest, to = order(g.a, k), g.a + 1 - 2 * way
        src = block(k).at[:, :, :, tail] if first else line_b.at[dest]
        return remote(src, line_b.at[place(way, dest, to)], pair(lb_sem, way, dest), g.at(a=to))

    def starts(k, act):
        if k == na - 1:
            return
        dest = order(g.a, k)

        @pl.when((g.a == 0) & (dest > g.a))
        def _():
            act(0)

        @pl.when((g.a == na - 1) & (dest < g.a))
        def _():
            act(1)

    def passes(k, act):
        if k == na - 1:
            return
        dest = order(g.a, k)

        @pl.when((g.a > 0) & (dest > g.a))
        def _():
            act(0)

        @pl.when((g.a < na - 1) & (dest < g.a))
        def _():
            act(1)

    def arrivals(act):
        mine = place(0, g.a, g.a)

        @pl.when(g.a == 0)
        def _():
            act((1,), (na,))

        @pl.when(g.a == na - 1)
        def _():
            act((0,), (mine,))

        @pl.when((g.a > 0) & (g.a < na - 1))
        def _():
            act((0, 1), (mine, na))

    def begin(k):
        if k >= na:
            return
        if siblings:
            for step in range(1, ns):
                came(g, s_sem.at[1, step - 1, k], s_buf.at[step - 1, k])
            for b in range(nb):
                for l in range(nl):
                    add_rows(s_buf.at[0, k, b, l], p_ref.at[order(g.a, k), b, l, g.s], *[s_buf.at[step, k, b, l] for step in range(ns - 1)])
        for step in range(1, nb):
            b_copy(k, step).start()
        starts(k, lambda way: tail_copy(way, k, True).start())

    def second(k):
        for step in range(1, nb):
            came(g, b_sem.at[1, step - 1, k], one.at[step - 1, k])
        for turn in range(nl):
            l = g.other("l", turn)
            add_rows(one.at[0, k, l], block(k).at[g.b, l, :, head], *[one.at[step, k, l] for step in range(nb - 1)])
            if turn:
                l_copy(k, turn).start()

    def third(k):
        for step in range(1, nl):
            came(g, l_sem.at[1, step - 1, k], two.at[step - 1, k])
        add_rows(total.at[k], one.at[0, k, g.l], *[two.at[step, k] for step in range(nl - 1)])
        starts(k, lambda way: head_copy(way, k).start())

    def pass_head(k):
        def act(way):
            dest = order(g.a, k)
            came(g, la_sem.at[1, way, dest], line_a.at[dest])
            add_rows(total.at[k], total.at[k], line_a.at[dest])
            head_copy(way, k).start()

        passes(k, act)

    def pass_tail(k):
        def act(way):
            dest = order(g.a, k)
            came(g, lb_sem.at[1, way, dest], line_b.at[dest])
            for b in range(nb):
                for l in range(nl):
                    add_rows(line_b.at[dest, b, l], line_b.at[dest, b, l], block(k).at[b, l, :, tail])
            tail_copy(way, k, False).start()

        passes(k, act)

    def tail_here():
        def act(ways, slots):
            for way, slot in zip(ways, slots):
                came(g, lb_sem.at[1, way, g.a], line_b.at[slot])
            for b in range(nb):
                for l in range(nl):
                    add_rows(tail_sum.at[b, l], block(na - 1).at[b, l, :, tail], *[line_b.at[slot, b, l] for slot in slots])

        arrivals(act)
        for step in range(1, nl):
            tail_l(step).start()

    def tail_l(step):
        to = g.other("l", step)
        return remote(tail_sum.at[:, to], tail_two.at[step - 1], pair(l2_sem, step - 1), g.at(l=to))

    def tail_b(step):
        to = g.other("b", step)
        return remote(tail_two.at[0, to], tail_three.at[step - 1], pair(b2_sem, step - 1), g.at(b=to))

    if siblings:
        for k in range(na):
            for step in range(1, ns):
                sibling_copy(k, step).start()
    begin(0)
    begin(1)
    yield
    for k in range(na):
        second(k)
        begin(k + 2)
        if k >= 1:
            third(k - 1)
            pass_tail(k - 1)
        if k >= 2:
            pass_head(k - 2)
        yield
    third(na - 1)
    pass_head(na - 2)
    tail_here()
    yield

    def head_here(ways, slots):
        for way, slot in zip(ways, slots):
            came(g, la_sem.at[1, way, g.a], line_a.at[slot])
        add_rows(o_ref.at[:, head], total.at[na - 1], *[line_a.at[slot] for slot in slots])

    for step in range(1, nl):
        came(g, l2_sem.at[1, step - 1], tail_two.at[step - 1])
    for b in range(nb):
        add_rows(tail_two.at[0, b], tail_sum.at[b, g.l], *[tail_two.at[step, b] for step in range(nl - 1)])
    for step in range(1, nb):
        tail_b(step).start()
    arrivals(head_here)
    yield
    for step in range(1, nb):
        came(g, b2_sem.at[1, step - 1], tail_three.at[step - 1])
    add_rows(o_ref.at[:, tail], tail_two.at[0, g.b], *[tail_three.at[step] for step in range(nb - 1)])

    for k in range(na):
        if siblings:
            for step in range(1, ns):
                sibling_copy(k, step).wait_send()
        for step in range(1, nb):
            b_copy(k, step).wait_send()
        for step in range(1, nl):
            l_copy(k, step).wait_send()

        def sent(way, first):
            tail_copy(way, k, first).wait_send()
            head_copy(way, k).wait_send()

        starts(k, lambda way: sent(way, True))
        passes(k, lambda way: sent(way, False))
    for step in range(1, nl):
        tail_l(step).wait_send()
    for step in range(1, nb):
        tail_b(step).wait_send()


def scatters_kernel(sizes, count, *refs):
    g = Grid(sizes)
    g.greet_neighbours(False)
    ins, outs, scratch = refs[:count], refs[count : 2 * count], refs[2 * count :]
    each = len(scratch) // count
    run_steps(
        *[
            scattering(g, False, ins[i], outs[i], scratch[i * each : (i + 1) * each])
            for i in range(count)
        ]
    )


def scatter(partials, sizes, collective_id):
    na, nb, nl, ns = sizes
    count = len(partials)
    rows, wide = partials[0].shape[0] // (na * nb * nl), partials[0].shape[1]
    return pl.pallas_call(
        functools.partial(scatters_kernel, sizes, count),
        out_shape=[jax.ShapeDtypeStruct((rows, wide), F32)] * count,
        in_specs=[VMEM] * count,
        out_specs=[VMEM] * count,
        scratch_shapes=scatter_scratch(sizes, False, rows, wide) * count,
        compiler_params=pltpu.CompilerParams(collective_id=collective_id, has_side_effects=True, vmem_limit_bytes=VMEM_LIMIT),
    )(*[partial.reshape(na, nb, nl, 1, rows, wide) for partial in partials])


def scatter_pair(p, q, sizes, first_id, second_id):
    if p.size <= 2048 * 2048:
        return scatter([p, q], sizes, first_id)
    return scatter([p], sizes, first_id) + scatter([q], sizes, second_id)


def shared_steps(g, part, blocks, own, other, sems):
    s_sem, c_sem, own_sem = sems
    na, nb, nl, ns = g.sizes
    steps = g.plane_steps()

    def aside(step):
        to = g.other("s", step)
        return remote(part.at[:, :, :, to], other.at[step - 1], (s_sem.at[0, step - 1], s_sem.at[1, step - 1]), g.at(s=to))

    def send(n, at):
        a, b, l, _ = g.plane_at(at)
        return remote(other.at[0, a, b, l], blocks.at[g.a, g.b, g.l], (c_sem.at[0, n], c_sem.at[1, n]), g.plane_at(at))

    mine = pltpu.make_async_copy(part.at[:, :, :, g.s], own, own_sem.at[0])
    mine.start()
    for step in range(1, ns):
        aside(step).start()
    yield
    mine.wait()
    for step in range(1, ns):
        came(g, s_sem.at[1, step - 1], other.at[step - 1])
    for a in range(na):
        for b in range(nb):
            for l in range(nl):
                add_rows(other.at[0, a, b, l], own.at[a, b, l], *[other.at[step, a, b, l] for step in range(ns - 1)])
    for n, at in enumerate(steps):
        send(n, at).start()
    here = pltpu.make_async_copy(other.at[0, g.a, g.b, g.l], blocks.at[g.a, g.b, g.l], own_sem.at[1])
    here.start()
    yield
    yield
    yield
    yield
    here.wait()
    for n, at in enumerate(steps):
        a, b, l, _ = g.plane_at(at, -1)
        came(g, c_sem.at[1, n], blocks.at[a, b, l])
        send(n, at).wait_send()
    for step in range(1, ns):
        aside(step).wait_send()


def across_steps(g, blocks, outs, sem):
    def send(i, step):
        return remote(blocks.at[i, step - 1], outs.at[i, step - 1], (sem.at[0, i, step - 1], sem.at[1, i, step - 1]), g.to("l", step))

    count = blocks.shape[0]
    for i in range(count):
        for step in range(1, g.nl):
            send(i, step).start()
        yield
        yield
    for i in range(count):
        for step in range(1, g.nl):
            send(i, step).wait()


def outputs_kernel(sizes, p_ref, shared_ref, cross_ref, o_ref, blocks_ref, cross_o, own, other, *scratch):
    g = Grid(sizes)
    g.greet_plane(True)
    run_steps(
        scattering(g, True, p_ref, o_ref, scratch[4:]),
        shared_steps(g, shared_ref, blocks_ref, own, other, scratch[:3]),
        across_steps(g, cross_ref, cross_o, scratch[3]),
    )


def outputs_scatter(partial, shared, cross, sizes, collective_id):
    na, nb, nl, ns = sizes
    rows, wide = partial.shape[0] // (na * nb * nl * ns), partial.shape[1]
    shared = shared.reshape(na, nb, nl, ns, -1, shared.shape[1])
    shape = jax.ShapeDtypeStruct
    return pl.pallas_call(
        functools.partial(outputs_kernel, sizes),
        out_shape=[
            shape((rows, wide), F32),
            shape((na, nb, nl, *shared.shape[4:]), BF16),
            shape(cross.shape, BF16),
        ],
        in_specs=[VMEM] + [ANY] * 2,
        out_specs=[VMEM] + [ANY] * 2,
        scratch_shapes=[
            pltpu.VMEM((na, nb, nl, *shared.shape[4:]), BF16),
            pltpu.VMEM((ns - 1, na, nb, nl, *shared.shape[4:]), BF16),
            DMA((2, ns - 1)),
            DMA((2, na * nb * nl - 1)),
            DMA((2,)),
            DMA((2, 3, nl - 1)),
        ]
        + scatter_scratch(sizes, True, rows, wide),
        compiler_params=pltpu.CompilerParams(collective_id=collective_id, has_side_effects=True, vmem_limit_bytes=VMEM_LIMIT),
    )(partial.reshape(na, nb, nl, ns, rows, wide), shared, cross)


def weights_kernel(sizes, gp, inner, xr, dg, du, own_o, cross_o, send, recv, own_buf, cross_buf, s_sem, c_sem):
    g = Grid(sizes)
    na, nb, nl, ns = sizes
    for step in range(1, ns):
        g.hello(g.to("s", step))
    pl.semaphore_wait(pltpu.get_barrier_semaphore(), ns - 1)
    rows, ffe = own_buf.shape[1:]
    jobs = ((xr, dg), (xr, du), (gp, inner))

    def product(i, l, s, out):
        left, right = jobs[i]
        at = (l * ns + s) * rows
        step = 256 if rows % 256 == 0 else rows

        @pl.loop(0, rows, step=step)
        def _(r):
            cols = pl.ds(pl.multiple_of(at + r, step), step)
            for to, tile in column_tiles(ffe, 256):
                value = dot_tn(left[:, cols], right[:, pl.ds(to, tile)])
                out[pl.ds(pl.multiple_of(r, step), step), pl.ds(to, tile)] = value.astype(out.dtype)

    def aside(i, turn, step):
        return remote(send.at[i % 2, turn, step - 1], recv.at[i, turn, step - 1], (s_sem.at[0, i, turn, step - 1], s_sem.at[1, i, turn, step - 1]), g.to("s", step))

    def keep(i):
        return [pltpu.make_async_copy(own_buf.at[i % 2], own_o.at[i], c_sem.at[i, 0])] + [
            pltpu.make_async_copy(cross_buf.at[i % 2, turn - 1], cross_o.at[i, turn - 1], c_sem.at[i, turn])
            for turn in range(1, nl)
        ]

    def sums(i):
        for turn in range(nl):
            out = cross_buf.at[i % 2, turn - 1] if turn else own_buf.at[i % 2]
            for step in range(1, ns):
                came(g, s_sem.at[1, i, turn, step - 1], recv.at[i, turn, step - 1])
            add_rows(out, out, *[recv.at[i, turn, step] for step in range(ns - 1)])
        for copy in keep(i):
            copy.start()

    for i in range(3):
        for turn in range(nl):
            for step in range(1, ns):
                if i >= 2:
                    aside(i - 2, turn, step).wait_send()
                product(i, g.other("l", turn), g.other("s", step), send.at[i % 2, turn, step - 1])
                aside(i, turn, step).start()
        if i >= 1:
            sums(i - 1)
        if i >= 2:
            for copy in keep(i - 2):
                copy.wait()
        for turn in range(nl):
            product(i, g.other("l", turn), g.s, cross_buf.at[i % 2, turn - 1] if turn else own_buf.at[i % 2])
    sums(2)
    for i in range(1, 3):
        for copy in keep(i):
            copy.wait()
        for turn in range(nl):
            for step in range(1, ns):
                aside(i, turn, step).wait_send()


def expert_weights(gp, inner, xr, dg, du, sizes, collective_id):
    na, nb, nl, ns = sizes
    rows, ffe = gp.shape[1] // (nl * ns), inner.shape[1]
    return pl.pallas_call(
        functools.partial(weights_kernel, sizes),
        out_shape=[
            jax.ShapeDtypeStruct((3, rows, ffe), F32),
            jax.ShapeDtypeStruct((3, nl - 1, rows, ffe), BF16),
        ],
        in_specs=[VMEM] * 5,
        out_specs=[ANY] * 2,
        scratch_shapes=[
            pltpu.VMEM((2, nl, ns - 1, rows, ffe), BF16),
            pltpu.VMEM((3, nl, ns - 1, rows, ffe), BF16),
            pltpu.VMEM((2, rows, ffe), F32),
            pltpu.VMEM((2, nl - 1, rows, ffe), BF16),
            DMA((2, 3, nl, ns - 1)),
            DMA((3, nl)),
        ],
        compiler_params=pltpu.CompilerParams(collective_id=collective_id, has_side_effects=True, vmem_limit_bytes=VMEM_LIMIT),
    )(gp, inner, xr, dg, du)


def rms_norm(values, gain_row):
    factor = lax.rsqrt(jnp.mean(values * values, axis=-1, keepdims=True) + EPS)
    return values * factor * gain_row


def rotate(values):
    length = values.shape[0]
    half_dim = values.shape[-1] // 2
    position = jnp.arange(length).astype(F32)
    inverse = ROPE_BASE ** (-jnp.arange(half_dim).astype(F32) * 2.0 / values.shape[-1])
    angle_table = position[:, None] * inverse[None, :]
    cosine = jnp.cos(angle_table)[:, None, :]
    sine = jnp.sin(angle_table)[:, None, :]
    lower = values[..., :half_dim]
    upper = values[..., half_dim:]
    return jnp.concatenate(
        [lower * cosine - upper * sine, upper * cosine + lower * sine], axis=-1
    )


def lane_pad(block):
    return jnp.pad(block, ((0, 0), (0, -block.shape[1] % 128)))


def silu_pair(gate_part, up_part):
    return jax.nn.silu(gate_part) * up_part


def silu_parts(v):
    sig = 1.0 / (1.0 + jnp.exp(-v))
    return sig, v * sig


def exact(left, right, dims):
    return lax.dot_general(
        left, right, (dims, ((), ())), preferred_element_type=F32, precision=lax.Precision.HIGHEST
    )


def column_tiles(wide, tile):
    return [(at, min(tile, wide - at)) for at in range(0, wide, tile)]


def moe_kernel(seqs, experts, x_ref, dy_ref, pick_ref, back_ref, router_ref, wg_ref, wu_ref, wd_ref, sgu_ref, sd_ref,
               xr_ref, gp_ref, inner_ref, dg_ref, du_ref, share_ref, dsgu_ref, out_ref, dx_ref, gg_ref,
               g_buf, u_buf, dyr_buf, gate_buf, sum_buf, mm_buf):
    length = x_ref.shape[0] // seqs
    cap = xr_ref.shape[0] // seqs
    width = x_ref.shape[1]
    ffe = wg_ref.shape[1]
    narrow = sd_ref.shape[0]
    lane = lax.broadcasted_iota(jnp.int32, (length, 128), 1)
    mine = (lax.axis_index(PLANE) == lane).astype(F32)

    for n in range(seqs):
        toks, slots = pl.ds(n * length, length), pl.ds(n * cap, cap)
        x = x_ref[toks, :]
        dy = dy_ref[toks, pl.ds(0, width)]
        xr_ref[slots, :] = dot(pick_ref[n], x).astype(BF16)
        dyr_buf[slots, :] = dot(pick_ref[n], dy).astype(BF16)
        hot = dy_ref[toks, pl.ds(width, 128)].astype(F32)
        logits = jnp.where(hot > 0, dot(x, router_ref[...]), -1e30)
        top = jnp.max(logits, axis=1, keepdims=True)
        raised = jnp.exp(logits - top)
        gate = jnp.sum(raised * mine, axis=1, keepdims=True) / jnp.sum(raised, axis=1, keepdims=True)
        gate = jnp.broadcast_to(gate, (length, 128))
        gate_buf[slots, :] = exact(pick_ref[n].astype(F32), gate, ((1,), (0,)))

    for at, tile in column_tiles(ffe, 256):
        cols = pl.ds(at, tile)
        g = dot(xr_ref[...], wg_ref[:, cols])
        u = dot(xr_ref[...], wu_ref[:, cols])
        g_buf[:, cols] = g
        u_buf[:, cols] = u
        inner_ref[:, cols] = (silu_parts(g)[1] * u).astype(BF16)
    share_gu = dot(x_ref[...], sgu_ref[...])
    d_share = dot_nt(dy_ref[:, pl.ds(0, width)], sd_ref[...])
    sg, su = share_gu[:, :narrow], share_gu[:, narrow:]
    sig, act = silu_parts(sg)
    share_ref[...] = (act * su).astype(BF16)
    dsgu_ref[:, :narrow] = (d_share * su * sig * (1.0 + sg * (1.0 - sig))).astype(BF16)
    dsgu_ref[:, narrow:] = (d_share * act).astype(BF16)
    sum_buf[...] = jnp.zeros_like(sum_buf)
    for at, tile in column_tiles(width, 256):
        cols = pl.ds(at, tile)
        produced = dot_nt(inner_ref[...], wd_ref[cols, :])
        dyr = dyr_buf[:, cols].astype(F32)
        gate = gate_buf[:, pl.ds(0, 1)]
        sum_buf[...] += jnp.broadcast_to(jnp.sum(produced * dyr, axis=1, keepdims=True), sum_buf.shape)
        gp_ref[:, cols] = (gate * dyr).astype(BF16)
        mm_buf[...] = (gate * produced).astype(BF16)
        for n in range(seqs):
            toks, slots = pl.ds(n * length, length), pl.ds(n * cap, cap)
            out_ref[toks, cols] = (dot(back_ref[n], mm_buf[slots, :]) + dot(share_ref[toks, :], sd_ref[:, cols])).astype(BF16)
    for n in range(seqs):
        slots = pl.ds(n * cap, cap)
        gg_ref[n] = exact(sum_buf[slots, :], pick_ref[n].astype(F32), ((0,), (0,)))[:8]

    for at, tile in column_tiles(ffe, 256):
        cols = pl.ds(at, tile)
        d_inner = dot(gp_ref[...], wd_ref[:, cols])
        g, u = g_buf[:, cols], u_buf[:, cols]
        sig, act = silu_parts(g)
        dg_ref[:, cols] = (d_inner * u * sig * (1.0 + g * (1.0 - sig))).astype(BF16)
        du_ref[:, cols] = (d_inner * act).astype(BF16)
    for at, tile in column_tiles(width, 256):
        cols = pl.ds(at, tile)
        rows = dot_nt(dg_ref[...], wg_ref[cols, :]) + dot_nt(du_ref[...], wu_ref[cols, :])
        mm_buf[...] = rows.astype(BF16)
        for n in range(seqs):
            toks, slots = pl.ds(n * length, length), pl.ds(n * cap, cap)
            dx_ref[toks, cols] = (dot(back_ref[n], mm_buf[slots, :]) + dot_nt(dsgu_ref[toks, :], sgu_ref[cols, :])).astype(BF16)


def moe(x_all, wide_dy, pick, router, wg, wu, wd, sgu, sd, experts, length, cap, steps):
    total = x_all.shape[0] // length
    seqs = total // steps
    width, ffe, narrow = x_all.shape[1], wg.shape[1], sd.shape[0]
    toks, slots = seqs * length, seqs * cap
    shape = jax.ShapeDtypeStruct

    def rows(count, wide):
        return pl.BlockSpec((count, wide), lambda i: (i, 0))

    def whole(array):
        return pl.BlockSpec(array.shape, lambda i: (0, 0), pipeline_mode=pl.Buffered(1))

    def out(count, wide):
        return shape((steps * count, wide), BF16)

    return pl.pallas_call(
        functools.partial(moe_kernel, seqs, experts),
        grid=(steps,),
        in_specs=[
            rows(toks, width),
            rows(toks, wide_dy.shape[1]),
            pl.BlockSpec((seqs, cap, length), lambda i: (i, 0, 0)),
            pl.BlockSpec((seqs, length, cap), lambda i: (i, 0, 0)),
            *[whole(w) for w in (router, wg, wu, wd, sgu, sd)],
        ],
        out_specs=[
            rows(slots, width),
            rows(slots, width),
            rows(slots, ffe),
            rows(slots, ffe),
            rows(slots, ffe),
            rows(toks, narrow),
            rows(toks, 2 * narrow),
            rows(toks, width),
            rows(toks, width),
            pl.BlockSpec((seqs, 8, length), lambda i: (i, 0, 0)),
        ],
        out_shape=[
            out(slots, width),
            out(slots, width),
            out(slots, ffe),
            out(slots, ffe),
            out(slots, ffe),
            out(toks, narrow),
            out(toks, 2 * narrow),
            out(toks, width),
            out(toks, width),
            shape((total, 8, length), F32),
        ],
        scratch_shapes=[
            pltpu.VMEM((slots, ffe), F32),
            pltpu.VMEM((slots, ffe), F32),
            pltpu.VMEM((slots, width), BF16),
            pltpu.VMEM((slots, 128), F32),
            pltpu.VMEM((slots, 128), F32),
            pltpu.VMEM((slots, 256), BF16),
        ],
        compiler_params=pltpu.CompilerParams(vmem_limit_bytes=VMEM_LIMIT),
        cost_estimate=pl.CostEstimate(flops=6 * 10**10, bytes_accessed=10**8, transcendentals=0),
    )(x_all, wide_dy, pick, pick.transpose(0, 2, 1), router, wg, wu, wd, sgu, sd)


def shards(
    tokens,
    doc_ids,
    routes,
    gain_attn,
    w_query,
    w_key,
    w_value,
    w_out,
    gain_moe,
    w_router,
    shared_gate,
    shared_up,
    shared_down,
    expert_gate,
    expert_up,
    expert_down,
    cotangent,
):
    length, width = tokens.shape
    group_size = HEADS // KV_HEADS
    score_scale = HEAD_DIM ** (-0.5)
    local_experts = expert_gate.shape[0]
    sub = lax.axis_size("s")
    groups = lax.axis_size("a") * lax.axis_size("b") * lax.axis_size("l")
    experts_total = groups
    capacity = length * TOP * 4 // (3 * experts_total)
    sizes = tuple(lax.axis_size(axis) for axis in ALL)
    my_expert = lax.axis_index(PLANE)
    kvw = w_key.shape[1]
    qw = w_query.shape[1]

    small = jnp.concatenate(
        [w_router, gain_attn[:, None], gain_moe[:, None]], axis=1
    )
    small = lane_pad(small)
    hot = jnp.any(routes[:, :, None] == jnp.arange(experts_total)[None, None, :], axis=1)
    wide_dy = jnp.concatenate([cotangent, lane_pad(hot.astype(BF16))], axis=1)
    shared = jnp.stack([shared_gate, shared_up]).reshape(2, shared_gate.shape[0], *sizes[:3], -1)
    sh_rows = shared_down.shape[0]
    sh_pad = -sh_rows % 16
    dense, dy_all, (wg, wu, wd), columns, downs = inputs_gather(
        jnp.concatenate([w_query, w_key, w_value, w_out, small], axis=1),
        wide_dy,
        (expert_gate, expert_up, expert_down),
        shared.transpose(2, 3, 4, 0, 1, 5),
        jnp.pad(shared_down, ((0, sh_pad), (0, 0))),
        sizes,
        1,
    )
    sgu = jnp.concatenate([lane_pad(columns[0]), lane_pad(columns[1])], axis=1)
    narrow = columns.shape[2]
    sd_w = downs[:, :sh_rows].reshape(-1, width)
    sd_w = jnp.pad(sd_w, ((0, -narrow % 128), (0, 0)))
    hot_all = dy_all[:, width : width + experts_total] > 0
    query_full = dense[:, :qw]
    key_full = dense[:, qw : qw + kvw]
    value_full = dense[:, qw + kvw : qw + 2 * kvw]
    out_full = dense[:, qw + 2 * kvw : qw + 2 * kvw + width]
    rest = dense[:, qw + 2 * kvw + width :]
    router_full = rest[:, :experts_total]
    attn_gain = rest[:, experts_total].astype(F32)
    moe_gain = rest[:, experts_total + 1].astype(F32)

    inputs = tokens.astype(F32)
    normed, attn_norm_pull = jax.vjp(rms_norm, inputs, attn_gain)
    normed_low = normed.astype(BF16)
    query_pre = dot(normed_low, query_full).reshape(length, HEADS, HEAD_DIM)
    key_pre = dot(normed_low, key_full).reshape(length, KV_HEADS, HEAD_DIM)
    value_low = dot(normed_low, value_full).astype(BF16).reshape(length, KV_HEADS, HEAD_DIM)
    query_rot, query_pull = jax.vjp(rotate, query_pre)
    key_rot, key_pull = jax.vjp(rotate, key_pre)
    query_low = query_rot.astype(BF16).reshape(length, KV_HEADS, group_size, HEAD_DIM)
    key_low = key_rot.astype(BF16)
    position = jnp.arange(length)
    doc_row = doc_ids[0]
    allowed = (position[None, :] <= position[:, None]) & (doc_row[None, :] == doc_row[:, None])
    scores = (
        jnp.einsum("tkgd,skd->kgts", query_low, key_low, preferred_element_type=F32) * score_scale
    )
    scores = jnp.where(allowed, scores, -1e30)
    exp_scores = jnp.exp(scores - jnp.max(scores, axis=-1, keepdims=True))
    attend = exp_scores / jnp.sum(exp_scores, axis=-1, keepdims=True)
    attend_low = attend.astype(BF16)
    mixed_low = (
        jnp.einsum("kgts,skd->tkgd", attend_low, value_low, preferred_element_type=F32)
        .reshape(length, HEADS * HEAD_DIM)
        .astype(BF16)
    )
    hidden = inputs + dot(mixed_low, out_full)
    normed_moe, moe_norm_pull = jax.vjp(rms_norm, hidden, moe_gain)
    moe_low = normed_moe.astype(BF16)

    x_all = gather(moe_low, sizes, 2)
    seqs = groups
    mine = jnp.any(hot_all & (jnp.arange(experts_total)[None, :] == my_expert), axis=1)
    mine = mine.reshape(seqs, length)
    hits = mine.astype(jnp.int32)
    before = jnp.cumsum(hits, axis=1) - hits
    slot_hot = (jnp.arange(capacity)[None, :, None] == before[:, None, :]) & mine[:, None, :]
    x_rows, gp, inner_low, dg, du, share_low, dsgu, part, dx_part, gate_grad = moe(
        x_all, dy_all, slot_hot.astype(BF16), lane_pad(router_full), wg, wu, wd, sgu, sd_w,
        experts_total, length, capacity, max(seqs // 4, 1),
    )
    gate_grad = lax.all_to_all(gate_grad[:, 0], PLANE, split_axis=0, concat_axis=0, tiled=True)
    dy_all = dy_all[:, :width]
    moe_out, dx = scatter_pair(part, dx_part, sizes, 3, 6)
    output = (hidden + moe_out).astype(BF16)
    own_experts, cross_experts = expert_weights(gp, inner_low, x_rows, dg, du, sizes, 4)
    shared_grads = dot_tn(x_all, dsgu).astype(BF16)
    grad_shared_down = lax.psum_scatter(
        dot_tn(share_low[:, :narrow], dy_all), "s", scatter_dimension=0, tiled=True
    )

    own_logits = jnp.where(hot, dot(moe_low, router_full), -1e30)
    own_gates = jax.nn.softmax(own_logits, axis=-1)
    grad_gate = gate_grad.reshape(experts_total, length).T
    grad_logits = own_gates * (
        grad_gate - jnp.sum(own_gates * grad_gate, axis=-1, keepdims=True)
    )
    grad_logits = grad_logits.astype(BF16)
    grad_router = dot_tn(moe_low, grad_logits)
    dx = dx + dot_nt(grad_logits, router_full)
    grad_hidden_norm, grad_gain_moe = moe_norm_pull(dx)
    grad_hidden = cotangent.astype(F32) + grad_hidden_norm

    grad_hidden_low = grad_hidden.astype(BF16)
    grad_out_proj = dot_tn(mixed_low, grad_hidden_low)
    grad_mixed = (
        dot_nt(grad_hidden_low, out_full)
        .astype(BF16)
        .reshape(length, KV_HEADS, group_size, HEAD_DIM)
    )
    grad_value = jnp.einsum("kgts,tkgd->skd", attend_low, grad_mixed, preferred_element_type=F32)
    grad_attend = jnp.einsum("tkgd,skd->kgts", grad_mixed, value_low, preferred_element_type=F32)
    grad_scores = (
        attend * (grad_attend - jnp.sum(grad_attend * attend, axis=-1, keepdims=True))
    ).astype(BF16)
    grad_query = (
        jnp.einsum("kgts,skd->tkgd", grad_scores, key_low, preferred_element_type=F32) * score_scale
    )
    grad_key = (
        jnp.einsum("kgts,tkgd->skd", grad_scores, query_low, preferred_element_type=F32)
        * score_scale
    )
    grad_query_low = (
        query_pull(grad_query.reshape(length, HEADS, HEAD_DIM))[0].reshape(length, -1).astype(BF16)
    )
    grad_key_low = key_pull(grad_key)[0].reshape(length, -1).astype(BF16)
    grad_value_low = grad_value.reshape(length, -1).astype(BF16)
    grad_normed = (
        dot_nt(grad_query_low, query_full)
        + dot_nt(grad_key_low, key_full)
        + dot_nt(grad_value_low, value_full)
    )
    grad_inputs_norm, grad_gain_attn = attn_norm_pull(grad_normed)
    grad_tokens = grad_hidden + grad_inputs_norm
    grad_small = jnp.concatenate(
        [grad_router, grad_gain_attn[:, None], grad_gain_moe[:, None]], axis=1
    )
    grad_small = lane_pad(grad_small)
    dense_grads = jnp.concatenate(
        [
            dot_tn(normed_low, grad_query_low).astype(BF16),
            dot_tn(normed_low, grad_key_low).astype(BF16),
            dot_tn(normed_low, grad_value_low).astype(BF16),
            grad_out_proj.astype(BF16),
            grad_small.astype(BF16),
        ],
        axis=1,
    )
    total, blocks, cross = outputs_scatter(dense_grads, shared_grads, cross_experts, sizes, 5)
    dense_sum, small_sum = total[:, :-128], total[:, -128:]
    blocks = blocks.reshape(groups, *blocks.shape[3:]).transpose(1, 0, 2).astype(F32)
    half = blocks.shape[2] // 2
    grad_shared_gate = blocks[:, :, :narrow].reshape(blocks.shape[0], -1)
    grad_shared_up = blocks[:, :, half : half + narrow].reshape(blocks.shape[0], -1)
    my_l = lax.axis_index("l")
    expert_grads = []
    for i in range(3):
        here = jnp.arange(local_experts)[:, None, None]
        grad = own_experts[i][None]
        for step in range(1, local_experts):
            from_l = (my_l - step) % local_experts
            grad = jnp.where(here == from_l, cross[i, step - 1].astype(F32)[None], grad)
        expert_grads.append(grad)
    return (
        output,
        grad_tokens,
        small_sum[:, experts_total],
        dense_sum[:, :qw],
        dense_sum[:, qw : qw + kvw],
        dense_sum[:, qw + kvw : qw + 2 * kvw],
        dense_sum[:, qw + 2 * kvw :],
        small_sum[:, experts_total + 1],
        small_sum[:, :experts_total],
        grad_shared_gate,
        grad_shared_up,
        grad_shared_down,
        *expert_grads,
    )


def solution(mesh):
    ranks, shards_of = mesh.shape["expert"], mesh.shape["dp"]
    local_experts = 2
    split = Mesh(
        mesh.devices.reshape(4, ranks // 4, local_experts, shards_of // local_experts), ALL
    )
    rows = P(ALL, None)
    flat = P(ALL)
    expert = P(("a", "b"), ("l", "s"), None)
    return jax.shard_map(
        shards,
        mesh=split,
        in_specs=(rows,) * 3
        + (flat,)
        + (rows,) * 4
        + (flat,)
        + (rows,) * 4
        + (expert,) * 3
        + (rows,),
        out_specs=(rows,) * 2
        + (flat,)
        + (rows,) * 4
        + (flat,)
        + (rows,) * 4
        + (expert,) * 3,
        check_vma=False,
    )
```

```python
import functools

import jax
import jax.numpy as jnp
from jax import lax
from jax.experimental import pallas as pl
from jax.experimental.pallas import tpu as pltpu
from jax.sharding import Mesh
from jax.sharding import PartitionSpec as P

HEADS = 16
KV_HEADS = 4
HEAD_DIM = 128
TOP = 6
EPS = 1e-06
ROPE_BASE = 10000.0
PLANE = ("a", "b", "l")
ALL = ("a", "b", "l", "s")
F32 = jnp.float32
BF16 = jnp.bfloat16
MESH = pl.DeviceIdType.MESH
VMEM_LIMIT = 60 * 1024 * 1024
DMA = pltpu.SemaphoreType.DMA
ANY = pl.BlockSpec(memory_space=pl.ANY)
VMEM = pl.BlockSpec(memory_space=pltpu.VMEM)


def dot(left, right):
    return jnp.dot(left, right, preferred_element_type=F32)


def dot_tn(left, right):
    return lax.dot_general(left, right, (((0,), (0,)), ((), ())), preferred_element_type=F32)


def dot_nt(left, right):
    return lax.dot_general(left, right, (((1,), (1,)), ((), ())), preferred_element_type=F32)


class Grid:
    def __init__(self, sizes):
        self.na, self.nb, self.nl, self.ns = self.sizes = sizes
        self.a, self.b, self.l, self.s = (lax.axis_index(axis) for axis in "abls")
        self.is_up = self.a < self.na - 1
        self.is_down = self.a > 0

    def at(self, a=None, b=None, l=None, s=None):
        return tuple(
            own if other is None else other
            for own, other in zip((self.a, self.b, self.l, self.s), (a, b, l, s))
        )

    def other(self, axis, step):
        size, own = {"b": (self.nb, self.b), "l": (self.nl, self.l), "s": (self.ns, self.s)}[axis]
        return lax.rem(own + step, size)

    def to(self, axis, step):
        return self.at(**{axis: self.other(axis, step)})

    def hello(self, device):
        pl.semaphore_signal(
            pltpu.get_barrier_semaphore(), inc=1, device_id=device, device_id_type=MESH
        )

    def greet_neighbours(self, siblings):
        @pl.when(self.is_down)
        def _():
            self.hello(self.at(a=self.a - 1))

        @pl.when(self.is_up)
        def _():
            self.hello(self.at(a=self.a + 1))

        count = 0
        for axis, size in (("b", self.nb), ("l", self.nl), ("s", self.ns if siblings else 1)):
            for step in range(1, size):
                self.hello(self.to(axis, step))
                count += 1
        above = 1 - (self.a + 1) // self.na
        below = (self.a + self.na - 1) // self.na
        pl.semaphore_wait(pltpu.get_barrier_semaphore(), count + above + below)

    def greet_plane(self, siblings):
        count = 0
        for index in self.plane_steps():
            self.hello(self.plane_at(index))
            count += 1
        for step in range(1, self.ns if siblings else 1):
            self.hello(self.to("s", step))
            count += 1
        pl.semaphore_wait(pltpu.get_barrier_semaphore(), count)

    def plane_steps(self):
        return [
            (i, j, k)
            for i in range(self.na)
            for j in range(self.nb)
            for k in range(self.nl)
            if i + j + k
        ]

    def plane_at(self, steps, sign=1):
        return self.at(
            a=lax.rem(self.a + sign * steps[0] + self.na, self.na),
            b=lax.rem(self.b + sign * steps[1] + self.nb, self.nb),
            l=lax.rem(self.l + sign * steps[2] + self.nl, self.nl),
        )


def remote(src, dst, sems, device):
    return pltpu.make_async_remote_copy(
        src_ref=src, dst_ref=dst, send_sem=sems[0], recv_sem=sems[1], device_id=device, device_id_type=MESH
    )


def came(g, sem, dst):
    remote(dst, dst, (sem, sem), g.at()).wait_recv()


def left(g, sem, src):
    remote(src, src, (sem, sem), g.at()).wait_send()


class Bounce:
    def __init__(self, src, via, dst, sems):
        self.there = pltpu.make_async_copy(src, via, sems.at[0])
        self.back = pltpu.make_async_copy(via, dst, sems.at[1])

    def start(self):
        self.there.start()

    def turn(self):
        self.there.wait()
        self.back.start()

    def wait(self):
        self.back.wait()


def split_of(wide):
    return (wide * 5 // 7) // 128 * 128


def gather_scratch(sizes, siblings, x):
    na, nb, nl, ns = sizes
    return [
        DMA((2, 2, na)),
        DMA((2, 2, na)),
        DMA((2, nb - 1, na)),
        DMA((2, nl - 1, na)),
        DMA((2, nl - 1, nb - 1, na)),
        DMA((2, nb - 1, nl - 1)),
        DMA((2, ns, na)) if siblings else DMA((2, 1, 1)),
        DMA((2,)),
        pltpu.VMEM(x.shape, x.dtype),
    ]


def gathering(g, siblings, x_ref, o_ref, sems):
    la_sem, lb_sem, b_sem, l_sem, lb2_sem, bl2_sem, s_sem, own_sem, own_buf = sems
    na, nb, nl, ns = g.sizes
    wide = x_ref.shape[-1]
    cut = split_of(wide)
    head, tail = pl.ds(0, cut), pl.ds(cut, wide - cut)
    me = g.s if siblings else 0

    def slot(a, b, l):
        return o_ref.at[a, b, l, me]

    def square(a):
        return o_ref.at[a, :, :, me]

    def pair(sem, *index):
        return sem.at[(0, *index)], sem.at[(1, *index)]

    def cols(origin):
        return (slice(None), head)

    def line_head(way, origin, first=False):
        src = x_ref.at[:, head] if first else slot(origin, g.b, g.l).at[:, head]
        return remote(src, slot(origin, g.b, g.l).at[:, head], pair(la_sem, way, origin), g.at(a=g.a + 1 - 2 * way))

    def line_tail(way, origin):
        block = o_ref.at[origin, :, :, me, :, tail]
        return remote(block, block, pair(lb_sem, way, origin), g.at(a=g.a + 1 - 2 * way))

    def spread(origin, first=False):
        for step in range(1, nl):
            if first:
                remote(x_ref, slot(origin, g.b, g.l), pair(l_sem, step - 1, origin), g.to("l", step)).start()
            else:
                part = slot(origin, g.b, g.l).at[:, head]
                remote(part, part, pair(l_sem, step - 1, origin), g.to("l", step)).start()
        for step in range(1, nb):
            if first:
                remote(x_ref, slot(origin, g.b, g.l), pair(b_sem, step - 1, origin), g.to("b", step)).start()
            else:
                part = slot(origin, g.b, g.l).at[:, head]
                remote(part, part, pair(b_sem, step - 1, origin), g.to("b", step)).start()

    def l_came(step, origin, first=False):
        l_from = g.other("l", nl - step)
        ref = slot(origin, g.b, l_from)
        came(g, l_sem.at[1, step - 1, origin], ref if first else ref.at[:, head])
        return l_from

    def b_came(step, origin, first=False):
        b_from = g.other("b", nb - step)
        ref = slot(origin, b_from, g.l)
        came(g, b_sem.at[1, step - 1, origin], ref if first else ref.at[:, head])
        return b_from

    def relay_head(origin, first=False):
        for step in range(1, nl):
            l_from = l_came(step, origin, first)
            part = slot(origin, g.b, l_from).at[:, head]
            for turn in range(1, nb):
                remote(part, part, pair(lb2_sem, step - 1, turn - 1, origin), g.to("b", turn)).start()

    def relay_tail():
        for step in range(1, nb):
            b_from = b_came(step, g.a, True)
            part = slot(g.a, b_from, g.l).at[:, tail]
            for turn in range(1, nl):
                remote(part, part, pair(bl2_sem, step - 1, turn - 1), g.to("l", turn)).start()

    def diagonal_head(origin):
        for step in range(1, nl):
            for turn in range(1, nb):
                ref = slot(origin, g.other("b", nb - turn), g.other("l", nl - step))
                came(g, lb2_sem.at[1, step - 1, turn - 1, origin], ref.at[:, head])

    def diagonal_tail():
        for step in range(1, nb):
            for turn in range(1, nl):
                ref = slot(g.a, g.other("b", nb - step), g.other("l", nl - turn))
                came(g, bl2_sem.at[1, step - 1, turn - 1], ref.at[:, tail])

    def siblings_send(origin):
        if siblings:
            for step in range(1, ns):
                remote(square(origin), square(origin), pair(s_sem, step - 1, origin), g.to("s", step)).start()

    def when_up_origin(k, act):
        @pl.when(g.a - k >= 0)
        def _():
            act(0, g.a - k)

    def when_down_origin(k, act):
        @pl.when(g.a + k < na)
        def _():
            act(1, g.a + k)

    def both(k, act):
        when_up_origin(k, act)
        when_down_origin(k, act)

    def onward(way, copy):
        @pl.when(g.is_up if way == 0 else g.is_down)
        def _():
            copy.start()

    def head_arrives(way, origin):
        came(g, la_sem.at[1, way, origin], slot(origin, g.b, g.l).at[:, head])
        onward(way, line_head(way, origin))
        spread(origin)

    def tail_arrives(way, origin):
        came(g, lb_sem.at[1, way, origin], o_ref.at[origin, :, :, me, :, tail])
        onward(way, line_tail(way, origin))

    own = Bounce(x_ref, own_buf, slot(g.a, g.b, g.l), own_sem)
    own.start()
    onward(0, line_head(0, g.a, True))
    onward(1, line_head(1, g.a, True))
    spread(g.a, True)
    yield
    own.turn()
    relay_head(g.a, True)
    relay_tail()
    yield
    both(1, head_arrives)
    diagonal_tail()
    own.wait()
    onward(0, line_tail(0, g.a))
    onward(1, line_tail(1, g.a))
    yield
    for k in range(1, na):
        both(k, lambda way, origin: relay_head(origin))
        if k + 1 < na:
            both(k + 1, head_arrives)
        both(k, tail_arrives)
        if k == 1:
            diagonal_head(g.a)
            siblings_send(g.a)
        yield

    def complete(way, origin):
        for step in range(1, nb):
            b_came(step, origin)
        diagonal_head(origin)
        siblings_send(origin)

    for k in range(1, na):
        both(k, complete)
    yield

    def sent_line(way, origin):
        @pl.when(g.is_up if way == 0 else g.is_down)
        def _():
            line_head(way, origin).wait_send()
            line_tail(way, origin).wait_send()

    when_up_origin(0, sent_line)
    when_down_origin(0, sent_line)
    for k in range(1, na):
        both(k, sent_line)

    def sent(way, origin, first=False):
        whole = slot(origin, g.b, g.l)
        for step in range(1, nl):
            left(g, l_sem.at[0, step - 1, origin], whole if first else whole.at[:, head])
            for turn in range(1, nb):
                left(g, lb2_sem.at[0, step - 1, turn - 1, origin], whole.at[:, head])
        for step in range(1, nb):
            left(g, b_sem.at[0, step - 1, origin], whole if first else whole.at[:, head])
        if siblings:
            for step in range(1, ns):
                left(g, s_sem.at[0, step - 1, origin], square(origin))
                came(g, s_sem.at[1, step - 1, origin], o_ref.at[origin, :, :, g.other("s", ns - step)])

    sent(0, g.a, True)
    for step in range(1, nb):
        for turn in range(1, nl):
            left(g, bl2_sem.at[0, step - 1, turn - 1], slot(g.a, g.b, g.l).at[:, tail])
    for k in range(1, na):
        both(k, sent)


def after(count, program):
    for _ in range(count):
        yield
    yield from program


def run_steps(*programs):
    alive = list(programs)
    while alive:
        for program in list(alive):
            try:
                next(program)
            except StopIteration:
                alive.remove(program)


def gather_kernel(sizes, x_ref, shard, o_ref, whole, *sems):
    g = Grid(sizes)
    g.greet_neighbours(True)
    run_steps(
        gathering(g, False, x_ref, o_ref, sems[:9]),
        matrix_steps(g, (shard,), (whole,), sems[9:], (0, 0, 0, 2, 2)),
    )


def gather(x, shard, sizes, collective_id):
    na, nb, nl, ns = sizes
    rows, wide = x.shape
    out, whole = pl.pallas_call(
        functools.partial(gather_kernel, sizes),
        out_shape=[jax.ShapeDtypeStruct((na, nb, nl, 1, rows, wide), x.dtype), matrix_shape(shard, sizes)],
        in_specs=[ANY] * 2,
        out_specs=[ANY] * 2,
        scratch_shapes=gather_scratch(sizes, False, x) + matrix_scratch(sizes, shard),
        compiler_params=pltpu.CompilerParams(collective_id=collective_id, has_side_effects=True, vmem_limit_bytes=VMEM_LIMIT),
    )(x, shard)
    return out.reshape(-1, wide), whole.reshape(-1, shard.shape[2])


CHUNKS = 4


def matrix_scratch(sizes, *shards):
    na, nb, nl, ns = sizes
    count = len(shards)
    return [
        DMA((2, count, nl - 1, CHUNKS)),
        DMA((2, count, nl, ns - 1, CHUNKS)),
        DMA((count, 2)),
        pltpu.VMEM((count, *shards[0].shape[1:]), BF16),
    ]


def matrix_steps(g, shards, wholes, sems, paces):
    e_sem, es_sem, own_sem, own_buf = sems
    na, nb, nl, ns = g.sizes
    count = len(shards)
    rows = shards[0].shape[1] // CHUNKS
    chunks = [(i, pl.ds(c * rows, rows), c) for i in range(count) for c in range(CHUNKS)]

    def across(i, at, c, step):
        to = g.other("l", step)
        return remote(shards[i].at[to, at], wholes[i].at[g.l, g.s, at], (e_sem.at[0, i, step - 1, c], e_sem.at[1, i, step - 1, c]), g.at(l=to))

    def aside(i, at, c, turn, step):
        l_from = g.other("l", nl - turn) if turn else g.l
        src = wholes[i].at[l_from, g.s, at] if turn else shards[i].at[g.l, at]
        return remote(src, wholes[i].at[l_from, g.s, at], (es_sem.at[0, i, turn, step - 1, c], es_sem.at[1, i, turn, step - 1, c]), g.to("s", step))

    def aside_came(i, at, c, turn, step):
        l_from = g.other("l", nl - turn) if turn else g.l
        came(g, es_sem.at[1, i, turn, step - 1, c], wholes[i].at[l_from, g.other("s", ns - step), at])

    owns = [Bounce(shards[i].at[g.l], own_buf.at[i], wholes[i].at[g.l, g.s], own_sem.at[i]) for i in range(count)]
    for copy in owns:
        copy.start()
    rest = list(chunks)
    for j, pace in enumerate(paces):
        for chunk in rest[:pace]:
            for step in range(1, nl):
                across(*chunk, step).start()
            for step in range(1, ns):
                aside(*chunk, 0, step).start()
        rest = rest[pace:]
        if j == 2:
            for copy in owns:
                copy.turn()
        yield
    for chunk in chunks:
        i, at, c = chunk
        for turn in range(1, nl):
            came(g, e_sem.at[1, i, turn - 1, c], wholes[i].at[g.other("l", nl - turn), g.s, at])
            for step in range(1, ns):
                aside(*chunk, turn, step).start()
    yield
    for copy in owns:
        copy.wait()
    for chunk in chunks:
        for step in range(1, nl):
            across(*chunk, step).wait_send()
        for turn in range(nl):
            for step in range(1, ns):
                aside(*chunk, turn, step).wait_send()
                aside_came(*chunk, turn, step)


def matrix_shape(shard, sizes):
    ranks, rows, ffe = shard.shape
    return jax.ShapeDtypeStruct((ranks, sizes[3], rows, ffe), BF16)


def column_steps(g, shared, columns, down, downs, sems):
    c_sem, cs_sem, d_sem, own_sem, own_buf, down_buf = sems
    ns = g.ns
    steps = g.plane_steps()

    def block(n, at):
        a, b, l, _ = g.plane_at(at)
        return remote(shared.at[a, b, l], columns.at[:, g.a, g.b, g.l, g.s], (c_sem.at[0, n], c_sem.at[1, n]), g.plane_at(at))

    def downward(step):
        return remote(down, downs.at[g.s], (d_sem.at[0, step - 1], d_sem.at[1, step - 1]), g.to("s", step))

    def columns_aside(step):
        part = columns.at[:, :, :, :, g.s]
        return remote(part, part, (cs_sem.at[0, step - 1], cs_sem.at[1, step - 1]), g.to("s", step))

    owns = [
        Bounce(shared.at[g.a, g.b, g.l], own_buf, columns.at[:, g.a, g.b, g.l, g.s], own_sem.at[0]),
        Bounce(down, down_buf, downs.at[g.s], own_sem.at[1]),
    ]
    yield
    for copy in owns:
        copy.start()
    for step in range(1, ns):
        downward(step).start()
    yield
    for n, at in enumerate(steps):
        block(n, at).start()
    for copy in owns:
        copy.turn()
    yield
    for copy in owns:
        copy.wait()
    yield
    for n, at in enumerate(steps):
        a, b, l, _ = g.plane_at(at, -1)
        came(g, c_sem.at[1, n], columns.at[:, a, b, l, g.s])
    for step in range(1, ns):
        columns_aside(step).start()
    yield
    for n, at in enumerate(steps):
        block(n, at).wait_send()
    for step in range(1, ns):
        downward(step).wait_send()
        came(g, d_sem.at[1, step - 1], downs.at[g.other("s", ns - step)])
        columns_aside(step).wait_send()
        came(g, cs_sem.at[1, step - 1], columns.at[:, :, :, :, g.other("s", ns - step)])


def inputs_kernel(sizes, dense, wide_dy, gate, up, shared, sh_down, dense_o, dy_o, gate_o, up_o, columns_o, downs_o, *sems):
    g = Grid(sizes)
    g.greet_plane(True)
    run_steps(
        gathering(g, True, dense, dense_o, sems[:9]),
        after(2, gathering(g, False, wide_dy, dy_o, sems[9:18])),
        matrix_steps(g, (gate, up), (gate_o, up_o), sems[18:22], (0, 0, 0, 2, 2, 2, 2)),
        after(2, column_steps(g, shared, columns_o, sh_down, downs_o, sems[22:])),
    )


def inputs_gather(dense, wide_dy, gate, up, shared, sh_down, sizes, collective_id):
    na, nb, nl, ns = sizes
    two, sh_rows, narrow = shared.shape[3:]
    shape = jax.ShapeDtypeStruct
    dense_o, dy_o, gate_o, up_o, columns, downs = pl.pallas_call(
        functools.partial(inputs_kernel, sizes),
        out_shape=[
            shape((na, nb, nl, ns, *dense.shape), BF16),
            shape((na, nb, nl, 1, *wide_dy.shape), BF16),
            matrix_shape(gate, sizes),
            matrix_shape(up, sizes),
            shape((two, na, nb, nl, ns, sh_rows, narrow), BF16),
            shape((ns, *sh_down.shape), BF16),
        ],
        in_specs=[ANY] * 6,
        out_specs=[ANY] * 6,
        scratch_shapes=gather_scratch(sizes, True, dense)
        + gather_scratch(sizes, False, wide_dy)
        + matrix_scratch(sizes, gate, up)
        + [
            DMA((2, na * nb * nl - 1)),
            DMA((2, ns - 1)),
            DMA((2, ns - 1)),
            DMA((2, 2)),
            pltpu.VMEM((two, sh_rows, narrow), BF16),
            pltpu.VMEM(sh_down.shape, BF16),
        ],
        compiler_params=pltpu.CompilerParams(collective_id=collective_id, has_side_effects=True, vmem_limit_bytes=VMEM_LIMIT),
    )(dense, wide_dy, gate, up, shared, sh_down)
    return (
        dense_o.reshape(-1, dense.shape[1]),
        dy_o.reshape(-1, wide_dy.shape[1]),
        gate_o.reshape(-1, gate.shape[2]),
        up_o.reshape(-1, up.shape[2]),
        columns.reshape(two, -1, narrow),
        downs,
    )


def order(a, k):
    high, odd = a // 2, lax.rem(a, 2)
    return (3 * (1 - high), 2 + high - 2 * odd, 1 + odd, a)[k]


def add_rows(out, *terms):
    rows = out.shape[0]
    step = min(rows, 32)

    @pl.loop(0, rows, step=step)
    def _(r):
        at = pl.ds(pl.multiple_of(r, step), step)
        total = terms[0][at, :].astype(F32)
        for term in terms[1:]:
            total = total + term[at, :].astype(F32)
        out[at, :] = total.astype(out.dtype)


def scatter_scratch(sizes, siblings, rows, wide):
    na, nb, nl, ns = sizes
    head = split_of(wide)
    tail = wide - head
    shapes = [
        (nb - 1, na, nl, rows, head),
        (nl - 1, na, rows, head),
        (na, rows, head),
        (na + 1, rows, head),
        (na + 1, nb, nl, rows, tail),
        (nb, nl, rows, tail),
        (nl - 1, nb, rows, tail),
        (nb - 1, rows, tail),
        (ns - 1, na, nb, nl, rows, wide) if siblings else (16, 128),
    ]
    sems = [(2, nb - 1, na), (2, nl - 1, na), (2, 2, na), (2, 2, na), (2, nl - 1), (2, nb - 1), (2, ns - 1, na)]
    return [pltpu.VMEM(s, BF16) for s in shapes] + [DMA(s) for s in sems]


def scattering(g, siblings, p_ref, o_ref, scratch, prepare=None):
    one, two, total, line_a, line_b, tail_sum, tail_two, tail_three, s_buf = scratch[:9]
    b_sem, l_sem, la_sem, lb_sem, l2_sem, b2_sem, s_sem = scratch[9:]
    na, nb, nl, ns = g.sizes
    wide = o_ref.shape[-1]
    cut = split_of(wide)
    head, tail = pl.ds(0, cut), pl.ds(cut, wide - cut)

    def pair(sem, *index):
        return sem.at[(0, *index)], sem.at[(1, *index)]

    def block(k):
        return s_buf.at[0, k] if siblings else p_ref.at[order(g.a, k), :, :, 0]

    def sibling_copy(k, step):
        to = g.other("s", step)
        return remote(p_ref.at[order(g.a, k), :, :, to], s_buf.at[step - 1, k], pair(s_sem, step - 1, k), g.at(s=to))

    def b_copy(k, step):
        to = g.other("b", step)
        return remote(block(k).at[to, :, :, head], one.at[step - 1, k], pair(b_sem, step - 1, k), g.at(b=to))

    def l_copy(k, step):
        to = g.other("l", step)
        return remote(one.at[0, k, to], two.at[step - 1, k], pair(l_sem, step - 1, k), g.at(l=to))

    def place(way, dest, at):
        if way == 0:
            return dest
        far = (at - dest + na - 1) // na
        return dest * far + na * (1 - far)

    def head_copy(way, k):
        dest, to = order(g.a, k), g.a + 1 - 2 * way
        return remote(total.at[k], line_a.at[place(way, dest, to)], pair(la_sem, way, dest), g.at(a=to))

    def tail_copy(way, k, first):
        dest, to = order(g.a, k), g.a + 1 - 2 * way
        src = block(k).at[:, :, :, tail] if first else line_b.at[dest]
        return remote(src, line_b.at[place(way, dest, to)], pair(lb_sem, way, dest), g.at(a=to))

    def starts(k, act):
        if k == na - 1:
            return
        dest = order(g.a, k)

        @pl.when((g.a == 0) & (dest > g.a))
        def _():
            act(0)

        @pl.when((g.a == na - 1) & (dest < g.a))
        def _():
            act(1)

    def passes(k, act):
        if k == na - 1:
            return
        dest = order(g.a, k)

        @pl.when((g.a > 0) & (dest > g.a))
        def _():
            act(0)

        @pl.when((g.a < na - 1) & (dest < g.a))
        def _():
            act(1)

    def arrivals(act):
        mine = place(0, g.a, g.a)

        @pl.when(g.a == 0)
        def _():
            act((1,), (na,))

        @pl.when(g.a == na - 1)
        def _():
            act((0,), (mine,))

        @pl.when((g.a > 0) & (g.a < na - 1))
        def _():
            act((0, 1), (mine, na))

    def begin(k):
        if k >= na:
            return
        if siblings:
            for step in range(1, ns):
                came(g, s_sem.at[1, step - 1, k], s_buf.at[step - 1, k])
            for b in range(nb):
                for l in range(nl):
                    add_rows(s_buf.at[0, k, b, l], p_ref.at[order(g.a, k), b, l, g.s], *[s_buf.at[step, k, b, l] for step in range(ns - 1)])
        for step in range(1, nb):
            b_copy(k, step).start()
        starts(k, lambda way: tail_copy(way, k, True).start())

    def second(k):
        for step in range(1, nb):
            came(g, b_sem.at[1, step - 1, k], one.at[step - 1, k])
        for turn in range(nl):
            l = g.other("l", turn)
            add_rows(one.at[0, k, l], block(k).at[g.b, l, :, head], *[one.at[step, k, l] for step in range(nb - 1)])
            if turn:
                l_copy(k, turn).start()

    def third(k):
        for step in range(1, nl):
            came(g, l_sem.at[1, step - 1, k], two.at[step - 1, k])
        add_rows(total.at[k], one.at[0, k, g.l], *[two.at[step, k] for step in range(nl - 1)])
        starts(k, lambda way: head_copy(way, k).start())

    def pass_head(k):
        def act(way):
            dest = order(g.a, k)
            came(g, la_sem.at[1, way, dest], line_a.at[dest])
            add_rows(total.at[k], total.at[k], line_a.at[dest])
            head_copy(way, k).start()

        passes(k, act)

    def pass_tail(k):
        def act(way):
            dest = order(g.a, k)
            came(g, lb_sem.at[1, way, dest], line_b.at[dest])
            for b in range(nb):
                for l in range(nl):
                    add_rows(line_b.at[dest, b, l], line_b.at[dest, b, l], block(k).at[b, l, :, tail])
            tail_copy(way, k, False).start()

        passes(k, act)

    def tail_here():
        def act(ways, slots):
            for way, slot in zip(ways, slots):
                came(g, lb_sem.at[1, way, g.a], line_b.at[slot])
            for b in range(nb):
                for l in range(nl):
                    add_rows(tail_sum.at[b, l], block(na - 1).at[b, l, :, tail], *[line_b.at[slot, b, l] for slot in slots])

        arrivals(act)
        for step in range(1, nl):
            tail_l(step).start()

    def tail_l(step):
        to = g.other("l", step)
        return remote(tail_sum.at[:, to], tail_two.at[step - 1], pair(l2_sem, step - 1), g.at(l=to))

    def tail_b(step):
        to = g.other("b", step)
        return remote(tail_two.at[0, to], tail_three.at[step - 1], pair(b2_sem, step - 1), g.at(b=to))

    def ahead(k):
        if siblings and k < na:
            prepare(order(g.a, k))
            for step in range(1, ns):
                sibling_copy(k, step).start()

    ahead(0)
    ahead(1)
    begin(0)
    ahead(2)
    begin(1)
    yield
    for k in range(na):
        ahead(k + 3)
        second(k)
        begin(k + 2)
        if k >= 1:
            third(k - 1)
            pass_tail(k - 1)
        if k >= 2:
            pass_head(k - 2)
        yield
    third(na - 1)
    pass_head(na - 2)
    tail_here()
    yield

    def head_here(ways, slots):
        for way, slot in zip(ways, slots):
            came(g, la_sem.at[1, way, g.a], line_a.at[slot])
        add_rows(o_ref.at[:, head], total.at[na - 1], *[line_a.at[slot] for slot in slots])

    for step in range(1, nl):
        came(g, l2_sem.at[1, step - 1], tail_two.at[step - 1])
    for b in range(nb):
        add_rows(tail_two.at[0, b], tail_sum.at[b, g.l], *[tail_two.at[step, b] for step in range(nl - 1)])
    for step in range(1, nb):
        tail_b(step).start()
    arrivals(head_here)
    yield
    for step in range(1, nb):
        came(g, b2_sem.at[1, step - 1], tail_three.at[step - 1])
    add_rows(o_ref.at[:, tail], tail_two.at[0, g.b], *[tail_three.at[step] for step in range(nb - 1)])

    for k in range(na):
        if siblings:
            for step in range(1, ns):
                sibling_copy(k, step).wait_send()
        for step in range(1, nb):
            b_copy(k, step).wait_send()
        for step in range(1, nl):
            l_copy(k, step).wait_send()

        def sent(way, first):
            tail_copy(way, k, first).wait_send()
            head_copy(way, k).wait_send()

        starts(k, lambda way: sent(way, True))
        passes(k, lambda way: sent(way, False))
    for step in range(1, nl):
        tail_l(step).wait_send()
    for step in range(1, nb):
        tail_b(step).wait_send()


def scatter_kernel(sizes, p_ref, o_ref, *scratch):
    g = Grid(sizes)
    g.greet_neighbours(False)
    run_steps(scattering(g, False, p_ref, o_ref, scratch))


def scatter_shapes(partial, sizes):
    na, nb, nl, ns = sizes
    rows, wide = partial.shape[0] // (na * nb * nl), partial.shape[1]
    return partial.reshape(na, nb, nl, 1, rows, wide), jax.ShapeDtypeStruct((rows, wide), F32)


def scatter(partial, sizes, collective_id):
    split, out = scatter_shapes(partial, sizes)
    return pl.pallas_call(
        functools.partial(scatter_kernel, sizes),
        out_shape=out,
        in_specs=[VMEM],
        out_specs=VMEM,
        scratch_shapes=scatter_scratch(sizes, False, *out.shape),
        compiler_params=pltpu.CompilerParams(collective_id=collective_id, has_side_effects=True, vmem_limit_bytes=VMEM_LIMIT),
    )(split)


def fits(partial):
    return partial.size <= 2048 * 2048


def each_tile(wide, tile, body):
    @pl.loop(0, wide // tile)
    def _(i):
        body(pl.ds(pl.multiple_of(i * tile, tile), tile))


def back_steps(dg, du, wg, wu, sgu, dsgu, back_ref, dx_o, scratch):
    *bufs, row_buf, stage, load_sem, out_sem = scratch
    dg_v, du_v, wg_v, wu_v, sgu_v, dsgu_v = bufs
    steps, toks, slots = back_ref.shape
    width = wg.shape[0]
    loads = [
        pltpu.make_async_copy(src, dst, load_sem.at[i])
        for i, (src, dst) in enumerate(zip((dg, du, wg, wu, sgu, dsgu), bufs))
    ]
    for load in loads:
        load.start()
    yield
    for load in loads:
        load.wait()

    def out_copy(t):
        return pltpu.make_async_copy(stage.at[t % 2], dx_o.at[pl.ds(t * toks, toks)], out_sem.at[t % 2])

    for t in range(steps):
        mine, theirs = pl.ds(t * slots, slots), pl.ds(t * toks, toks)

        @functools.partial(each_tile, width, 512)
        def _(cols):
            rows = dot_nt(dg_v[mine, :], wg_v[cols, :]) + dot_nt(du_v[mine, :], wu_v[cols, :])
            row_buf[:, cols] = rows.astype(BF16)

        yield
        if t >= 2:
            out_copy(t - 2).wait()

        @functools.partial(each_tile, width, 512)
        def _(cols):
            total = dot(back_ref[t], row_buf[:, cols]) + dot_nt(dsgu_v[theirs, :], sgu_v[cols, :])
            stage[t % 2, :, cols] = total.astype(BF16)

        out_copy(t).start()
        yield
    for t in range(max(steps - 2, 0), steps):
        out_copy(t).wait()


def back_kernel(sizes, scattered, *refs):
    ins, refs = refs[: 7 + scattered], refs[7 + scattered :]
    outs, scratch = refs[: 1 + scattered], refs[1 + scattered :]
    programs = [back_steps(*ins[:7], outs[0], scratch[:10])]
    if scattered:
        g = Grid(sizes)
        g.greet_neighbours(False)
        programs.insert(0, scattering(g, False, ins[7], outs[1], scratch[10:]))
    run_steps(*programs)


def back_rows(dg, du, wg, wu, sgu, dsgu, back, partial, sizes, first_id):
    steps, toks, slots = back.shape
    width, ffe = wg.shape
    together = fits(partial)
    split, total = scatter_shapes(partial, sizes)
    params = {"collective_id": first_id, "has_side_effects": True} if together else {}
    sources = (dg, du, wg, wu, sgu, dsgu)
    out = pl.pallas_call(
        functools.partial(back_kernel, sizes, int(together)),
        out_shape=[jax.ShapeDtypeStruct((steps * toks, width), BF16)] + [total] * together,
        in_specs=[ANY] * 6 + [VMEM] + [VMEM] * together,
        out_specs=[ANY] + [VMEM] * together,
        scratch_shapes=[pltpu.VMEM(source.shape, BF16) for source in sources]
        + [pltpu.VMEM((slots, width), BF16), pltpu.VMEM((2, toks, width), BF16), DMA((6,)), DMA((2,))]
        + (scatter_scratch(sizes, False, *total.shape) if together else []),
        compiler_params=pltpu.CompilerParams(vmem_limit_bytes=VMEM_LIMIT, **params),
    )(*sources, back, *([split] if together else []))
    return out if together else (out[0], scatter(partial, sizes, first_id))


def shared_steps(g, part, blocks, own, other, sems):
    s_sem, c_sem, own_sem = sems
    na, nb, nl, ns = g.sizes
    steps = g.plane_steps()

    def aside(step):
        to = g.other("s", step)
        return remote(part.at[:, :, :, to], other.at[step - 1], (s_sem.at[0, step - 1], s_sem.at[1, step - 1]), g.at(s=to))

    def send(n, at):
        a, b, l, _ = g.plane_at(at)
        return remote(other.at[0, a, b, l], blocks.at[g.a, g.b, g.l], (c_sem.at[0, n], c_sem.at[1, n]), g.plane_at(at))

    mine = pltpu.make_async_copy(part.at[:, :, :, g.s], own, own_sem.at[0])
    mine.start()
    for step in range(1, ns):
        aside(step).start()
    yield
    mine.wait()
    for step in range(1, ns):
        came(g, s_sem.at[1, step - 1], other.at[step - 1])
    for a in range(na):
        for b in range(nb):
            for l in range(nl):
                add_rows(other.at[0, a, b, l], own.at[a, b, l], *[other.at[step, a, b, l] for step in range(ns - 1)])
    for n, at in enumerate(steps):
        send(n, at).start()
    here = pltpu.make_async_copy(other.at[0, g.a, g.b, g.l], blocks.at[g.a, g.b, g.l], own_sem.at[1])
    here.start()
    yield
    yield
    yield
    yield
    here.wait()
    for n, at in enumerate(steps):
        a, b, l, _ = g.plane_at(at, -1)
        came(g, c_sem.at[1, n], blocks.at[a, b, l])
        send(n, at).wait_send()
    for step in range(1, ns):
        aside(step).wait_send()


def across_steps(g, blocks, outs, sem):
    def send(step):
        return remote(blocks.at[step - 1], outs.at[step - 1], (sem.at[0, step - 1], sem.at[1, step - 1]), g.to("l", step))

    for step in range(1, g.nl):
        send(step).start()
    yield
    for step in range(1, g.nl):
        send(step).wait()


def outputs_kernel(sizes, normed, grads, mixed, gh, small, shared_ref, cross_ref, o_ref, blocks_ref, cross_o, p_buf, own, other, *scratch):
    g = Grid(sizes)
    na, nb, nl, ns = sizes
    g.greet_plane(True)
    rows = p_buf.shape[4]
    chunk = nb * nl * ns * rows
    left = grads.shape[1]

    def prepare(a):
        at = pl.ds(pl.multiple_of(a * chunk, chunk), chunk)

        def store(value, cols):
            value = value.astype(BF16)
            for n in range(nb * nl * ns):
                b, l, s = n // (nl * ns), n // ns % nl, n % ns
                p_buf[a, b, l, s, :, cols] = value[n * rows : (n + 1) * rows]

        for base, one, two in ((0, normed, grads), (left, mixed, gh)):
            tile = 512
            @pl.loop(0, two.shape[1], step=tile)
            def _(c):
                c = pl.multiple_of(c, tile)
                store(dot_tn(one[:, at], two[:, pl.ds(c, tile)]), pl.ds(pl.multiple_of(base + c, 128), tile))
        store(small[at, :], pl.ds(left + gh.shape[1], small.shape[1]))

    run_steps(
        scattering(g, True, p_buf, o_ref, scratch[4:], prepare),
        shared_steps(g, shared_ref, blocks_ref, own, other, scratch[:3]),
        across_steps(g, cross_ref, cross_o, scratch[3]),
    )


def outputs_scatter(normed, grads, mixed, gh, small, shared, cross, sizes, collective_id):
    na, nb, nl, ns = sizes
    rows = normed.shape[1] // (na * nb * nl * ns)
    wide = grads.shape[1] + gh.shape[1] + small.shape[1]
    shared = shared.reshape(na, nb, nl, ns, -1, shared.shape[1])
    shape = jax.ShapeDtypeStruct
    return pl.pallas_call(
        functools.partial(outputs_kernel, sizes),
        out_shape=[
            shape((rows, wide), F32),
            shape((na, nb, nl, *shared.shape[4:]), BF16),
            shape(cross.shape, BF16),
        ],
        in_specs=[VMEM] * 5 + [ANY] * 2,
        out_specs=[VMEM] + [ANY] * 2,
        scratch_shapes=[
            pltpu.VMEM((na, nb, nl, ns, rows, wide), BF16),
            pltpu.VMEM((na, nb, nl, *shared.shape[4:]), BF16),
            pltpu.VMEM((ns - 1, na, nb, nl, *shared.shape[4:]), BF16),
            DMA((2, ns - 1)),
            DMA((2, na * nb * nl - 1)),
            DMA((2,)),
            DMA((2, nl - 1)),
        ]
        + scatter_scratch(sizes, True, rows, wide),
        compiler_params=pltpu.CompilerParams(collective_id=collective_id, has_side_effects=True, vmem_limit_bytes=VMEM_LIMIT),
    )(normed, grads, mixed, gh, small, shared, cross)


def weight_steps(g, gp, inner, xr, dg, du, own_os, cross_os, crossed_o, scratch):
    left_buf, right_buf, send, recv, own_buf, cross_buf, load_sem, s_sem, c_sem, l_sem = scratch
    na, nb, nl, ns = g.sizes
    rows, ffe = own_buf.shape
    lefts, rights = (xr, xr, gp), (dg, du, inner)

    def load_left(i):
        return pltpu.make_async_copy(lefts[i], left_buf, load_sem.at[0])

    def load_right(i):
        return pltpu.make_async_copy(rights[i], right_buf.at[i % 2], load_sem.at[1 + i % 2])

    def product(i, l, s, out):
        at = (l * ns + s) * rows
        step = 256

        @pl.loop(0, rows, step=step)
        def _(r):
            cols = pl.ds(pl.multiple_of(at + r, step), step)
            for to, tile in column_tiles(ffe, 512):
                value = dot_tn(left_buf[:, cols], right_buf[i % 2, :, pl.ds(to, tile)])
                out[pl.ds(pl.multiple_of(r, step), step), pl.ds(to, tile)] = value.astype(out.dtype)

    def aside(i, turn, step):
        return remote(send.at[turn, step - 1], recv.at[i, turn, step - 1], (s_sem.at[0, i, turn, step - 1], s_sem.at[1, i, turn, step - 1]), g.to("s", step))

    def keep(i):
        return [pltpu.make_async_copy(own_buf, own_os[i], c_sem.at[i, 0])] + [
            pltpu.make_async_copy(cross_buf.at[turn - 1], cross_os[i].at[turn - 1], c_sem.at[i, turn])
            for turn in range(1, nl)
        ]

    def over(step):
        return remote(cross_os[0].at[step - 1], crossed_o.at[step - 1], (l_sem.at[0, step - 1], l_sem.at[1, step - 1]), g.to("l", step))

    def sums(i):
        for turn in range(nl):
            out = cross_buf.at[turn - 1] if turn else own_buf
            for step in range(1, ns):
                came(g, s_sem.at[1, i, turn, step - 1], recv.at[i, turn, step - 1])
            add_rows(out, out, *[recv.at[i, turn, step] for step in range(ns - 1)])
        for copy in keep(i):
            copy.start()

    def kept(i):
        for copy in keep(i):
            copy.wait()
        if i == 0:
            for step in range(1, nl):
                over(step).start()

    load_left(0).start()
    load_right(0).start()
    load_right(1).start()
    yield
    load_left(0).wait()
    for i in range(3):
        load_right(i).wait()
        if i == 2:
            load_left(2).wait()
        for turn in range(nl):
            for step in range(1, ns):
                if i >= 1:
                    aside(i - 1, turn, step).wait_send()
                product(i, g.other("l", turn), g.other("s", step), send.at[turn, step - 1])
                aside(i, turn, step).start()
        yield
        if i >= 1:
            sums(i - 1)
            kept(i - 1)
        for turn in range(nl):
            product(i, g.other("l", turn), g.s, cross_buf.at[turn - 1] if turn else own_buf)
        if i == 0:
            load_right(2).start()
        if i == 1:
            load_left(2).start()
        yield
    sums(2)
    kept(2)
    yield
    for step in range(1, nl):
        over(step).wait()
    for turn in range(nl):
        for step in range(1, ns):
            aside(2, turn, step).wait_send()


def weights_kernel(sizes, scattered, *refs):
    g = Grid(sizes)
    g.greet_neighbours(True)
    ins, refs = refs[: 5 + scattered], refs[5 + scattered :]
    outs, scratch = refs[: 7 + scattered], refs[7 + scattered :]
    programs = [weight_steps(g, *ins[:5], outs[:3], outs[3:6], outs[6], scratch[:10])]
    if scattered:
        programs.insert(0, scattering(g, False, ins[5], outs[7], scratch[10:]))
    run_steps(*programs)


def expert_weights(gp, inner, xr, dg, du, partial, sizes, first_id, second_id):
    na, nb, nl, ns = sizes
    rows, ffe = gp.shape[1] // (nl * ns), inner.shape[1]
    together = fits(partial)
    split, total = scatter_shapes(partial, sizes)
    shape = jax.ShapeDtypeStruct
    out = pl.pallas_call(
        functools.partial(weights_kernel, sizes, int(together)),
        out_shape=[
            *[shape((rows, ffe), F32)] * 3,
            *[shape((nl - 1, rows, ffe), BF16)] * 4,
        ]
        + [total] * together,
        in_specs=[ANY] * 5 + [VMEM] * together,
        out_specs=[ANY] * 7 + [VMEM] * together,
        scratch_shapes=[
            pltpu.VMEM(gp.shape, BF16),
            pltpu.VMEM((2, *inner.shape), BF16),
            pltpu.VMEM((nl, ns - 1, rows, ffe), BF16),
            pltpu.VMEM((3, nl, ns - 1, rows, ffe), BF16),
            pltpu.VMEM((rows, ffe), F32),
            pltpu.VMEM((nl - 1, rows, ffe), BF16),
            DMA((3,)),
            DMA((2, 3, nl, ns - 1)),
            DMA((3, nl)),
            DMA((2, nl - 1)),
        ]
        + (scatter_scratch(sizes, False, *total.shape) if together else []),
        compiler_params=pltpu.CompilerParams(collective_id=first_id, has_side_effects=True, vmem_limit_bytes=VMEM_LIMIT),
    )(gp, inner, xr, dg, du, *([split] if together else []))
    own, (_, second, third, crossed) = out[:3], out[3:7]
    return own, crossed, second, third, out[7] if together else scatter(partial, sizes, second_id)


def rms_norm(values, gain_row):
    factor = lax.rsqrt(jnp.mean(values * values, axis=-1, keepdims=True) + EPS)
    return values * factor * gain_row


def rotate(values):
    length = values.shape[0]
    half_dim = values.shape[-1] // 2
    position = jnp.arange(length).astype(F32)
    inverse = ROPE_BASE ** (-jnp.arange(half_dim).astype(F32) * 2.0 / values.shape[-1])
    angle_table = position[:, None] * inverse[None, :]
    cosine = jnp.cos(angle_table)[:, None, :]
    sine = jnp.sin(angle_table)[:, None, :]
    lower = values[..., :half_dim]
    upper = values[..., half_dim:]
    return jnp.concatenate(
        [lower * cosine - upper * sine, upper * cosine + lower * sine], axis=-1
    )


def lane_pad(block):
    return jnp.pad(block, ((0, 0), (0, -block.shape[1] % 128)))


def silu_pair(gate_part, up_part):
    return jax.nn.silu(gate_part) * up_part


def silu_parts(v):
    sig = 1.0 / (1.0 + jnp.exp(-v))
    return sig, v * sig


def exact(left, right, dims):
    return lax.dot_general(
        left, right, (dims, ((), ())), preferred_element_type=F32, precision=lax.Precision.HIGHEST
    )


def column_tiles(wide, tile):
    return [(at, min(tile, wide - at)) for at in range(0, wide, tile)]


def moe_kernel(x_ref, dy_ref, pick_ref, back_ref, router_ref, wg_ref, wu_ref, wd_ref, sgu_ref, sd_ref,
               xr_ref, gp_ref, inner_ref, dg_ref, du_ref, share_ref, dsgu_ref, out_ref, gg_ref,
               g_buf, u_buf, dyr_buf, gate_buf, sum_buf, mm_buf):
    toks, width = x_ref.shape
    ffe = wg_ref.shape[1]
    narrow = sd_ref.shape[0]
    lane = lax.broadcasted_iota(jnp.int32, (toks, 128), 1)
    mine = (lax.axis_index(PLANE) == lane).astype(F32)

    hot = dy_ref[:, pl.ds(width, 128)].astype(F32)
    logits = jnp.where(hot > 0, dot(x_ref[...], router_ref[...]), -1e30)
    top = jnp.max(logits, axis=1, keepdims=True)
    raised = jnp.exp(logits - top)
    gate = jnp.sum(raised * mine, axis=1, keepdims=True) / jnp.sum(raised, axis=1, keepdims=True)
    gate = jnp.broadcast_to(gate, (toks, 128))
    gate_buf[...] = exact(pick_ref[...].astype(F32), gate, ((1,), (0,)))
    for at, tile in column_tiles(width, 512):
        cols = pl.ds(at, tile)
        xr_ref[:, cols] = dot(pick_ref[...], x_ref[:, cols]).astype(BF16)
        dyr_buf[:, cols] = dot(pick_ref[...], dy_ref[:, cols]).astype(BF16)

    for at, tile in column_tiles(ffe, 256):
        cols = pl.ds(at, tile)
        g = dot(xr_ref[...], wg_ref[:, cols])
        u = dot(xr_ref[...], wu_ref[:, cols])
        g_buf[:, cols] = g
        u_buf[:, cols] = u
        inner_ref[:, cols] = (silu_parts(g)[1] * u).astype(BF16)
    share_gu = dot(x_ref[...], sgu_ref[...])
    d_share = dot_nt(dy_ref[:, pl.ds(0, width)], sd_ref[...])
    sg, su = share_gu[:, :narrow], share_gu[:, narrow:]
    sig, act = silu_parts(sg)
    share_ref[...] = (act * su).astype(BF16)
    dsgu_ref[:, :narrow] = (d_share * su * sig * (1.0 + sg * (1.0 - sig))).astype(BF16)
    dsgu_ref[:, narrow:] = (d_share * act).astype(BF16)
    sum_buf[...] = jnp.zeros_like(sum_buf)
    for at, tile in column_tiles(width, 256):
        cols = pl.ds(at, tile)
        produced = dot_nt(inner_ref[...], wd_ref[cols, :])
        dyr = dyr_buf[:, cols].astype(F32)
        gate = gate_buf[:, pl.ds(0, 1)]
        for half in range(0, tile, 128):
            sum_buf[...] += produced[:, half : half + 128] * dyr[:, half : half + 128]
        gp_ref[:, cols] = (gate * dyr).astype(BF16)
        mm_buf[:, cols] = (gate * produced).astype(BF16)
    for at, tile in column_tiles(width, 256):
        cols = pl.ds(at, tile)
        out_ref[:, cols] = (dot(back_ref[...], mm_buf[:, cols]) + dot(share_ref[...], sd_ref[:, cols])).astype(BF16)
    total = jnp.broadcast_to(jnp.sum(sum_buf[...], axis=1, keepdims=True), sum_buf.shape)
    gg_ref[0] = exact(total, pick_ref[...].astype(F32), ((0,), (0,)))[:8]

    for at, tile in column_tiles(ffe, 256):
        cols = pl.ds(at, tile)
        d_inner = dot(gp_ref[...], wd_ref[:, cols])
        g, u = g_buf[:, cols], u_buf[:, cols]
        sig, act = silu_parts(g)
        dg_ref[:, cols] = (d_inner * u * sig * (1.0 + g * (1.0 - sig))).astype(BF16)
        du_ref[:, cols] = (d_inner * act).astype(BF16)


def moe(x_all, wide_dy, pick, back, router, wg, wu, wd, sgu, sd):
    steps, slots, toks = pick.shape
    width, ffe, narrow = x_all.shape[1], wg.shape[1], sd.shape[0]
    shape = jax.ShapeDtypeStruct

    def rows(count, wide):
        return pl.BlockSpec((count, wide), lambda i: (i, 0))

    def whole(array):
        return pl.BlockSpec(array.shape, lambda i: (0, 0), pipeline_mode=pl.Buffered(1))

    def out(count, wide):
        return shape((steps * count, wide), BF16)

    return pl.pallas_call(
        moe_kernel,
        grid=(steps,),
        in_specs=[
            rows(toks, width),
            rows(toks, wide_dy.shape[1]),
            pl.BlockSpec((None, slots, toks), lambda i: (i, 0, 0)),
            pl.BlockSpec((None, toks, slots), lambda i: (i, 0, 0)),
            *[whole(w) for w in (router, wg, wu, wd, sgu, sd)],
        ],
        out_specs=[
            rows(slots, width),
            rows(slots, width),
            rows(slots, ffe),
            rows(slots, ffe),
            rows(slots, ffe),
            rows(toks, narrow),
            rows(toks, 2 * narrow),
            rows(toks, width),
            pl.BlockSpec((1, 8, toks), lambda i: (i, 0, 0)),
        ],
        out_shape=[
            out(slots, width),
            out(slots, width),
            out(slots, ffe),
            out(slots, ffe),
            out(slots, ffe),
            out(toks, narrow),
            out(toks, 2 * narrow),
            out(toks, width),
            shape((steps, 8, toks), F32),
        ],
        scratch_shapes=[
            pltpu.VMEM((slots, ffe), F32),
            pltpu.VMEM((slots, ffe), F32),
            pltpu.VMEM((slots, width), BF16),
            pltpu.VMEM((slots, 128), F32),
            pltpu.VMEM((slots, 128), F32),
            pltpu.VMEM((slots, width), BF16),
        ],
        compiler_params=pltpu.CompilerParams(vmem_limit_bytes=VMEM_LIMIT),
        cost_estimate=pl.CostEstimate(flops=6 * 10**10, bytes_accessed=10**8, transcendentals=0),
    )(x_all, wide_dy, pick, back, router, wg, wu, wd, sgu, sd)


def shards(
    tokens,
    doc_ids,
    routes,
    gain_attn,
    w_query,
    w_key,
    w_value,
    w_out,
    gain_moe,
    w_router,
    shared_gate,
    shared_up,
    shared_down,
    expert_gate,
    expert_up,
    expert_down,
    cotangent,
):
    length, width = tokens.shape
    group_size = HEADS // KV_HEADS
    score_scale = HEAD_DIM ** (-0.5)
    local_experts = expert_gate.shape[0]
    sub = lax.axis_size("s")
    groups = lax.axis_size("a") * lax.axis_size("b") * lax.axis_size("l")
    experts_total = groups
    capacity = length * TOP * 4 // (3 * experts_total)
    sizes = tuple(lax.axis_size(axis) for axis in ALL)
    my_expert = lax.axis_index(PLANE)
    kvw = w_key.shape[1]
    qw = w_query.shape[1]

    small = jnp.concatenate(
        [w_router, gain_attn[:, None], gain_moe[:, None]], axis=1
    )
    small = lane_pad(small)
    hot = jnp.any(routes[:, :, None] == jnp.arange(experts_total)[None, None, :], axis=1)
    wide_dy = jnp.concatenate([cotangent, lane_pad(hot.astype(BF16))], axis=1)
    shared = jnp.stack([shared_gate, shared_up]).reshape(2, shared_gate.shape[0], *sizes[:3], -1)
    sh_rows = shared_down.shape[0]
    sh_pad = -sh_rows % 16
    dense, dy_all, wg, wu, columns, downs = inputs_gather(
        jnp.concatenate([w_query, w_key, w_value, w_out, small], axis=1),
        wide_dy,
        expert_gate,
        expert_up,
        shared.transpose(2, 3, 4, 0, 1, 5),
        jnp.pad(shared_down, ((0, sh_pad), (0, 0))),
        sizes,
        1,
    )
    sgu = jnp.concatenate([lane_pad(columns[0]), lane_pad(columns[1])], axis=1)
    narrow = columns.shape[2]
    sd_w = downs[:, :sh_rows].reshape(-1, width)
    sd_w = jnp.pad(sd_w, ((0, -narrow % 128), (0, 0)))
    hot_all = dy_all[:, width : width + experts_total] > 0
    query_full = dense[:, :qw]
    key_full = dense[:, qw : qw + kvw]
    value_full = dense[:, qw + kvw : qw + 2 * kvw]
    out_full = dense[:, qw + 2 * kvw : qw + 2 * kvw + width]
    rest = dense[:, qw + 2 * kvw + width :]
    router_full = rest[:, :experts_total]
    attn_gain = rest[:, experts_total].astype(F32)
    moe_gain = rest[:, experts_total + 1].astype(F32)

    inputs = tokens.astype(F32)
    normed, attn_norm_pull = jax.vjp(rms_norm, inputs, attn_gain)
    normed_low = normed.astype(BF16)
    query_pre = dot(normed_low, query_full).reshape(length, HEADS, HEAD_DIM)
    key_pre = dot(normed_low, key_full).reshape(length, KV_HEADS, HEAD_DIM)
    value_low = dot(normed_low, value_full).astype(BF16).reshape(length, KV_HEADS, HEAD_DIM)
    query_rot, query_pull = jax.vjp(rotate, query_pre)
    key_rot, key_pull = jax.vjp(rotate, key_pre)
    query_low = query_rot.astype(BF16).reshape(length, KV_HEADS, group_size, HEAD_DIM)
    key_low = key_rot.astype(BF16)
    position = jnp.arange(length)
    doc_row = doc_ids[0]
    allowed = (position[None, :] <= position[:, None]) & (doc_row[None, :] == doc_row[:, None])
    scores = (
        jnp.einsum("tkgd,skd->kgts", query_low, key_low, preferred_element_type=F32) * score_scale
    )
    scores = jnp.where(allowed, scores, -1e30)
    exp_scores = jnp.exp(scores - jnp.max(scores, axis=-1, keepdims=True))
    attend = exp_scores / jnp.sum(exp_scores, axis=-1, keepdims=True)
    attend_low = attend.astype(BF16)
    mixed_low = (
        jnp.einsum("kgts,skd->tkgd", attend_low, value_low, preferred_element_type=F32)
        .reshape(length, HEADS * HEAD_DIM)
        .astype(BF16)
    )
    hidden = inputs + dot(mixed_low, out_full)
    normed_moe, moe_norm_pull = jax.vjp(rms_norm, hidden, moe_gain)
    moe_low = normed_moe.astype(BF16)

    x_all, wd = gather(moe_low, expert_down, sizes, 2)
    seqs = groups
    mine = jnp.any(hot_all & (jnp.arange(experts_total)[None, :] == my_expert), axis=1)
    mine = mine.reshape(seqs, length)
    hits = mine.astype(jnp.int32)
    before = jnp.cumsum(hits, axis=1) - hits
    slot_hot = (jnp.arange(capacity)[None, :, None] == before[:, None, :]) & mine[:, None, :]
    together = min(seqs, 4)
    slot_hot = slot_hot.reshape(-1, together, capacity, 1, length)
    slot_hot = slot_hot & jnp.eye(together, dtype=bool)[None, :, None, :, None]
    slot_hot = slot_hot.reshape(-1, together * capacity, together * length).astype(BF16)
    token_hot = slot_hot.transpose(0, 2, 1)
    x_rows, gp, inner_low, dg, du, share_low, dsgu, part, gate_grad = moe(
        x_all, dy_all, slot_hot, token_hot, lane_pad(router_full), wg, wu, wd, sgu, sd_w
    )
    gate_grad = gate_grad[:, 0].reshape(seqs, length)
    gate_grad = lax.all_to_all(gate_grad, PLANE, split_axis=0, concat_axis=0, tiled=True)
    dy_all = dy_all[:, :width]
    dx_part, moe_out = back_rows(dg, du, wg, wu, sgu, dsgu, token_hot, part, sizes, 3)
    own_experts, cross_gate, cross_up, cross_down, dx = expert_weights(
        gp, inner_low, x_rows, dg, du, dx_part, sizes, 4, 6
    )
    ranks = sizes[2]
    cross_up = [
        lax.ppermute(cross_up[step - 1], "l", [(i, (i + step) % ranks) for i in range(ranks)])
        for step in range(1, ranks)
    ]
    output = (hidden + moe_out).astype(BF16)
    shared_grads = dot_tn(x_all, dsgu).astype(BF16)
    grad_shared_down = lax.psum_scatter(
        dot_tn(share_low[:, :narrow], dy_all), "s", scatter_dimension=0, tiled=True
    )

    own_logits = jnp.where(hot, dot(moe_low, router_full), -1e30)
    own_gates = jax.nn.softmax(own_logits, axis=-1)
    grad_gate = gate_grad.reshape(experts_total, length).T
    grad_logits = own_gates * (
        grad_gate - jnp.sum(own_gates * grad_gate, axis=-1, keepdims=True)
    )
    grad_logits = grad_logits.astype(BF16)
    grad_router = dot_tn(moe_low, grad_logits)
    dx = dx + dot_nt(grad_logits, router_full)
    grad_hidden_norm, grad_gain_moe = moe_norm_pull(dx)
    grad_hidden = cotangent.astype(F32) + grad_hidden_norm

    grad_hidden_low = grad_hidden.astype(BF16)
    grad_mixed = (
        dot_nt(grad_hidden_low, out_full)
        .astype(BF16)
        .reshape(length, KV_HEADS, group_size, HEAD_DIM)
    )
    grad_value = jnp.einsum("kgts,tkgd->skd", attend_low, grad_mixed, preferred_element_type=F32)
    grad_attend = jnp.einsum("tkgd,skd->kgts", grad_mixed, value_low, preferred_element_type=F32)
    grad_scores = (
        attend * (grad_attend - jnp.sum(grad_attend * attend, axis=-1, keepdims=True))
    ).astype(BF16)
    grad_query = (
        jnp.einsum("kgts,skd->tkgd", grad_scores, key_low, preferred_element_type=F32) * score_scale
    )
    grad_key = (
        jnp.einsum("kgts,tkgd->skd", grad_scores, query_low, preferred_element_type=F32)
        * score_scale
    )
    grad_query_low = (
        query_pull(grad_query.reshape(length, HEADS, HEAD_DIM))[0].reshape(length, -1).astype(BF16)
    )
    grad_key_low = key_pull(grad_key)[0].reshape(length, -1).astype(BF16)
    grad_value_low = grad_value.reshape(length, -1).astype(BF16)
    grad_normed = (
        dot_nt(grad_query_low, query_full)
        + dot_nt(grad_key_low, key_full)
        + dot_nt(grad_value_low, value_full)
    )
    grad_inputs_norm, grad_gain_attn = attn_norm_pull(grad_normed)
    grad_tokens = grad_hidden + grad_inputs_norm
    grad_small = jnp.concatenate(
        [grad_router, grad_gain_attn[:, None], grad_gain_moe[:, None]], axis=1
    )
    grad_small = lane_pad(grad_small)
    grad_small, cross_up = lax.optimization_barrier((grad_small, cross_up))
    total, blocks, cross_down = outputs_scatter(
        normed_low,
        jnp.concatenate([grad_query_low, grad_key_low, grad_value_low], axis=1),
        mixed_low,
        grad_hidden_low,
        grad_small,
        shared_grads,
        cross_down,
        sizes,
        5,
    )
    dense_sum, small_sum = total[:, :-128], total[:, -128:]
    blocks = blocks.reshape(groups, *blocks.shape[3:]).transpose(1, 0, 2).astype(F32)
    half = blocks.shape[2] // 2
    grad_shared_gate = blocks[:, :, :narrow].reshape(blocks.shape[0], -1)
    grad_shared_up = blocks[:, :, half : half + narrow].reshape(blocks.shape[0], -1)
    my_l = lax.axis_index("l")
    expert_grads = []
    for grad, cross in zip(own_experts, (cross_gate, cross_up, cross_down)):
        here = jnp.arange(local_experts)[:, None, None]
        grad = grad[None]
        for step in range(1, local_experts):
            from_l = (my_l - step) % local_experts
            grad = jnp.where(here == from_l, cross[step - 1].astype(F32)[None], grad)
        expert_grads.append(grad)
    return (
        output,
        grad_tokens,
        small_sum[:, experts_total],
        dense_sum[:, :qw],
        dense_sum[:, qw : qw + kvw],
        dense_sum[:, qw + kvw : qw + 2 * kvw],
        dense_sum[:, qw + 2 * kvw :],
        small_sum[:, experts_total + 1],
        small_sum[:, :experts_total],
        grad_shared_gate,
        grad_shared_up,
        grad_shared_down,
        *expert_grads,
    )


def solution(mesh):
    ranks, shards_of = mesh.shape["expert"], mesh.shape["dp"]
    local_experts = 2
    split = Mesh(
        mesh.devices.reshape(4, ranks // 4, local_experts, shards_of // local_experts), ALL
    )
    rows = P(ALL, None)
    flat = P(ALL)
    expert = P(("a", "b"), ("l", "s"), None)
    return jax.shard_map(
        shards,
        mesh=split,
        in_specs=(rows,) * 3
        + (flat,)
        + (rows,) * 4
        + (flat,)
        + (rows,) * 4
        + (expert,) * 3
        + (rows,),
        out_specs=(rows,) * 2
        + (flat,)
        + (rows,) * 4
        + (flat,)
        + (rows,) * 4
        + (expert,) * 3,
        check_vma=False,
    )
```

```python
import functools

import jax
import jax.numpy as jnp
from jax import lax
from jax.experimental import pallas as pl
from jax.experimental.pallas import tpu as pltpu
from jax.sharding import Mesh
from jax.sharding import PartitionSpec as P

HEADS = 16
KV_HEADS = 4
HEAD_DIM = 128
TOP = 6
EPS = 1e-06
ROPE_BASE = 10000.0
PLANE = ("a", "b", "l")
ALL = ("a", "b", "l", "s")
F32 = jnp.float32
BF16 = jnp.bfloat16
MESH = pl.DeviceIdType.MESH
VMEM_LIMIT = 60 * 1024 * 1024
DMA = pltpu.SemaphoreType.DMA
ANY = pl.BlockSpec(memory_space=pl.ANY)
VMEM = pl.BlockSpec(memory_space=pltpu.VMEM)


def dot(left, right):
    return jnp.dot(left, right, preferred_element_type=F32)


def dot_tn(left, right):
    return lax.dot_general(left, right, (((0,), (0,)), ((), ())), preferred_element_type=F32)


def dot_nt(left, right):
    return lax.dot_general(left, right, (((1,), (1,)), ((), ())), preferred_element_type=F32)


class Grid:
    def __init__(self, sizes):
        self.na, self.nb, self.nl, self.ns = self.sizes = sizes
        self.a, self.b, self.l, self.s = (lax.axis_index(axis) for axis in "abls")
        self.is_up = self.a < self.na - 1
        self.is_down = self.a > 0

    def at(self, a=None, b=None, l=None, s=None):
        return tuple(
            own if other is None else other
            for own, other in zip((self.a, self.b, self.l, self.s), (a, b, l, s))
        )

    def other(self, axis, step):
        size, own = {"b": (self.nb, self.b), "l": (self.nl, self.l), "s": (self.ns, self.s)}[axis]
        return lax.rem(own + step, size)

    def to(self, axis, step):
        return self.at(**{axis: self.other(axis, step)})

    def hello(self, device):
        pl.semaphore_signal(
            pltpu.get_barrier_semaphore(), inc=1, device_id=device, device_id_type=MESH
        )

    def greet_neighbours(self, siblings):
        @pl.when(self.is_down)
        def _():
            self.hello(self.at(a=self.a - 1))

        @pl.when(self.is_up)
        def _():
            self.hello(self.at(a=self.a + 1))

        count = 0
        for axis, size in (("b", self.nb), ("l", self.nl), ("s", self.ns if siblings else 1)):
            for step in range(1, size):
                self.hello(self.to(axis, step))
                count += 1
        above = 1 - (self.a + 1) // self.na
        below = (self.a + self.na - 1) // self.na
        pl.semaphore_wait(pltpu.get_barrier_semaphore(), count + above + below)

    def greet_plane(self, siblings):
        count = 0
        for index in self.plane_steps():
            self.hello(self.plane_at(index))
            count += 1
        for step in range(1, self.ns if siblings else 1):
            self.hello(self.to("s", step))
            count += 1
        pl.semaphore_wait(pltpu.get_barrier_semaphore(), count)

    def plane_steps(self):
        return [
            (i, j, k)
            for i in range(self.na)
            for j in range(self.nb)
            for k in range(self.nl)
            if i + j + k
        ]

    def plane_at(self, steps, sign=1):
        return self.at(
            a=lax.rem(self.a + sign * steps[0] + self.na, self.na),
            b=lax.rem(self.b + sign * steps[1] + self.nb, self.nb),
            l=lax.rem(self.l + sign * steps[2] + self.nl, self.nl),
        )


def remote(src, dst, sems, device):
    return pltpu.make_async_remote_copy(
        src_ref=src, dst_ref=dst, send_sem=sems[0], recv_sem=sems[1], device_id=device, device_id_type=MESH
    )


def came(g, sem, dst):
    remote(dst, dst, (sem, sem), g.at()).wait_recv()


def left(g, sem, src):
    remote(src, src, (sem, sem), g.at()).wait_send()


class Bounce:
    def __init__(self, src, via, dst, sems):
        self.there = pltpu.make_async_copy(src, via, sems.at[0])
        self.back = pltpu.make_async_copy(via, dst, sems.at[1])

    def start(self):
        self.there.start()

    def turn(self):
        self.there.wait()
        self.back.start()

    def wait(self):
        self.back.wait()


def split_of(wide):
    return (wide * 5 // 7) // 128 * 128


def gather_scratch(sizes, siblings, x):
    na, nb, nl, ns = sizes
    return [
        DMA((2, 2, na)),
        DMA((2, 2, na)),
        DMA((2, nb - 1, na)),
        DMA((2, nl - 1, na)),
        DMA((2, nl - 1, nb - 1, na)),
        DMA((2, nb - 1, nl - 1)),
        DMA((2, ns, na)) if siblings else DMA((2, 1, 1)),
        DMA((2,)),
        pltpu.VMEM(x.shape, x.dtype),
    ]


def gathering(g, siblings, x_ref, o_ref, sems):
    la_sem, lb_sem, b_sem, l_sem, lb2_sem, bl2_sem, s_sem, own_sem, own_buf = sems
    na, nb, nl, ns = g.sizes
    wide = x_ref.shape[-1]
    cut = split_of(wide)
    head, tail = pl.ds(0, cut), pl.ds(cut, wide - cut)
    me = g.s if siblings else 0

    def slot(a, b, l):
        return o_ref.at[a, b, l, me]

    def square(a):
        return o_ref.at[a, :, :, me]

    def pair(sem, *index):
        return sem.at[(0, *index)], sem.at[(1, *index)]

    def cols(origin):
        return (slice(None), head)

    def line_head(way, origin, first=False):
        src = x_ref.at[:, head] if first else slot(origin, g.b, g.l).at[:, head]
        return remote(src, slot(origin, g.b, g.l).at[:, head], pair(la_sem, way, origin), g.at(a=g.a + 1 - 2 * way))

    def line_tail(way, origin):
        block = o_ref.at[origin, :, :, me, :, tail]
        return remote(block, block, pair(lb_sem, way, origin), g.at(a=g.a + 1 - 2 * way))

    def spread(origin, first=False):
        for step in range(1, nl):
            if first:
                remote(x_ref, slot(origin, g.b, g.l), pair(l_sem, step - 1, origin), g.to("l", step)).start()
            else:
                part = slot(origin, g.b, g.l).at[:, head]
                remote(part, part, pair(l_sem, step - 1, origin), g.to("l", step)).start()
        for step in range(1, nb):
            if first:
                remote(x_ref, slot(origin, g.b, g.l), pair(b_sem, step - 1, origin), g.to("b", step)).start()
            else:
                part = slot(origin, g.b, g.l).at[:, head]
                remote(part, part, pair(b_sem, step - 1, origin), g.to("b", step)).start()

    def l_came(step, origin, first=False):
        l_from = g.other("l", nl - step)
        ref = slot(origin, g.b, l_from)
        came(g, l_sem.at[1, step - 1, origin], ref if first else ref.at[:, head])
        return l_from

    def b_came(step, origin, first=False):
        b_from = g.other("b", nb - step)
        ref = slot(origin, b_from, g.l)
        came(g, b_sem.at[1, step - 1, origin], ref if first else ref.at[:, head])
        return b_from

    def relay_head(origin, first=False):
        for step in range(1, nl):
            l_from = l_came(step, origin, first)
            part = slot(origin, g.b, l_from).at[:, head]
            for turn in range(1, nb):
                remote(part, part, pair(lb2_sem, step - 1, turn - 1, origin), g.to("b", turn)).start()

    def relay_tail():
        for step in range(1, nb):
            b_from = b_came(step, g.a, True)
            part = slot(g.a, b_from, g.l).at[:, tail]
            for turn in range(1, nl):
                remote(part, part, pair(bl2_sem, step - 1, turn - 1), g.to("l", turn)).start()

    def diagonal_head(origin):
        for step in range(1, nl):
            for turn in range(1, nb):
                ref = slot(origin, g.other("b", nb - turn), g.other("l", nl - step))
                came(g, lb2_sem.at[1, step - 1, turn - 1, origin], ref.at[:, head])

    def diagonal_tail():
        for step in range(1, nb):
            for turn in range(1, nl):
                ref = slot(g.a, g.other("b", nb - step), g.other("l", nl - turn))
                came(g, bl2_sem.at[1, step - 1, turn - 1], ref.at[:, tail])

    def siblings_send(origin):
        if siblings:
            for step in range(1, ns):
                remote(square(origin), square(origin), pair(s_sem, step - 1, origin), g.to("s", step)).start()

    def when_up_origin(k, act):
        @pl.when(g.a - k >= 0)
        def _():
            act(0, g.a - k)

    def when_down_origin(k, act):
        @pl.when(g.a + k < na)
        def _():
            act(1, g.a + k)

    def both(k, act):
        when_up_origin(k, act)
        when_down_origin(k, act)

    def onward(way, copy):
        @pl.when(g.is_up if way == 0 else g.is_down)
        def _():
            copy.start()

    def head_arrives(way, origin):
        came(g, la_sem.at[1, way, origin], slot(origin, g.b, g.l).at[:, head])
        onward(way, line_head(way, origin))
        spread(origin)

    def tail_arrives(way, origin):
        came(g, lb_sem.at[1, way, origin], o_ref.at[origin, :, :, me, :, tail])
        onward(way, line_tail(way, origin))

    own = Bounce(x_ref, own_buf, slot(g.a, g.b, g.l), own_sem)
    own.start()
    onward(0, line_head(0, g.a, True))
    onward(1, line_head(1, g.a, True))
    spread(g.a, True)
    yield
    own.turn()
    relay_head(g.a, True)
    relay_tail()
    yield
    both(1, head_arrives)
    diagonal_tail()
    own.wait()
    onward(0, line_tail(0, g.a))
    onward(1, line_tail(1, g.a))
    yield
    for k in range(1, na):
        both(k, lambda way, origin: relay_head(origin))
        if k + 1 < na:
            both(k + 1, head_arrives)
        both(k, tail_arrives)
        if k == 1:
            diagonal_head(g.a)
            siblings_send(g.a)
        yield

    def complete(way, origin):
        for step in range(1, nb):
            b_came(step, origin)
        diagonal_head(origin)
        siblings_send(origin)

    for k in range(1, na):
        both(k, complete)
    yield

    def sent_line(way, origin):
        @pl.when(g.is_up if way == 0 else g.is_down)
        def _():
            line_head(way, origin).wait_send()
            line_tail(way, origin).wait_send()

    when_up_origin(0, sent_line)
    when_down_origin(0, sent_line)
    for k in range(1, na):
        both(k, sent_line)

    def sent(way, origin, first=False):
        whole = slot(origin, g.b, g.l)
        for step in range(1, nl):
            left(g, l_sem.at[0, step - 1, origin], whole if first else whole.at[:, head])
            for turn in range(1, nb):
                left(g, lb2_sem.at[0, step - 1, turn - 1, origin], whole.at[:, head])
        for step in range(1, nb):
            left(g, b_sem.at[0, step - 1, origin], whole if first else whole.at[:, head])
        if siblings:
            for step in range(1, ns):
                left(g, s_sem.at[0, step - 1, origin], square(origin))
                came(g, s_sem.at[1, step - 1, origin], o_ref.at[origin, :, :, g.other("s", ns - step)])

    sent(0, g.a, True)
    for step in range(1, nb):
        for turn in range(1, nl):
            left(g, bl2_sem.at[0, step - 1, turn - 1], slot(g.a, g.b, g.l).at[:, tail])
    for k in range(1, na):
        both(k, sent)


def after(count, program):
    for _ in range(count):
        yield
    yield from program


def run_steps(*programs):
    alive = list(programs)
    while alive:
        for program in list(alive):
            try:
                next(program)
            except StopIteration:
                alive.remove(program)


def gather_kernel(sizes, x_ref, shard, o_ref, whole, *sems):
    g = Grid(sizes)
    g.greet_neighbours(True)
    run_steps(
        gathering(g, False, x_ref, o_ref, sems[:9]),
        matrix_steps(g, (shard,), (whole,), sems[9:], (0, 0, 0, 2, 2)),
    )


def gather(x, shard, sizes, collective_id):
    na, nb, nl, ns = sizes
    rows, wide = x.shape
    out, whole = pl.pallas_call(
        functools.partial(gather_kernel, sizes),
        out_shape=[jax.ShapeDtypeStruct((na, nb, nl, 1, rows, wide), x.dtype), matrix_shape(shard, sizes)],
        in_specs=[ANY] * 2,
        out_specs=[ANY] * 2,
        scratch_shapes=gather_scratch(sizes, False, x) + matrix_scratch(sizes, shard),
        compiler_params=pltpu.CompilerParams(collective_id=collective_id, has_side_effects=True, vmem_limit_bytes=VMEM_LIMIT),
    )(x, shard)
    return out.reshape(-1, wide), whole.reshape(-1, shard.shape[2])


CHUNKS = 4


def matrix_scratch(sizes, *shards):
    na, nb, nl, ns = sizes
    count = len(shards)
    return [
        DMA((2, count, nl - 1, CHUNKS)),
        DMA((2, count, nl, ns - 1, CHUNKS)),
        DMA((count, 2)),
        pltpu.VMEM((count, *shards[0].shape[1:]), BF16),
    ]


def matrix_steps(g, shards, wholes, sems, paces):
    e_sem, es_sem, own_sem, own_buf = sems
    na, nb, nl, ns = g.sizes
    count = len(shards)
    rows = shards[0].shape[1] // CHUNKS
    chunks = [(i, pl.ds(c * rows, rows), c) for i in range(count) for c in range(CHUNKS)]

    def across(i, at, c, step):
        to = g.other("l", step)
        return remote(shards[i].at[to, at], wholes[i].at[g.l, g.s, at], (e_sem.at[0, i, step - 1, c], e_sem.at[1, i, step - 1, c]), g.at(l=to))

    def aside(i, at, c, turn, step):
        l_from = g.other("l", nl - turn) if turn else g.l
        src = wholes[i].at[l_from, g.s, at] if turn else shards[i].at[g.l, at]
        return remote(src, wholes[i].at[l_from, g.s, at], (es_sem.at[0, i, turn, step - 1, c], es_sem.at[1, i, turn, step - 1, c]), g.to("s", step))

    def aside_came(i, at, c, turn, step):
        l_from = g.other("l", nl - turn) if turn else g.l
        came(g, es_sem.at[1, i, turn, step - 1, c], wholes[i].at[l_from, g.other("s", ns - step), at])

    owns = [Bounce(shards[i].at[g.l], own_buf.at[i], wholes[i].at[g.l, g.s], own_sem.at[i]) for i in range(count)]
    for copy in owns:
        copy.start()
    rest = list(chunks)
    for j, pace in enumerate(paces):
        for chunk in rest[:pace]:
            for step in range(1, nl):
                across(*chunk, step).start()
            for step in range(1, ns):
                aside(*chunk, 0, step).start()
        rest = rest[pace:]
        if j == 2:
            for copy in owns:
                copy.turn()
        yield
    for chunk in chunks:
        i, at, c = chunk
        for turn in range(1, nl):
            came(g, e_sem.at[1, i, turn - 1, c], wholes[i].at[g.other("l", nl - turn), g.s, at])
            for step in range(1, ns):
                aside(*chunk, turn, step).start()
    yield
    for copy in owns:
        copy.wait()
    for chunk in chunks:
        for step in range(1, nl):
            across(*chunk, step).wait_send()
        for turn in range(nl):
            for step in range(1, ns):
                aside(*chunk, turn, step).wait_send()
                aside_came(*chunk, turn, step)


def matrix_shape(shard, sizes):
    ranks, rows, ffe = shard.shape
    return jax.ShapeDtypeStruct((ranks, sizes[3], rows, ffe), BF16)


def column_steps(g, shared, columns, down, downs, sems):
    c_sem, cs_sem, d_sem, own_sem, own_buf, down_buf = sems
    ns = g.ns
    steps = g.plane_steps()

    def block(n, at):
        a, b, l, _ = g.plane_at(at)
        return remote(shared.at[a, b, l], columns.at[:, g.a, g.b, g.l, g.s], (c_sem.at[0, n], c_sem.at[1, n]), g.plane_at(at))

    def downward(step):
        return remote(down, downs.at[g.s], (d_sem.at[0, step - 1], d_sem.at[1, step - 1]), g.to("s", step))

    def columns_aside(step):
        part = columns.at[:, :, :, :, g.s]
        return remote(part, part, (cs_sem.at[0, step - 1], cs_sem.at[1, step - 1]), g.to("s", step))

    owns = [
        Bounce(shared.at[g.a, g.b, g.l], own_buf, columns.at[:, g.a, g.b, g.l, g.s], own_sem.at[0]),
        Bounce(down, down_buf, downs.at[g.s], own_sem.at[1]),
    ]
    yield
    for copy in owns:
        copy.start()
    for step in range(1, ns):
        downward(step).start()
    yield
    for n, at in enumerate(steps):
        block(n, at).start()
    for copy in owns:
        copy.turn()
    yield
    for copy in owns:
        copy.wait()
    yield
    for n, at in enumerate(steps):
        a, b, l, _ = g.plane_at(at, -1)
        came(g, c_sem.at[1, n], columns.at[:, a, b, l, g.s])
    for step in range(1, ns):
        columns_aside(step).start()
    yield
    for n, at in enumerate(steps):
        block(n, at).wait_send()
    for step in range(1, ns):
        downward(step).wait_send()
        came(g, d_sem.at[1, step - 1], downs.at[g.other("s", ns - step)])
        columns_aside(step).wait_send()
        came(g, cs_sem.at[1, step - 1], columns.at[:, :, :, :, g.other("s", ns - step)])


def inputs_kernel(sizes, dense, wide_dy, gate, up, shared, sh_down, dense_o, dy_o, gate_o, up_o, columns_o, downs_o, *sems):
    g = Grid(sizes)
    g.greet_plane(True)
    run_steps(
        gathering(g, True, dense, dense_o, sems[:9]),
        after(2, gathering(g, False, wide_dy, dy_o, sems[9:18])),
        matrix_steps(g, (gate, up), (gate_o, up_o), sems[18:22], (0, 0, 0, 2, 2, 2, 2)),
        after(2, column_steps(g, shared, columns_o, sh_down, downs_o, sems[22:])),
    )


def inputs_gather(dense, wide_dy, gate, up, shared, sh_down, sizes, collective_id):
    na, nb, nl, ns = sizes
    two, sh_rows, narrow = shared.shape[3:]
    shape = jax.ShapeDtypeStruct
    dense_o, dy_o, gate_o, up_o, columns, downs = pl.pallas_call(
        functools.partial(inputs_kernel, sizes),
        out_shape=[
            shape((na, nb, nl, ns, *dense.shape), BF16),
            shape((na, nb, nl, 1, *wide_dy.shape), BF16),
            matrix_shape(gate, sizes),
            matrix_shape(up, sizes),
            shape((two, na, nb, nl, ns, sh_rows, narrow), BF16),
            shape((ns, *sh_down.shape), BF16),
        ],
        in_specs=[ANY] * 6,
        out_specs=[ANY] * 6,
        scratch_shapes=gather_scratch(sizes, True, dense)
        + gather_scratch(sizes, False, wide_dy)
        + matrix_scratch(sizes, gate, up)
        + [
            DMA((2, na * nb * nl - 1)),
            DMA((2, ns - 1)),
            DMA((2, ns - 1)),
            DMA((2, 2)),
            pltpu.VMEM((two, sh_rows, narrow), BF16),
            pltpu.VMEM(sh_down.shape, BF16),
        ],
        compiler_params=pltpu.CompilerParams(collective_id=collective_id, has_side_effects=True, vmem_limit_bytes=VMEM_LIMIT),
    )(dense, wide_dy, gate, up, shared, sh_down)
    return (
        dense_o.reshape(-1, dense.shape[1]),
        dy_o.reshape(-1, wide_dy.shape[1]),
        gate_o.reshape(-1, gate.shape[2]),
        up_o.reshape(-1, up.shape[2]),
        columns.reshape(two, -1, narrow),
        downs,
    )


def order(a, k):
    high, odd = a // 2, lax.rem(a, 2)
    return (3 * (1 - high), 2 + high - 2 * odd, 1 + odd, a)[k]


def add_rows(out, *terms):
    rows = out.shape[0]
    step = min(rows, 32)

    @pl.loop(0, rows, step=step)
    def _(r):
        at = pl.ds(pl.multiple_of(r, step), step)
        total = terms[0][at, :].astype(F32)
        for term in terms[1:]:
            total = total + term[at, :].astype(F32)
        out[at, :] = total.astype(out.dtype)


def scatter_scratch(sizes, siblings, rows, wide):
    na, nb, nl, ns = sizes
    head = split_of(wide)
    tail = wide - head
    shapes = [
        (nb - 1, na, nl, rows, head),
        (nl - 1, na, rows, head),
        (na, rows, head),
        (na + 1, rows, head),
        (na + 1, nb, nl, rows, tail),
        (nb, nl, rows, tail),
        (nl - 1, nb, rows, tail),
        (nb - 1, rows, tail),
        (ns - 1, na, nb, nl, rows, wide) if siblings else (16, 128),
    ]
    sems = [(2, nb - 1, na), (2, nl - 1, na), (2, 2, na), (2, 2, na), (2, nl - 1), (2, nb - 1), (2, ns - 1, na)]
    return [pltpu.VMEM(s, BF16) for s in shapes] + [DMA(s) for s in sems]


def scattering(g, siblings, p_ref, o_ref, scratch, prepare=None):
    one, two, total, line_a, line_b, tail_sum, tail_two, tail_three, s_buf = scratch[:9]
    b_sem, l_sem, la_sem, lb_sem, l2_sem, b2_sem, s_sem = scratch[9:]
    na, nb, nl, ns = g.sizes
    wide = o_ref.shape[-1]
    cut = split_of(wide)
    head, tail = pl.ds(0, cut), pl.ds(cut, wide - cut)

    def pair(sem, *index):
        return sem.at[(0, *index)], sem.at[(1, *index)]

    def block(k):
        return s_buf.at[0, k] if siblings else p_ref.at[order(g.a, k), :, :, 0]

    def sibling_copy(k, step):
        to = g.other("s", step)
        return remote(p_ref.at[order(g.a, k), :, :, to], s_buf.at[step - 1, k], pair(s_sem, step - 1, k), g.at(s=to))

    def b_copy(k, step):
        to = g.other("b", step)
        return remote(block(k).at[to, :, :, head], one.at[step - 1, k], pair(b_sem, step - 1, k), g.at(b=to))

    def l_copy(k, step):
        to = g.other("l", step)
        return remote(one.at[0, k, to], two.at[step - 1, k], pair(l_sem, step - 1, k), g.at(l=to))

    def place(way, dest, at):
        if way == 0:
            return dest
        far = (at - dest + na - 1) // na
        return dest * far + na * (1 - far)

    def head_copy(way, k):
        dest, to = order(g.a, k), g.a + 1 - 2 * way
        return remote(total.at[k], line_a.at[place(way, dest, to)], pair(la_sem, way, dest), g.at(a=to))

    def tail_copy(way, k, first):
        dest, to = order(g.a, k), g.a + 1 - 2 * way
        src = block(k).at[:, :, :, tail] if first else line_b.at[dest]
        return remote(src, line_b.at[place(way, dest, to)], pair(lb_sem, way, dest), g.at(a=to))

    def starts(k, act):
        if k == na - 1:
            return
        dest = order(g.a, k)

        @pl.when((g.a == 0) & (dest > g.a))
        def _():
            act(0)

        @pl.when((g.a == na - 1) & (dest < g.a))
        def _():
            act(1)

    def passes(k, act):
        if k == na - 1:
            return
        dest = order(g.a, k)

        @pl.when((g.a > 0) & (dest > g.a))
        def _():
            act(0)

        @pl.when((g.a < na - 1) & (dest < g.a))
        def _():
            act(1)

    def arrivals(act):
        mine = place(0, g.a, g.a)

        @pl.when(g.a == 0)
        def _():
            act((1,), (na,))

        @pl.when(g.a == na - 1)
        def _():
            act((0,), (mine,))

        @pl.when((g.a > 0) & (g.a < na - 1))
        def _():
            act((0, 1), (mine, na))

    def begin(k):
        if k >= na:
            return
        if siblings:
            for step in range(1, ns):
                came(g, s_sem.at[1, step - 1, k], s_buf.at[step - 1, k])
            for b in range(nb):
                for l in range(nl):
                    add_rows(s_buf.at[0, k, b, l], p_ref.at[order(g.a, k), b, l, g.s], *[s_buf.at[step, k, b, l] for step in range(ns - 1)])
        for step in range(1, nb):
            b_copy(k, step).start()
        starts(k, lambda way: tail_copy(way, k, True).start())

    def second(k):
        for step in range(1, nb):
            came(g, b_sem.at[1, step - 1, k], one.at[step - 1, k])
        for turn in range(nl):
            l = g.other("l", turn)
            add_rows(one.at[0, k, l], block(k).at[g.b, l, :, head], *[one.at[step, k, l] for step in range(nb - 1)])
            if turn:
                l_copy(k, turn).start()

    def third(k):
        for step in range(1, nl):
            came(g, l_sem.at[1, step - 1, k], two.at[step - 1, k])
        add_rows(total.at[k], one.at[0, k, g.l], *[two.at[step, k] for step in range(nl - 1)])
        starts(k, lambda way: head_copy(way, k).start())

    def pass_head(k):
        def act(way):
            dest = order(g.a, k)
            came(g, la_sem.at[1, way, dest], line_a.at[dest])
            add_rows(total.at[k], total.at[k], line_a.at[dest])
            head_copy(way, k).start()

        passes(k, act)

    def pass_tail(k):
        def act(way):
            dest = order(g.a, k)
            came(g, lb_sem.at[1, way, dest], line_b.at[dest])
            for b in range(nb):
                for l in range(nl):
                    add_rows(line_b.at[dest, b, l], line_b.at[dest, b, l], block(k).at[b, l, :, tail])
            tail_copy(way, k, False).start()

        passes(k, act)

    def tail_here():
        def act(ways, slots):
            for way, slot in zip(ways, slots):
                came(g, lb_sem.at[1, way, g.a], line_b.at[slot])
            for b in range(nb):
                for l in range(nl):
                    add_rows(tail_sum.at[b, l], block(na - 1).at[b, l, :, tail], *[line_b.at[slot, b, l] for slot in slots])

        arrivals(act)
        for step in range(1, nl):
            tail_l(step).start()

    def tail_l(step):
        to = g.other("l", step)
        return remote(tail_sum.at[:, to], tail_two.at[step - 1], pair(l2_sem, step - 1), g.at(l=to))

    def tail_b(step):
        to = g.other("b", step)
        return remote(tail_two.at[0, to], tail_three.at[step - 1], pair(b2_sem, step - 1), g.at(b=to))

    def ahead(k):
        if siblings and k < na:
            prepare(order(g.a, k))
            for step in range(1, ns):
                sibling_copy(k, step).start()

    ahead(0)
    ahead(1)
    begin(0)
    ahead(2)
    begin(1)
    yield
    for k in range(na):
        ahead(k + 3)
        second(k)
        begin(k + 2)
        if k >= 1:
            third(k - 1)
            pass_tail(k - 1)
        if k >= 2:
            pass_head(k - 2)
        yield
    third(na - 1)
    pass_head(na - 2)
    tail_here()
    yield

    def head_here(ways, slots):
        for way, slot in zip(ways, slots):
            came(g, la_sem.at[1, way, g.a], line_a.at[slot])
        add_rows(o_ref.at[:, head], total.at[na - 1], *[line_a.at[slot] for slot in slots])

    for step in range(1, nl):
        came(g, l2_sem.at[1, step - 1], tail_two.at[step - 1])
    for b in range(nb):
        add_rows(tail_two.at[0, b], tail_sum.at[b, g.l], *[tail_two.at[step, b] for step in range(nl - 1)])
    for step in range(1, nb):
        tail_b(step).start()
    arrivals(head_here)
    yield
    for step in range(1, nb):
        came(g, b2_sem.at[1, step - 1], tail_three.at[step - 1])
    add_rows(o_ref.at[:, tail], tail_two.at[0, g.b], *[tail_three.at[step] for step in range(nb - 1)])

    for k in range(na):
        if siblings:
            for step in range(1, ns):
                sibling_copy(k, step).wait_send()
        for step in range(1, nb):
            b_copy(k, step).wait_send()
        for step in range(1, nl):
            l_copy(k, step).wait_send()

        def sent(way, first):
            tail_copy(way, k, first).wait_send()
            head_copy(way, k).wait_send()

        starts(k, lambda way: sent(way, True))
        passes(k, lambda way: sent(way, False))
    for step in range(1, nl):
        tail_l(step).wait_send()
    for step in range(1, nb):
        tail_b(step).wait_send()


def scatter_kernel(sizes, p_ref, o_ref, *scratch):
    g = Grid(sizes)
    g.greet_neighbours(False)
    run_steps(scattering(g, False, p_ref, o_ref, scratch))


def scatter_shapes(partial, sizes):
    na, nb, nl, ns = sizes
    rows, wide = partial.shape[0] // (na * nb * nl), partial.shape[1]
    return partial.reshape(na, nb, nl, 1, rows, wide), jax.ShapeDtypeStruct((rows, wide), F32)


def scatter(partial, sizes, collective_id):
    split, out = scatter_shapes(partial, sizes)
    return pl.pallas_call(
        functools.partial(scatter_kernel, sizes),
        out_shape=out,
        in_specs=[VMEM],
        out_specs=VMEM,
        scratch_shapes=scatter_scratch(sizes, False, *out.shape),
        compiler_params=pltpu.CompilerParams(collective_id=collective_id, has_side_effects=True, vmem_limit_bytes=VMEM_LIMIT),
    )(split)


def fits(partial):
    return partial.size <= 2048 * 2048


def each_tile(wide, tile, body):
    @pl.loop(0, wide // tile)
    def _(i):
        body(pl.ds(pl.multiple_of(i * tile, tile), tile))


def back_steps(dg, du, wg, wu, sgu, dsgu, back_ref, dx_o, scratch):
    *bufs, row_buf, stage, load_sem, out_sem = scratch
    dg_v, du_v, wg_v, wu_v, sgu_v, dsgu_v = bufs
    steps, toks, slots = back_ref.shape
    width = wg.shape[0]
    loads = [
        pltpu.make_async_copy(src, dst, load_sem.at[i])
        for i, (src, dst) in enumerate(zip((dg, du, wg, wu, sgu, dsgu), bufs))
    ]
    for load in loads:
        load.start()
    yield
    for load in loads:
        load.wait()

    def out_copy(t):
        return pltpu.make_async_copy(stage.at[t % 2], dx_o.at[pl.ds(t * toks, toks)], out_sem.at[t % 2])

    for t in range(steps):
        mine, theirs = pl.ds(t * slots, slots), pl.ds(t * toks, toks)

        @functools.partial(each_tile, width, 512)
        def _(cols):
            rows = dot_nt(dg_v[mine, :], wg_v[cols, :]) + dot_nt(du_v[mine, :], wu_v[cols, :])
            row_buf[:, cols] = rows.astype(BF16)

        yield
        if t >= 2:
            out_copy(t - 2).wait()

        @functools.partial(each_tile, width, 512)
        def _(cols):
            total = dot(back_ref[t], row_buf[:, cols]) + dot_nt(dsgu_v[theirs, :], sgu_v[cols, :])
            stage[t % 2, :, cols] = total.astype(BF16)

        out_copy(t).start()
        yield
    for t in range(max(steps - 2, 0), steps):
        out_copy(t).wait()


def back_kernel(sizes, scattered, *refs):
    ins, refs = refs[: 7 + scattered], refs[7 + scattered :]
    outs, scratch = refs[: 1 + scattered], refs[1 + scattered :]
    programs = [back_steps(*ins[:7], outs[0], scratch[:10])]
    if scattered:
        g = Grid(sizes)
        g.greet_neighbours(False)
        programs.insert(0, scattering(g, False, ins[7], outs[1], scratch[10:]))
    run_steps(*programs)


def back_rows(dg, du, wg, wu, sgu, dsgu, back, partial, sizes, first_id):
    steps, toks, slots = back.shape
    width, ffe = wg.shape
    together = fits(partial)
    split, total = scatter_shapes(partial, sizes)
    params = {"collective_id": first_id, "has_side_effects": True} if together else {}
    sources = (dg, du, wg, wu, sgu, dsgu)
    out = pl.pallas_call(
        functools.partial(back_kernel, sizes, int(together)),
        out_shape=[jax.ShapeDtypeStruct((steps * toks, width), BF16)] + [total] * together,
        in_specs=[ANY] * 6 + [VMEM] + [VMEM] * together,
        out_specs=[ANY] + [VMEM] * together,
        scratch_shapes=[pltpu.VMEM(source.shape, BF16) for source in sources]
        + [pltpu.VMEM((slots, width), BF16), pltpu.VMEM((2, toks, width), BF16), DMA((6,)), DMA((2,))]
        + (scatter_scratch(sizes, False, *total.shape) if together else []),
        compiler_params=pltpu.CompilerParams(vmem_limit_bytes=VMEM_LIMIT, **params),
    )(*sources, back, *([split] if together else []))
    return out if together else (out[0], scatter(partial, sizes, first_id))


def shared_steps(g, part, blocks, own, other, sems):
    s_sem, c_sem, own_sem = sems
    na, nb, nl, ns = g.sizes
    steps = g.plane_steps()

    def aside(step):
        to = g.other("s", step)
        return remote(part.at[:, :, :, to], other.at[step - 1], (s_sem.at[0, step - 1], s_sem.at[1, step - 1]), g.at(s=to))

    def send(n, at):
        a, b, l, _ = g.plane_at(at)
        return remote(other.at[0, a, b, l], blocks.at[g.a, g.b, g.l], (c_sem.at[0, n], c_sem.at[1, n]), g.plane_at(at))

    mine = pltpu.make_async_copy(part.at[:, :, :, g.s], own, own_sem.at[0])
    mine.start()
    for step in range(1, ns):
        aside(step).start()
    yield
    mine.wait()
    for step in range(1, ns):
        came(g, s_sem.at[1, step - 1], other.at[step - 1])
    for a in range(na):
        for b in range(nb):
            for l in range(nl):
                add_rows(other.at[0, a, b, l], own.at[a, b, l], *[other.at[step, a, b, l] for step in range(ns - 1)])
    for n, at in enumerate(steps):
        send(n, at).start()
    here = pltpu.make_async_copy(other.at[0, g.a, g.b, g.l], blocks.at[g.a, g.b, g.l], own_sem.at[1])
    here.start()
    yield
    yield
    yield
    yield
    here.wait()
    for n, at in enumerate(steps):
        a, b, l, _ = g.plane_at(at, -1)
        came(g, c_sem.at[1, n], blocks.at[a, b, l])
        send(n, at).wait_send()
    for step in range(1, ns):
        aside(step).wait_send()


def across_steps(g, blocks, outs, sem):
    def send(step):
        return remote(blocks.at[step - 1], outs.at[step - 1], (sem.at[0, step - 1], sem.at[1, step - 1]), g.to("l", step))

    for step in range(1, g.nl):
        send(step).start()
    yield
    for step in range(1, g.nl):
        send(step).wait()


def outputs_kernel(sizes, normed, grads, mixed, gh, small, shared_ref, cross_ref, o_ref, blocks_ref, cross_o, p_buf, own, other, *scratch):
    g = Grid(sizes)
    na, nb, nl, ns = sizes
    g.greet_plane(True)
    rows = p_buf.shape[4]
    chunk = nb * nl * ns * rows
    left = grads.shape[1]

    def prepare(a):
        at = pl.ds(pl.multiple_of(a * chunk, chunk), chunk)

        def store(value, cols):
            value = value.astype(BF16)
            for n in range(nb * nl * ns):
                b, l, s = n // (nl * ns), n // ns % nl, n % ns
                p_buf[a, b, l, s, :, cols] = value[n * rows : (n + 1) * rows]

        for base, one, two in ((0, normed, grads), (left, mixed, gh)):
            tile = 512
            @pl.loop(0, two.shape[1], step=tile)
            def _(c):
                c = pl.multiple_of(c, tile)
                store(dot_tn(one[:, at], two[:, pl.ds(c, tile)]), pl.ds(pl.multiple_of(base + c, 128), tile))
        store(small[at, :], pl.ds(left + gh.shape[1], small.shape[1]))

    run_steps(
        scattering(g, True, p_buf, o_ref, scratch[4:], prepare),
        shared_steps(g, shared_ref, blocks_ref, own, other, scratch[:3]),
        across_steps(g, cross_ref, cross_o, scratch[3]),
    )


def outputs_scatter(normed, grads, mixed, gh, small, shared, cross, sizes, collective_id):
    na, nb, nl, ns = sizes
    rows = normed.shape[1] // (na * nb * nl * ns)
    wide = grads.shape[1] + gh.shape[1] + small.shape[1]
    shared = shared.reshape(na, nb, nl, ns, -1, shared.shape[1])
    shape = jax.ShapeDtypeStruct
    return pl.pallas_call(
        functools.partial(outputs_kernel, sizes),
        out_shape=[
            shape((rows, wide), F32),
            shape((na, nb, nl, *shared.shape[4:]), BF16),
            shape(cross.shape, BF16),
        ],
        in_specs=[VMEM] * 5 + [ANY] * 2,
        out_specs=[VMEM] + [ANY] * 2,
        scratch_shapes=[
            pltpu.VMEM((na, nb, nl, ns, rows, wide), BF16),
            pltpu.VMEM((na, nb, nl, *shared.shape[4:]), BF16),
            pltpu.VMEM((ns - 1, na, nb, nl, *shared.shape[4:]), BF16),
            DMA((2, ns - 1)),
            DMA((2, na * nb * nl - 1)),
            DMA((2,)),
            DMA((2, nl - 1)),
        ]
        + scatter_scratch(sizes, True, rows, wide),
        compiler_params=pltpu.CompilerParams(collective_id=collective_id, has_side_effects=True, vmem_limit_bytes=VMEM_LIMIT),
    )(normed, grads, mixed, gh, small, shared, cross)


def weight_steps(g, gp, inner, xr, dg, du, own_os, cross_os, scratch):
    left_buf, right_buf, send, recv, own_buf, cross_buf, load_sem, s_sem, c_sem = scratch
    na, nb, nl, ns = g.sizes
    rows, ffe = own_buf.shape
    lefts, rights = (xr, xr, gp), (dg, du, inner)

    def load_left(i):
        return pltpu.make_async_copy(lefts[i], left_buf, load_sem.at[0])

    def load_right(i):
        return pltpu.make_async_copy(rights[i], right_buf.at[i % 2], load_sem.at[1 + i % 2])

    def product(i, l, s, out):
        at = (l * ns + s) * rows
        step = 256

        @pl.loop(0, rows, step=step)
        def _(r):
            cols = pl.ds(pl.multiple_of(at + r, step), step)
            for to, tile in column_tiles(ffe, 512):
                value = dot_tn(left_buf[:, cols], right_buf[i % 2, :, pl.ds(to, tile)])
                out[pl.ds(pl.multiple_of(r, step), step), pl.ds(to, tile)] = value.astype(out.dtype)

    def aside(i, turn, step):
        return remote(send.at[turn, step - 1], recv.at[i, turn, step - 1], (s_sem.at[0, i, turn, step - 1], s_sem.at[1, i, turn, step - 1]), g.to("s", step))

    def keep(i):
        return [pltpu.make_async_copy(own_buf, own_os[i], c_sem.at[i, 0])] + [
            pltpu.make_async_copy(cross_buf.at[turn - 1], cross_os[i].at[turn - 1], c_sem.at[i, turn])
            for turn in range(1, nl)
        ]

    def sums(i):
        for turn in range(nl):
            out = cross_buf.at[turn - 1] if turn else own_buf
            for step in range(1, ns):
                came(g, s_sem.at[1, i, turn, step - 1], recv.at[i, turn, step - 1])
            add_rows(out, out, *[recv.at[i, turn, step] for step in range(ns - 1)])
        for copy in keep(i):
            copy.start()

    def kept(i):
        for copy in keep(i):
            copy.wait()

    load_left(0).start()
    load_right(0).start()
    load_right(1).start()
    yield
    load_left(0).wait()
    for i in range(3):
        load_right(i).wait()
        if i == 2:
            load_left(2).wait()
        for turn in range(nl):
            for step in range(1, ns):
                if i >= 1:
                    aside(i - 1, turn, step).wait_send()
                product(i, g.other("l", turn), g.other("s", step), send.at[turn, step - 1])
                aside(i, turn, step).start()
        yield
        if i >= 1:
            sums(i - 1)
            kept(i - 1)
        for turn in range(nl):
            product(i, g.other("l", turn), g.s, cross_buf.at[turn - 1] if turn else own_buf)
        if i == 0:
            load_right(2).start()
        if i == 1:
            load_left(2).start()
        yield
    sums(2)
    kept(2)
    yield
    for turn in range(nl):
        for step in range(1, ns):
            aside(2, turn, step).wait_send()


def weights_kernel(sizes, scattered, *refs):
    g = Grid(sizes)
    g.greet_neighbours(True)
    ins, refs = refs[: 5 + scattered], refs[5 + scattered :]
    outs, scratch = refs[: 6 + scattered], refs[6 + scattered :]
    programs = [weight_steps(g, *ins[:5], outs[:3], outs[3:6], scratch[:9])]
    if scattered:
        programs.insert(0, scattering(g, False, ins[5], outs[6], scratch[9:]))
    run_steps(*programs)


def expert_weights(gp, inner, xr, dg, du, partial, sizes, first_id, second_id):
    na, nb, nl, ns = sizes
    rows, ffe = gp.shape[1] // (nl * ns), inner.shape[1]
    together = fits(partial)
    split, total = scatter_shapes(partial, sizes)
    shape = jax.ShapeDtypeStruct
    out = pl.pallas_call(
        functools.partial(weights_kernel, sizes, int(together)),
        out_shape=[
            *[shape((rows, ffe), F32)] * 3,
            *[shape((nl - 1, rows, ffe), BF16)] * 3,
        ]
        + [total] * together,
        in_specs=[ANY] * 5 + [VMEM] * together,
        out_specs=[ANY] * 6 + [VMEM] * together,
        scratch_shapes=[
            pltpu.VMEM(gp.shape, BF16),
            pltpu.VMEM((2, *inner.shape), BF16),
            pltpu.VMEM((nl, ns - 1, rows, ffe), BF16),
            pltpu.VMEM((3, nl, ns - 1, rows, ffe), BF16),
            pltpu.VMEM((rows, ffe), F32),
            pltpu.VMEM((nl - 1, rows, ffe), BF16),
            DMA((3,)),
            DMA((2, 3, nl, ns - 1)),
            DMA((3, nl)),
        ]
        + (scatter_scratch(sizes, False, *total.shape) if together else []),
        compiler_params=pltpu.CompilerParams(collective_id=first_id, has_side_effects=True, vmem_limit_bytes=VMEM_LIMIT),
    )(gp, inner, xr, dg, du, *([split] if together else []))
    return out[:3], *out[3:6], out[6] if together else scatter(partial, sizes, second_id)


def rms_norm(values, gain_row):
    factor = lax.rsqrt(jnp.mean(values * values, axis=-1, keepdims=True) + EPS)
    return values * factor * gain_row


def rotate(values):
    length = values.shape[0]
    half_dim = values.shape[-1] // 2
    position = jnp.arange(length).astype(F32)
    inverse = ROPE_BASE ** (-jnp.arange(half_dim).astype(F32) * 2.0 / values.shape[-1])
    angle_table = position[:, None] * inverse[None, :]
    cosine = jnp.cos(angle_table)[:, None, :]
    sine = jnp.sin(angle_table)[:, None, :]
    lower = values[..., :half_dim]
    upper = values[..., half_dim:]
    return jnp.concatenate(
        [lower * cosine - upper * sine, upper * cosine + lower * sine], axis=-1
    )


def lane_pad(block):
    return jnp.pad(block, ((0, 0), (0, -block.shape[1] % 128)))


def silu_pair(gate_part, up_part):
    return jax.nn.silu(gate_part) * up_part


def silu_parts(v):
    sig = 1.0 / (1.0 + jnp.exp(-v))
    return sig, v * sig


def exact(left, right, dims):
    return lax.dot_general(
        left, right, (dims, ((), ())), preferred_element_type=F32, precision=lax.Precision.HIGHEST
    )


def column_tiles(wide, tile):
    return [(at, min(tile, wide - at)) for at in range(0, wide, tile)]


def moe_kernel(x_ref, dy_ref, pick_ref, back_ref, router_ref, wg_ref, wu_ref, wd_ref, sgu_ref, sd_ref,
               xr_ref, gp_ref, inner_ref, dg_ref, du_ref, share_ref, dsgu_ref, out_ref, gg_ref,
               g_buf, u_buf, dyr_buf, gate_buf, sum_buf, mm_buf):
    toks, width = x_ref.shape
    ffe = wg_ref.shape[1]
    narrow = sd_ref.shape[0]
    lane = lax.broadcasted_iota(jnp.int32, (toks, 128), 1)
    mine = (lax.axis_index(PLANE) == lane).astype(F32)

    hot = dy_ref[:, pl.ds(width, 128)].astype(F32)
    logits = jnp.where(hot > 0, dot(x_ref[...], router_ref[...]), -1e30)
    top = jnp.max(logits, axis=1, keepdims=True)
    raised = jnp.exp(logits - top)
    gate = jnp.sum(raised * mine, axis=1, keepdims=True) / jnp.sum(raised, axis=1, keepdims=True)
    gate = jnp.broadcast_to(gate, (toks, 128))
    gate_buf[...] = exact(pick_ref[...].astype(F32), gate, ((1,), (0,)))
    for at, tile in column_tiles(width, 512):
        cols = pl.ds(at, tile)
        xr_ref[:, cols] = dot(pick_ref[...], x_ref[:, cols]).astype(BF16)
        dyr_buf[:, cols] = dot(pick_ref[...], dy_ref[:, cols]).astype(BF16)

    for at, tile in column_tiles(ffe, 256):
        cols = pl.ds(at, tile)
        g = dot(xr_ref[...], wg_ref[:, cols])
        u = dot(xr_ref[...], wu_ref[:, cols])
        g_buf[:, cols] = g
        u_buf[:, cols] = u
        inner_ref[:, cols] = (silu_parts(g)[1] * u).astype(BF16)
    share_gu = dot(x_ref[...], sgu_ref[...])
    d_share = dot_nt(dy_ref[:, pl.ds(0, width)], sd_ref[...])
    sg, su = share_gu[:, :narrow], share_gu[:, narrow:]
    sig, act = silu_parts(sg)
    share_ref[...] = (act * su).astype(BF16)
    dsgu_ref[:, :narrow] = (d_share * su * sig * (1.0 + sg * (1.0 - sig))).astype(BF16)
    dsgu_ref[:, narrow:] = (d_share * act).astype(BF16)
    sum_buf[...] = jnp.zeros_like(sum_buf)
    for at, tile in column_tiles(width, 256):
        cols = pl.ds(at, tile)
        produced = dot_nt(inner_ref[...], wd_ref[cols, :])
        dyr = dyr_buf[:, cols].astype(F32)
        gate = gate_buf[:, pl.ds(0, 1)]
        for half in range(0, tile, 128):
            sum_buf[...] += produced[:, half : half + 128] * dyr[:, half : half + 128]
        gp_ref[:, cols] = (gate * dyr).astype(BF16)
        mm_buf[:, cols] = (gate * produced).astype(BF16)
    for at, tile in column_tiles(width, 256):
        cols = pl.ds(at, tile)
        out_ref[:, cols] = (dot(back_ref[...], mm_buf[:, cols]) + dot(share_ref[...], sd_ref[:, cols])).astype(BF16)
    total = jnp.broadcast_to(jnp.sum(sum_buf[...], axis=1, keepdims=True), sum_buf.shape)
    gg_ref[0] = exact(total, pick_ref[...].astype(F32), ((0,), (0,)))[:8]

    for at, tile in column_tiles(ffe, 256):
        cols = pl.ds(at, tile)
        d_inner = dot(gp_ref[...], wd_ref[:, cols])
        g, u = g_buf[:, cols], u_buf[:, cols]
        sig, act = silu_parts(g)
        dg_ref[:, cols] = (d_inner * u * sig * (1.0 + g * (1.0 - sig))).astype(BF16)
        du_ref[:, cols] = (d_inner * act).astype(BF16)


def moe(x_all, wide_dy, pick, back, router, wg, wu, wd, sgu, sd):
    steps, slots, toks = pick.shape
    width, ffe, narrow = x_all.shape[1], wg.shape[1], sd.shape[0]
    shape = jax.ShapeDtypeStruct

    def rows(count, wide):
        return pl.BlockSpec((count, wide), lambda i: (i, 0))

    def whole(array):
        return pl.BlockSpec(array.shape, lambda i: (0, 0), pipeline_mode=pl.Buffered(1))

    def out(count, wide):
        return shape((steps * count, wide), BF16)

    return pl.pallas_call(
        moe_kernel,
        grid=(steps,),
        in_specs=[
            rows(toks, width),
            rows(toks, wide_dy.shape[1]),
            pl.BlockSpec((None, slots, toks), lambda i: (i, 0, 0)),
            pl.BlockSpec((None, toks, slots), lambda i: (i, 0, 0)),
            *[whole(w) for w in (router, wg, wu, wd, sgu, sd)],
        ],
        out_specs=[
            rows(slots, width),
            rows(slots, width),
            rows(slots, ffe),
            rows(slots, ffe),
            rows(slots, ffe),
            rows(toks, narrow),
            rows(toks, 2 * narrow),
            rows(toks, width),
            pl.BlockSpec((1, 8, toks), lambda i: (i, 0, 0)),
        ],
        out_shape=[
            out(slots, width),
            out(slots, width),
            out(slots, ffe),
            out(slots, ffe),
            out(slots, ffe),
            out(toks, narrow),
            out(toks, 2 * narrow),
            out(toks, width),
            shape((steps, 8, toks), F32),
        ],
        scratch_shapes=[
            pltpu.VMEM((slots, ffe), F32),
            pltpu.VMEM((slots, ffe), F32),
            pltpu.VMEM((slots, width), BF16),
            pltpu.VMEM((slots, 128), F32),
            pltpu.VMEM((slots, 128), F32),
            pltpu.VMEM((slots, width), BF16),
        ],
        compiler_params=pltpu.CompilerParams(vmem_limit_bytes=VMEM_LIMIT),
        cost_estimate=pl.CostEstimate(flops=6 * 10**10, bytes_accessed=10**8, transcendentals=0),
    )(x_all, wide_dy, pick, back, router, wg, wu, wd, sgu, sd)


def shards(
    tokens,
    doc_ids,
    routes,
    gain_attn,
    w_query,
    w_key,
    w_value,
    w_out,
    gain_moe,
    w_router,
    shared_gate,
    shared_up,
    shared_down,
    expert_gate,
    expert_up,
    expert_down,
    cotangent,
):
    length, width = tokens.shape
    group_size = HEADS // KV_HEADS
    score_scale = HEAD_DIM ** (-0.5)
    local_experts = expert_gate.shape[0]
    sub = lax.axis_size("s")
    groups = lax.axis_size("a") * lax.axis_size("b") * lax.axis_size("l")
    experts_total = groups
    capacity = length * TOP * 4 // (3 * experts_total)
    sizes = tuple(lax.axis_size(axis) for axis in ALL)
    my_expert = lax.axis_index(PLANE)
    kvw = w_key.shape[1]
    qw = w_query.shape[1]

    small = jnp.concatenate(
        [w_router, gain_attn[:, None], gain_moe[:, None]], axis=1
    )
    small = lane_pad(small)
    hot = jnp.any(routes[:, :, None] == jnp.arange(experts_total)[None, None, :], axis=1)
    wide_dy = jnp.concatenate([cotangent, lane_pad(hot.astype(BF16))], axis=1)
    shared = jnp.stack([shared_gate, shared_up]).reshape(2, shared_gate.shape[0], *sizes[:3], -1)
    sh_rows = shared_down.shape[0]
    sh_pad = -sh_rows % 16
    dense, dy_all, wg, wu, columns, downs = inputs_gather(
        jnp.concatenate([w_query, w_key, w_value, w_out, small], axis=1),
        wide_dy,
        expert_gate,
        expert_up,
        shared.transpose(2, 3, 4, 0, 1, 5),
        jnp.pad(shared_down, ((0, sh_pad), (0, 0))),
        sizes,
        1,
    )
    sgu = jnp.concatenate([lane_pad(columns[0]), lane_pad(columns[1])], axis=1)
    narrow = columns.shape[2]
    sd_w = downs[:, :sh_rows].reshape(-1, width)
    sd_w = jnp.pad(sd_w, ((0, -narrow % 128), (0, 0)))
    hot_all = dy_all[:, width : width + experts_total] > 0
    query_full = dense[:, :qw]
    key_full = dense[:, qw : qw + kvw]
    value_full = dense[:, qw + kvw : qw + 2 * kvw]
    out_full = dense[:, qw + 2 * kvw : qw + 2 * kvw + width]
    rest = dense[:, qw + 2 * kvw + width :]
    router_full = rest[:, :experts_total]
    attn_gain = rest[:, experts_total].astype(F32)
    moe_gain = rest[:, experts_total + 1].astype(F32)

    inputs = tokens.astype(F32)
    normed, attn_norm_pull = jax.vjp(rms_norm, inputs, attn_gain)
    normed_low = normed.astype(BF16)
    query_pre = dot(normed_low, query_full).reshape(length, HEADS, HEAD_DIM)
    key_pre = dot(normed_low, key_full).reshape(length, KV_HEADS, HEAD_DIM)
    value_low = dot(normed_low, value_full).astype(BF16).reshape(length, KV_HEADS, HEAD_DIM)
    query_rot, query_pull = jax.vjp(rotate, query_pre)
    key_rot, key_pull = jax.vjp(rotate, key_pre)
    query_low = query_rot.astype(BF16).reshape(length, KV_HEADS, group_size, HEAD_DIM)
    key_low = key_rot.astype(BF16)
    position = jnp.arange(length)
    doc_row = doc_ids[0]
    allowed = (position[None, :] <= position[:, None]) & (doc_row[None, :] == doc_row[:, None])
    scores = (
        jnp.einsum("tkgd,skd->kgts", query_low, key_low, preferred_element_type=F32) * score_scale
    )
    scores = jnp.where(allowed, scores, -1e30)
    exp_scores = jnp.exp(scores - jnp.max(scores, axis=-1, keepdims=True))
    attend = exp_scores / jnp.sum(exp_scores, axis=-1, keepdims=True)
    attend_low = attend.astype(BF16)
    mixed_low = (
        jnp.einsum("kgts,skd->tkgd", attend_low, value_low, preferred_element_type=F32)
        .reshape(length, HEADS * HEAD_DIM)
        .astype(BF16)
    )
    hidden = inputs + dot(mixed_low, out_full)
    normed_moe, moe_norm_pull = jax.vjp(rms_norm, hidden, moe_gain)
    moe_low = normed_moe.astype(BF16)

    x_all, wd = gather(moe_low, expert_down, sizes, 2)
    seqs = groups
    mine = jnp.any(hot_all & (jnp.arange(experts_total)[None, :] == my_expert), axis=1)
    mine = mine.reshape(seqs, length)
    hits = mine.astype(jnp.int32)
    before = jnp.cumsum(hits, axis=1) - hits
    slot_hot = (jnp.arange(capacity)[None, :, None] == before[:, None, :]) & mine[:, None, :]
    together = min(seqs, 4)
    slot_hot = slot_hot.reshape(-1, together, capacity, 1, length)
    slot_hot = slot_hot & jnp.eye(together, dtype=bool)[None, :, None, :, None]
    slot_hot = slot_hot.reshape(-1, together * capacity, together * length).astype(BF16)
    token_hot = slot_hot.transpose(0, 2, 1)
    x_rows, gp, inner_low, dg, du, share_low, dsgu, part, gate_grad = moe(
        x_all, dy_all, slot_hot, token_hot, lane_pad(router_full), wg, wu, wd, sgu, sd_w
    )
    gate_grad = gate_grad[:, 0].reshape(seqs, length)
    gate_grad = lax.all_to_all(gate_grad, PLANE, split_axis=0, concat_axis=0, tiled=True)
    dy_all = dy_all[:, :width]
    dx_part, moe_out = back_rows(dg, du, wg, wu, sgu, dsgu, token_hot, part, sizes, 3)
    own_experts, cross_gate, cross_up, cross_down, dx = expert_weights(
        gp, inner_low, x_rows, dg, du, dx_part, sizes, 4, 6
    )
    ranks = sizes[2]
    crossing = [
        [
            lax.ppermute(cross[step - 1], "l", [(i, (i + step) % ranks) for i in range(ranks)])
            for step in range(1, ranks)
        ]
        for cross in (cross_gate, cross_up)
    ]
    output = (hidden + moe_out).astype(BF16)
    shared_grads = dot_tn(x_all, dsgu).astype(BF16)
    grad_shared_down = lax.psum_scatter(
        dot_tn(share_low[:, :narrow], dy_all), "s", scatter_dimension=0, tiled=True
    )

    own_logits = jnp.where(hot, dot(moe_low, router_full), -1e30)
    own_gates = jax.nn.softmax(own_logits, axis=-1)
    grad_gate = gate_grad.reshape(experts_total, length).T
    grad_logits = own_gates * (
        grad_gate - jnp.sum(own_gates * grad_gate, axis=-1, keepdims=True)
    )
    grad_logits = grad_logits.astype(BF16)
    grad_router = dot_tn(moe_low, grad_logits)
    dx = dx + dot_nt(grad_logits, router_full)
    grad_hidden_norm, grad_gain_moe = moe_norm_pull(dx)
    grad_hidden = cotangent.astype(F32) + grad_hidden_norm

    grad_hidden_low = grad_hidden.astype(BF16)
    grad_mixed = (
        dot_nt(grad_hidden_low, out_full)
        .astype(BF16)
        .reshape(length, KV_HEADS, group_size, HEAD_DIM)
    )
    grad_value = jnp.einsum("kgts,tkgd->skd", attend_low, grad_mixed, preferred_element_type=F32)
    grad_attend = jnp.einsum("tkgd,skd->kgts", grad_mixed, value_low, preferred_element_type=F32)
    grad_scores = (
        attend * (grad_attend - jnp.sum(grad_attend * attend, axis=-1, keepdims=True))
    ).astype(BF16)
    grad_query = (
        jnp.einsum("kgts,skd->tkgd", grad_scores, key_low, preferred_element_type=F32) * score_scale
    )
    grad_key = (
        jnp.einsum("kgts,tkgd->skd", grad_scores, query_low, preferred_element_type=F32)
        * score_scale
    )
    grad_query_low = (
        query_pull(grad_query.reshape(length, HEADS, HEAD_DIM))[0].reshape(length, -1).astype(BF16)
    )
    grad_key_low = key_pull(grad_key)[0].reshape(length, -1).astype(BF16)
    grad_value_low = grad_value.reshape(length, -1).astype(BF16)
    grad_normed = (
        dot_nt(grad_query_low, query_full)
        + dot_nt(grad_key_low, key_full)
        + dot_nt(grad_value_low, value_full)
    )
    grad_inputs_norm, grad_gain_attn = attn_norm_pull(grad_normed)
    grad_tokens = grad_hidden + grad_inputs_norm
    grad_small = jnp.concatenate(
        [grad_router, grad_gain_attn[:, None], grad_gain_moe[:, None]], axis=1
    )
    grad_small = lane_pad(grad_small)
    grad_small, crossing = lax.optimization_barrier((grad_small, crossing))
    total, blocks, cross_down = outputs_scatter(
        normed_low,
        jnp.concatenate([grad_query_low, grad_key_low, grad_value_low], axis=1),
        mixed_low,
        grad_hidden_low,
        grad_small,
        shared_grads,
        cross_down,
        sizes,
        5,
    )
    dense_sum, small_sum = total[:, :-128], total[:, -128:]
    blocks = blocks.reshape(groups, *blocks.shape[3:]).transpose(1, 0, 2).astype(F32)
    half = blocks.shape[2] // 2
    grad_shared_gate = blocks[:, :, :narrow].reshape(blocks.shape[0], -1)
    grad_shared_up = blocks[:, :, half : half + narrow].reshape(blocks.shape[0], -1)
    my_l = lax.axis_index("l")
    expert_grads = []
    for grad, cross in zip(own_experts, (*crossing, cross_down)):
        here = jnp.arange(local_experts)[:, None, None]
        grad = grad[None]
        for step in range(1, local_experts):
            from_l = (my_l - step) % local_experts
            grad = jnp.where(here == from_l, cross[step - 1].astype(F32)[None], grad)
        expert_grads.append(grad)
    return (
        output,
        grad_tokens,
        small_sum[:, experts_total],
        dense_sum[:, :qw],
        dense_sum[:, qw : qw + kvw],
        dense_sum[:, qw + kvw : qw + 2 * kvw],
        dense_sum[:, qw + 2 * kvw :],
        small_sum[:, experts_total + 1],
        small_sum[:, :experts_total],
        grad_shared_gate,
        grad_shared_up,
        grad_shared_down,
        *expert_grads,
    )


def solution(mesh):
    ranks, shards_of = mesh.shape["expert"], mesh.shape["dp"]
    local_experts = 2
    split = Mesh(
        mesh.devices.reshape(4, ranks // 4, local_experts, shards_of // local_experts), ALL
    )
    rows = P(ALL, None)
    flat = P(ALL)
    expert = P(("a", "b"), ("l", "s"), None)
    return jax.shard_map(
        shards,
        mesh=split,
        in_specs=(rows,) * 3
        + (flat,)
        + (rows,) * 4
        + (flat,)
        + (rows,) * 4
        + (expert,) * 3
        + (rows,),
        out_specs=(rows,) * 2
        + (flat,)
        + (rows,) * 4
        + (flat,)
        + (rows,) * 4
        + (expert,) * 3,
        check_vma=False,
    )
```
